32 devices in a mesh: pipe: 4 (over z), dp: 4 (over x, core), tensor: 2 (over y).
Axes of the slice: x: 2, y: 2, z: 4, core: 2. Of those that a mesh axis runs over, the one named last changes fastest.
Arguments:
- x_in: bfloat16 [4, 2, 4, 128, 1600], P('pipe', None, 'dp', 'tensor'), may hold values from -6 to 6
- out_grad: bfloat16 [2, 4, 128, 1600], P(None, 'dp'), may hold values from -6 to 6
- layer_scale: float32 [4, 1600], P('pipe'), may hold values from 0.05 to 1
- norm_gain: float32 [4, 1600], P('pipe'), may hold values from 0.5 to 1.5
- master: float32 [4, 1600, 8192], P('pipe', 'dp', 'tensor'), may hold values from -0.15625 to 0.15625
- moment_one: float32 [4, 1600, 8192], P('pipe', 'dp', 'tensor'), may hold values from -4 to 4
- moment_two: float32 [4, 1600, 8192], P('pipe', 'dp', 'tensor'), may hold values from 0.05 to 5
Outputs:
- input_grads: bfloat16 [4, 2, 4, 128, 1600], P('pipe', None, 'dp', 'tensor')
- new_master: float32 [4, 1600, 8192], P('pipe', 'dp', 'tensor')
- new_moment_one: float32 [4, 1600, 8192], P('pipe', 'dp', 'tensor')
- new_moment_two: float32 [4, 1600, 8192], P('pipe', 'dp', 'tensor')
- scale_grads: float32 [4, 2, 1600], P('pipe')
The draws below stay inside these ranges and needn't reach their ends.
All inputs are finite; a program needn't handle non-finite values.
Results may differ from the reference program's by a relative error of at most 0.027.
Values may be sent and summed in bfloat16 or wider, within the bound.
No kernel may reach another device: no remote copies, remote signals or barrier semaphores. Data moves between devices by JAX's collectives and lax.ppermute only.
A program may use at most 128 MiB of HBM per device.

```python
import math
import jax
import jax.numpy as jnp
from jax import lax

D = 1600
HEADS = 16
HD = 128
S = 128
MICRO = 2
IMAGES = 4
COLS = 8192
N_PIPE = 4
N_DP = 4
N_TENSOR = 2


def levels(own_key, shape, cuts, low, largest):
    def one(axis_at, parts):
        heights = jax.random.uniform(jax.random.fold_in(jax.random.fold_in(own_key, 6), axis_at), (parts,), jnp.float32, low / len(cuts), largest / len(cuts))
        return jnp.repeat(jnp.exp(heights), shape[axis_at] // parts).reshape((-1,) + (1,) * (len(shape) - axis_at - 1))

    factor_of = one(*cuts[0])
    for cut in cuts[1:]:
        factor_of = factor_of * one(*cut)
    return factor_of


def scatter_about(rng, extent, deviation, bound, cuts=(), dtype=jnp.bfloat16):
    drawn = jax.random.normal(rng, extent, jnp.float32) * deviation
    if len(cuts) > 0:
        drawn = levels(rng, extent, cuts, -0.22, 0.18) * drawn
    return jnp.clip(drawn, min=-bound, max=bound).astype(dtype)


def setup_inputs(seed: int = 0) -> dict:
    key_list = jax.random.split(jax.random.key(seed), 8)
    x_in = scatter_about(key_list[0], (N_PIPE, MICRO, IMAGES, S, D), 1.0, 6.0, ((0, 4), (2, 4), (3, 2)))
    out_grad = scatter_about(key_list[1], (MICRO, IMAGES, S, D), 1.0, 6.0, ((1, 4),))
    layer_scale = jnp.clip(jnp.exp(math.log(1.0) - 2.9957323 * jax.random.uniform(key_list[2], (N_PIPE, D), jnp.float32) ** levels(key_list[2], (N_PIPE, D), ((0, 4),), -0.2, 0.2)), 0.05, 1.0)
    norm_gain = jnp.clip(1.0 + 0.1 * jax.random.normal(key_list[3], (N_PIPE, D), jnp.float32), 0.5, 1.5)
    master = scatter_about(key_list[4], (N_PIPE, D, COLS), D ** -0.5, 0.15625, ((0, 4), (1, 4), (2, 2)), jnp.float32)
    moment_one = scatter_about(key_list[5], (N_PIPE, D, COLS), 0.3, 4.0, ((0, 4), (1, 4), (2, 2)), jnp.float32)
    moment_two = jnp.clip(jnp.exp(math.log(5.0) - 4.6051702 * jax.random.uniform(key_list[6], (N_PIPE, D, COLS), jnp.float32) ** levels(key_list[6], (N_PIPE, D, COLS), ((0, 4), (1, 4), (2, 2)), -0.2, 0.2)), 0.05, 5.0)
    return {"x_in": x_in, "out_grad": out_grad, "layer_scale": layer_scale, "norm_gain": norm_gain, "master": master, "moment_one": moment_one, "moment_two": moment_two}


beta_one = 0.9
beta_two = 0.95
adam_eps = 1e-08
learn_rate = 0.001
weight_decay = 0.05
adam_step = 100.0
norm_eps = 1e-06

def split_columns(weights):
    row_count = weights.shape[0]
    groups = weights.reshape(row_count, N_TENSOR, 4, weights.shape[1] // (4 * N_TENSOR))
    return [groups[:, :, member].reshape(row_count, -1) for member in range(4)]

def join_columns(members):
    row_count = members[0].shape[0]
    stacked = jnp.stack([member.reshape(row_count, N_TENSOR, -1) for member in members], axis=2)
    return stacked.reshape(row_count, -1)

def by_replica(array):
    shape = array.shape
    split = array.reshape(shape[:1] + (N_DP, shape[1] // N_DP) + shape[2:])
    return jnp.moveaxis(split, 1, 0)

def product(form, left, right):
    return jnp.einsum(form, left.astype(jnp.float32), right.astype(jnp.float32))

def rounded(value):
    return lax.optimization_barrier(value.astype(jnp.bfloat16)).astype(jnp.float32)

def reference(x_in, out_grad, layer_scale, norm_gain, master, moment_one, moment_two):
    score_root = math.sqrt(HD)
    group_width = HEADS * HD // N_TENSOR
    bias_one = 1.0 - beta_one ** adam_step
    bias_two = 1.0 - beta_two ** adam_step
    incoming = out_grad
    passed_list = [None] * N_PIPE
    master_list = [None] * N_PIPE
    first_list = [None] * N_PIPE
    second_list = [None] * N_PIPE
    scale_list = [None] * N_PIPE
    for section in range(N_PIPE - 1, -1, -1):
        weights = master[section].astype(jnp.bfloat16)
        w_query, w_keys, w_values, w_out = split_columns(weights)
        gain_vec = norm_gain[section]
        scale_vec = layer_scale[section]
        activations = x_in[section].astype(jnp.float32)
        inverse = lax.rsqrt(lax.optimization_barrier(jnp.mean(activations * activations, axis=-1, keepdims=True)) + norm_eps)
        unit_rows = activations * inverse
        normed = (unit_rows * gain_vec).astype(jnp.bfloat16)
        query = product('mbsd,dc->mbsc', normed, w_query).astype(jnp.bfloat16)
        keys = product('mbsd,dc->mbsc', normed, w_keys).astype(jnp.bfloat16)
        values = product('mbsd,dc->mbsc', normed, w_values).astype(jnp.bfloat16)
        heads_shape = query.shape[:3] + (HEADS, HD)
        query_heads = query.reshape(heads_shape)
        keys_heads = keys.reshape(heads_shape)
        values_heads = values.reshape(heads_shape)
        probs = jax.nn.softmax(product('mbqhe,mbkhe->mbhqk', query_heads, keys_heads) / score_root, axis=-1)
        probs_low = probs.astype(jnp.bfloat16)
        attended = product('mbhqk,mbkhe->mbqhe', probs_low, values_heads).astype(jnp.bfloat16)
        attended_flat = attended.reshape(query.shape)
        grad_wide = incoming.astype(jnp.float32)
        scaled = (scale_vec * grad_wide).astype(jnp.bfloat16)
        d_att = product('mbsd,dc->mbsc', scaled, w_out).astype(jnp.bfloat16)
        d_att_heads = d_att.reshape(heads_shape)
        d_prob = product('mbqhe,mbkhe->mbhqk', d_att_heads, values_heads)
        row_delta = product('mbqhe,mbqhe->mbhq', d_att_heads, attended)
        d_score = (probs * (d_prob - row_delta[..., None]) / score_root).astype(jnp.bfloat16)
        d_query = product('mbhqk,mbkhe->mbqhe', d_score, keys_heads).astype(jnp.bfloat16).reshape(query.shape)
        d_keys = product('mbhqk,mbqhe->mbkhe', d_score, query_heads).astype(jnp.bfloat16).reshape(query.shape)
        d_values = product('mbhqk,mbqhe->mbkhe', probs_low, d_att_heads).astype(jnp.bfloat16).reshape(query.shape)
        d_normed = jnp.zeros(activations.shape, jnp.float32)
        for tensor_group in range(N_TENSOR):
            col_start = tensor_group * group_width
            col_end = col_start + group_width
            group_sum = product('mbsc,dc->mbsd', d_query[..., col_start:col_end], w_query[:, col_start:col_end])
            group_sum = group_sum + product('mbsc,dc->mbsd', d_keys[..., col_start:col_end], w_keys[:, col_start:col_end])
            group_sum = group_sum + product('mbsc,dc->mbsd', d_values[..., col_start:col_end], w_values[:, col_start:col_end])
            d_normed = d_normed + rounded(group_sum)
        d_unit = d_normed * gain_vec
        d_input = inverse * (d_unit - unit_rows * lax.optimization_barrier(jnp.mean(d_unit * unit_rows, axis=-1, keepdims=True)))
        passed = (grad_wide + d_input).astype(jnp.bfloat16)
        output_proj = product('mbsc,dc->mbsd', attended_flat, w_out)
        scale_grad = lax.optimization_barrier(jnp.sum(grad_wide * output_proj, axis=(0, 1, 2)))
        gain_grad = lax.optimization_barrier(jnp.sum(d_normed * unit_rows, axis=(0, 1, 2)))

        def replica_sum(total, pieces):
            p_normed, p_query, p_keys, p_values, p_scaled, p_attended = pieces
            members = [product('mbsd,mbsc->dc', p_normed, p_query), product('mbsd,mbsc->dc', p_normed, p_keys), product('mbsd,mbsc->dc', p_normed, p_values), product('mbsd,mbsc->dc', p_scaled, p_attended)]
            return (total + rounded(join_columns(members)), None)
        stacked_inputs = tuple((by_replica(array) for array in (normed, d_query, d_keys, d_values, scaled, attended_flat)))
        weight_grad = lax.scan(replica_sum, jnp.zeros(master.shape[1:], jnp.float32), stacked_inputs)[0]
        first_new = beta_one * moment_one[section] + (1.0 - beta_one) * weight_grad
        second_new = beta_two * moment_two[section] + (1.0 - beta_two) * weight_grad * weight_grad
        update = first_new / bias_one / (jnp.sqrt(second_new / bias_two) + adam_eps)
        master_new = master[section] - learn_rate * (update + weight_decay * master[section])
        passed_list[section] = passed
        master_list[section] = master_new
        first_list[section] = first_new
        second_list[section] = second_new
        scale_list[section] = jnp.stack([scale_grad, gain_grad])
        incoming = passed
    return (jnp.stack(passed_list), jnp.stack(master_list), jnp.stack(first_list), jnp.stack(second_list), jnp.stack(scale_list))
```

```python
import functools
import math

import jax
import jax.numpy as jnp
from jax import lax
from jax.experimental import pallas as pl
from jax.experimental.pallas import tpu as pltpu
from jax.sharding import PartitionSpec as P

HD = 128

beta_one = 0.9
beta_two = 0.95
adam_eps = 1e-08
learn_rate = 0.001
weight_decay = 0.05
adam_step = 100.0
norm_eps = 1e-06
VMEM_LIMIT = 48 * 1024 * 1024

VMEM = pl.BlockSpec(memory_space=pltpu.VMEM)
SMEM = pl.BlockSpec(memory_space=pltpu.SMEM)
ANY = pl.BlockSpec(memory_space=pl.ANY)


def dot(a, b, dims=((1,), (0,))):
    return lax.dot_general(a, b, (dims, ((), ())), preferred_element_type=jnp.float32)


def softmax_rows(query, keys, root):
    scores = dot(query, keys, ((1,), (1,))) * (1.0 / root)
    scores = jnp.exp(scores - jnp.max(scores, axis=-1, keepdims=True))
    return scores / jnp.sum(scores, axis=-1, keepdims=True)


def start_weights(place_ref, pieces, buffer, sems):
    depth = pieces[0].shape[0]
    for at, piece in enumerate(pieces):
        chunk, source = divmod(at, 4)
        start = pl.multiple_of(place_ref[source], 16)
        pltpu.make_async_copy(
            piece, buffer.at[chunk, pl.ds(start, depth), :], sems.at[chunk, source]
        ).start()


def wait_weights(place_ref, pieces, buffer, sems, chunk):
    depth = pieces[0].shape[0]
    for source in range(4):
        start = pl.multiple_of(place_ref[source], 16)
        pltpu.make_async_copy(
            pieces[chunk * 4 + source],
            buffer.at[chunk, pl.ds(start, depth), :],
            sems.at[chunk, source],
        ).wait()


def forward_kernel(chunks, seq, width, place_ref, normed_ref, *refs):
    pieces = refs[: 4 * chunks]
    saved = refs[4 * chunks : 5 * chunks]
    buffer, sems = refs[5 * chunks :]
    root = math.sqrt(HD)
    start_weights(place_ref, pieces, buffer, sems)
    rows = normed_ref.shape[0]
    for chunk in range(chunks):
        wait_weights(place_ref, pieces, buffer, sems, chunk)
        projected = dot(normed_ref[...], buffer[chunk, :, : 3 * width]).astype(jnp.bfloat16)
        saved[chunk][:, : 3 * width] = projected
        for first in range(0, rows, seq):
            span = slice(first, first + seq)
            for head in range(0, width, HD):
                query = projected[span, head : head + HD]
                keys = projected[span, width + head : width + head + HD]
                values = projected[span, 2 * width + head : 2 * width + head + HD]
                probs = softmax_rows(query, keys, root).astype(jnp.bfloat16)
                saved[chunk][span, 3 * width + head : 3 * width + head + HD] = dot(
                    probs, values
                ).astype(jnp.bfloat16)


def forward(place, normed, pieces, seq):
    chunks = len(pieces) // 4
    rows, channels = normed.shape
    cols = pieces[0].shape[1]
    return pl.pallas_call(
        functools.partial(forward_kernel, chunks, seq, cols // 4),
        out_shape=[jax.ShapeDtypeStruct((rows, cols), jnp.bfloat16)] * chunks,
        in_specs=[SMEM, VMEM] + [ANY] * len(pieces),
        out_specs=[VMEM] * chunks,
        scratch_shapes=[
            pltpu.VMEM((chunks, channels, cols), jnp.bfloat16),
            pltpu.SemaphoreType.DMA((chunks, 4)),
        ],
        compiler_params=pltpu.CompilerParams(vmem_limit_bytes=VMEM_LIMIT),
        cost_estimate=pl.CostEstimate(
            flops=2 * rows * channels * cols * chunks,
            bytes_accessed=2 * channels * cols * chunks,
            transcendentals=0,
        ),
    )(place, normed, *pieces)


def backward_kernel(chunks, seq, width, own, place_ref, incoming_ref, scale_ref, *refs):
    acts = refs[:chunks]
    pieces = refs[chunks : 5 * chunks]
    rest = refs[5 * chunks :]
    if own:
        _, proj_ref, keep_ref, send_ref, buffer, sems, proj, total, out_sem = rest
    else:
        proj_ref, buffer, sems, proj, out_sem = rest
    root = math.sqrt(HD)
    rows = incoming_ref.shape[0]
    head_cols = width * chunks

    def body():
        start_weights(place_ref, pieces, buffer, sems)
        scaled = (scale_ref[...] * incoming_ref[...].astype(jnp.float32)).astype(jnp.bfloat16)
        for chunk in range(chunks):
            wait_weights(place_ref, pieces, buffer, sems, chunk)
            d_att = dot(scaled, buffer[chunk, :, 3 * width :])
            d_att = d_att.astype(jnp.bfloat16)
            for first in range(0, rows, seq):
                span = slice(first, first + seq)
                for head in range(0, width, HD):
                    at = [member * width + head for member in range(4)]
                    query, keys, values, attended = [
                        acts[chunk][span, begin : begin + HD] for begin in at
                    ]
                    d_head = d_att[span, head : head + HD]
                    probs = softmax_rows(query, keys, root)
                    d_prob = dot(d_head, values, ((1,), (1,)))
                    delta = jnp.sum(
                        d_head.astype(jnp.float32) * attended.astype(jnp.float32),
                        axis=-1,
                        keepdims=True,
                    )
                    d_score = (probs * (d_prob - delta) * (1.0 / root)).astype(jnp.bfloat16)
                    place = chunk * width + head
                    proj[span, place : place + HD] = dot(d_score, keys).astype(jnp.bfloat16)
                    place = place + head_cols
                    proj[span, place : place + HD] = dot(
                        d_score, query, ((0,), (0,))
                    ).astype(jnp.bfloat16)
                    place = place + head_cols
                    proj[span, place : place + HD] = dot(
                        probs.astype(jnp.bfloat16), d_head, ((0,), (0,))
                    ).astype(jnp.bfloat16)
            if own:
                for member in range(3):
                    begin = member * head_cols + chunk * width
                    part = dot(
                        proj[:, begin : begin + width],
                        buffer[chunk, :, member * width : (member + 1) * width],
                        ((1,), (1,)),
                    )
                    if chunk == 0 and member == 0:
                        total[...] = part
                    else:
                        total[...] += part
        copy = pltpu.make_async_copy(proj, proj_ref, out_sem)
        copy.start()
        if own:
            half = keep_ref.shape[0]
            rank = place_ref[5]
            keep_ref[...] = total[pl.ds(pl.multiple_of(rank * half, 16), half), :]
            send_ref[...] = total[pl.ds(pl.multiple_of((1 - rank) * half, 16), half), :].astype(
                jnp.bfloat16
            )
        copy.wait()

    if own:
        pl.when(place_ref[4] == 1)(body)
    else:
        body()


def backward(place, incoming, scale, acts, micro, pieces, seq, saved=None):
    chunks = len(acts)
    rows, channels = incoming.shape
    cols = pieces[0].shape[1]
    width = cols // 4
    proj_shape = jax.ShapeDtypeStruct((rows, 3 * width * chunks), jnp.bfloat16)
    own = saved is not None
    scratch = [
        pltpu.VMEM((chunks, channels, cols), jnp.bfloat16),
        pltpu.SemaphoreType.DMA((chunks, 4)),
        pltpu.VMEM(proj_shape.shape, jnp.bfloat16),
    ]
    act_spec = pl.BlockSpec((rows, cols), lambda i: (micro, 0), memory_space=pltpu.VMEM)
    in_specs = [SMEM, VMEM, VMEM] + [act_spec] * chunks + [ANY] * len(pieces)
    args = [place, incoming, scale, *acts, *pieces]
    out_shape, out_specs, aliases = [proj_shape], [ANY], {}
    if own:
        half = rows // 2
        aliases = {len(args): 0}
        in_specs.append(ANY)
        args.append(saved)
        out_shape += [
            jax.ShapeDtypeStruct((half, channels), jnp.float32),
            jax.ShapeDtypeStruct((half, channels), jnp.bfloat16),
        ]
        out_specs += [VMEM, VMEM]
        scratch.append(pltpu.VMEM((rows, channels), jnp.float32))
    scratch.append(pltpu.SemaphoreType.DMA)
    flops = 2 * rows * channels * width * chunks * (4 if own else 1)
    return pl.pallas_call(
        functools.partial(backward_kernel, chunks, seq, width, own),
        grid=(1,),
        out_shape=out_shape,
        in_specs=in_specs,
        out_specs=out_specs,
        scratch_shapes=scratch,
        input_output_aliases=aliases,
        compiler_params=pltpu.CompilerParams(vmem_limit_bytes=VMEM_LIMIT),
        cost_estimate=pl.CostEstimate(
            flops=flops, bytes_accessed=2 * channels * cols * chunks, transcendentals=0
        ),
    )(*args)


def input_kernel(
    place_ref, keep_ref, landed_ref, incoming_ref, x_ref, gain_ref, old_ref, acc_ref, new_ref, sum_ref
):
    half = keep_ref.shape[0]

    @pl.when(place_ref[4] == 1)
    def _():
        wide = x_ref[0].astype(jnp.float32)
        inverse = lax.rsqrt(jnp.mean(wide * wide, axis=-1, keepdims=True) + norm_eps)
        unit = wide * inverse
        d_normed = keep_ref[...] + landed_ref[...].astype(jnp.float32)
        sum_ref[...] = acc_ref[...] + jnp.sum(d_normed * unit, axis=0, keepdims=True)
        d_unit = d_normed * gain_ref[...]
        d_input = inverse * (d_unit - unit * jnp.mean(d_unit * unit, axis=-1, keepdims=True))
        start = pl.multiple_of(place_ref[5] * half, 16)
        grad = incoming_ref[pl.ds(start, half), :].astype(jnp.float32)
        new_ref[...] = (grad + d_input).astype(jnp.bfloat16)

    @pl.when(place_ref[4] != 1)
    def _():
        new_ref[...] = old_ref[...]
        sum_ref[...] = acc_ref[...]


def input_gradient(place, keep, landed, incoming, x_own, micro, gain, old, acc):
    half, channels = keep.shape
    x_spec = pl.BlockSpec((1, half, channels), lambda i: (micro, 0, 0), memory_space=pltpu.VMEM)
    return pl.pallas_call(
        input_kernel,
        grid=(1,),
        out_shape=[
            jax.ShapeDtypeStruct((half, channels), jnp.bfloat16),
            jax.ShapeDtypeStruct((1, channels), jnp.float32),
        ],
        in_specs=[SMEM, VMEM, VMEM, VMEM, x_spec, VMEM, VMEM, VMEM],
        out_specs=[VMEM, VMEM],
        compiler_params=pltpu.CompilerParams(vmem_limit_bytes=VMEM_LIMIT),
        cost_estimate=pl.CostEstimate(
            flops=20 * half * channels, bytes_accessed=12 * half * channels, transcendentals=0
        ),
    )(place, keep, landed, incoming, x_own, gain, old, acc)


def update_kernel(parts, with_sums, left_ref, *refs):
    rights = refs[:parts]
    master_ref, one_ref, two_ref = refs[parts : parts + 3]
    if with_sums:
        master_new, one_new, two_new, sums = refs[parts + 3 :]
    else:
        master_new, one_new, two_new = refs[parts + 6 :]
    grad = None
    begin = 0
    for right in rights:
        depth = right.shape[0]
        part = dot(left_ref[:, begin : begin + depth], right[...])
        grad = part if grad is None else grad + part
        begin += depth
    bias_one = 1.0 - beta_one**adam_step
    bias_two = 1.0 - beta_two**adam_step
    master = master_ref[0]
    first_new = beta_one * one_ref[0] + (1.0 - beta_one) * grad
    second_new = beta_two * two_ref[0] + (1.0 - beta_two) * grad * grad
    update = first_new / bias_one / (jnp.sqrt(second_new / bias_two) + adam_eps)
    master_new[0] = master - learn_rate * (update + weight_decay * master)
    one_new[0] = first_new
    two_new[0] = second_new
    if with_sums:
        low = master.astype(jnp.bfloat16).astype(jnp.float32)
        part = jnp.sum(low * grad, axis=1, keepdims=True)

        @pl.when(pl.program_id(0) == 0)
        def _():
            sums[...] = part

        @pl.when(pl.program_id(0) != 0)
        def _():
            sums[...] += part


def adam_update(left, rights, state, first_col, cols, earlier=None, block=512):
    _, depth, all_cols = state[0].shape
    offset = first_col // block
    state_spec = pl.BlockSpec((1, depth, block), lambda i: (0, 0, i + offset))
    right_specs = [pl.BlockSpec((r.shape[0], block), lambda i: (0, i)) for r in rights]
    left_spec = pl.BlockSpec(left.shape, lambda i: (0, 0))
    with_sums = earlier is None
    in_specs = [left_spec] + right_specs + [state_spec] * 3
    args = [left, *rights, *state]
    out_shape = [jax.ShapeDtypeStruct(state[0].shape, jnp.float32)] * 3
    out_specs = [state_spec] * 3
    aliases = {}
    if with_sums:
        out_shape.append(jax.ShapeDtypeStruct((depth, 1), jnp.float32))
        out_specs.append(pl.BlockSpec((depth, 1), lambda i: (0, 0)))
    else:
        aliases = {len(args) + i: i for i in range(3)}
        in_specs += [ANY] * 3
        args += list(earlier)
    return pl.pallas_call(
        functools.partial(update_kernel, len(rights), with_sums),
        grid=(cols // block,),
        out_shape=out_shape,
        in_specs=in_specs,
        out_specs=out_specs,
        input_output_aliases=aliases,
        compiler_params=pltpu.CompilerParams(vmem_limit_bytes=VMEM_LIMIT),
        cost_estimate=pl.CostEstimate(
            flops=2 * left.shape[0] * left.shape[1] * cols,
            bytes_accessed=24 * depth * cols,
            transcendentals=0,
        ),
    )(*args)


def swap(value, axis, mask):
    return lax.ppermute(value, axis, [(i, i ^ mask) for i in range(lax.axis_size(axis))])


def join_halves(mine, other, rank, axis):
    low = jnp.where(rank == 0, mine, other)
    high = jnp.where(rank == 0, other, mine)
    return jnp.concatenate([low, high], axis=axis)


def local_two_by_two(x_in, out_grad, layer_scale, norm_gain, master, moment_one, moment_two):
    n_pipe = lax.axis_size("pipe")
    pipe_rank = lax.axis_index("pipe")
    data_rank = lax.axis_index("dp")
    rank = lax.axis_index("tensor")
    micros, images, shard, channels = x_in.shape[1:]
    seq = shard * 2
    depth, all_cols = master.shape[1:]
    head_cols = all_cols // 4
    chunks = 4 if head_cols % (4 * HD) == 0 else 1
    width = head_cols // chunks
    rows = micros * seq

    pieces = []
    for chunk in range(chunks):
        own = jnp.concatenate(
            [
                master[0, :, m * head_cols + chunk * width : m * head_cols + (chunk + 1) * width]
                for m in range(4)
            ],
            axis=1,
        ).astype(jnp.bfloat16)
        far = swap(own, "dp", 2)
        near = swap(own, "dp", 1)
        across = swap(far, "dp", 1)
        pieces.append([own, near, far, across])
    flat_pieces = [piece for group in pieces for piece in group]
    sources = jnp.stack([data_rank ^ k for k in range(4)]) * depth

    def place_of(active):
        return jnp.concatenate(
            [sources, jnp.stack([jnp.asarray(active, jnp.int32), rank])]
        ).astype(jnp.int32)

    place = place_of(1)
    gain = norm_gain
    scale = layer_scale

    x_own = x_in[0, :, 0]
    x_full = join_halves(x_own, swap(x_own, "tensor", 1), rank, 1).reshape(rows, channels)
    x_far = swap(x_full, "dp", 2)

    def normalize(values):
        wide = values.astype(jnp.float32)
        inverse = lax.rsqrt(jnp.mean(wide * wide, axis=-1, keepdims=True) + norm_eps)
        return (wide * inverse * gain).astype(jnp.bfloat16)

    normed = normalize(x_full)
    normed_far = normalize(x_far)
    acts = [forward(place, normed, pieces[chunk], seq)[0] for chunk in range(chunks)]

    saved_proj = [jnp.zeros((seq, 3 * head_cols), jnp.bfloat16) for _ in range(micros)]
    passed = [jnp.zeros((shard, channels), jnp.bfloat16) for _ in range(micros)]
    gain_sum = jnp.zeros((1, channels), jnp.float32)
    incoming = [out_grad[m, 0] for m in range(micros)]
    incoming_far = [None] * micros
    straight = [(i + 1, i) for i in range(n_pipe - 1)]
    crossed = [((i + 1) * 2 + t, i * 2 + 1 - t) for i in range(n_pipe - 1) for t in range(2)]
    for stage in range(n_pipe):
        active = pipe_rank == n_pipe - 1 - stage
        here = place_of(active)
        halves = []
        for m in range(micros):
            if stage > 0:
                mine = lax.ppermute(passed[m], "pipe", straight)
                other = lax.ppermute(passed[m], ("pipe", "tensor"), crossed)
                incoming[m] = jnp.where(
                    active, join_halves(mine, other, rank, 0), incoming[m]
                )
            if stage == n_pipe - 1:
                incoming_far[m] = swap(incoming[m], "dp", 2)
            saved_proj[m], keep, send = backward(
                here, incoming[m], scale, acts, m, flat_pieces, seq, saved_proj[m]
            )
            halves.append((keep, swap(send, "tensor", 1)))
        for m in range(micros):
            keep, landed = halves[m]
            passed[m], gain_sum = input_gradient(
                here, keep, landed, incoming[m], x_own, m, gain, passed[m], gain_sum
            )
    input_grads = jnp.stack(passed)[None, :, None]

    acts_far = forward(place, normed_far, flat_pieces, seq)
    proj_far = backward(
        place, jnp.concatenate(incoming_far), scale, acts_far, 0, flat_pieces, seq
    )[0]

    mine_at, near_at = data_rank * depth, (data_rank ^ 1) * depth

    def columns_of(mine, far):
        both = jnp.concatenate([mine, far])
        kept = lax.dynamic_slice_in_dim(both, mine_at, depth, 1)
        sent = lax.dynamic_slice_in_dim(both, near_at, depth, 1)
        return jnp.concatenate([kept, swap(sent, "dp", 1)])

    normed_cols = columns_of(normed, normed_far).T
    incoming_cols = columns_of(jnp.concatenate(incoming), jnp.concatenate(incoming_far))
    scale_cols = lax.dynamic_slice_in_dim(scale, mine_at, depth, 1)
    scaled_cols = (scale_cols * incoming_cols.astype(jnp.float32)).astype(jnp.bfloat16).T

    def attended_of(group):
        return jnp.concatenate([act[:, 3 * width :] for act in group], axis=1)

    attended = [attended_of(acts), attended_of(acts_far)]
    attended = attended + [swap(value, "dp", 1) for value in attended]
    state = [master, moment_one, moment_two]
    *new_state, row_sums = adam_update(scaled_cols, attended, state, 3 * head_cols, head_cols)
    scale_part = row_sums / scale_cols.T

    def from_group(value):
        got = {}
        for d in range(4):
            for t in range(2):
                if d == 0 and t == 0:
                    got[d, t] = value
                else:
                    pairs = [(i * 2 + u, (i ^ d) * 2 + (u ^ t)) for i in range(4) for u in range(2)]
                    got[d, t] = lax.ppermute(value, ("dp", "tensor"), pairs)
        return got

    gains = from_group(gain_sum)
    scales = from_group(scale_part)
    projs = saved_proj + [proj_far]
    projs = projs + [swap(value, "dp", 1) for value in projs]
    new_state = adam_update(normed_cols, projs, state, 0, 3 * head_cols, new_state)
    gain_grad = sum(gains.values())[0]
    by_distance = jnp.stack([scales[d, 0] + scales[d, 1] for d in range(4)])
    scale_grad = by_distance[jnp.stack([data_rank ^ k for k in range(4)])].reshape(channels)
    scale_both = jnp.stack([scale_grad, gain_grad])[None]
    return (input_grads, *new_state, scale_both)


def from_behind(block, axis, distance):
    devices = range(lax.axis_size(axis))
    route = [(i - distance, i) for i in devices if i - distance in devices]
    return lax.ppermute(block, axis, route)


def normalize(values_in):
    inverse = lax.rsqrt(jnp.mean(values_in * values_in, axis=-1, keepdims=True) + norm_eps)
    return (inverse, values_in * inverse)


def select_micro(array, micro_index):
    return lax.dynamic_index_in_dim(array, micro_index, 0, keepdims=False)


def store_slot(buffer, value, slot_index):
    return lax.dynamic_update_index_in_dim(buffer, value, slot_index, 0)


def local_any(x_in, out_grad, layer_scale, norm_gain, master, moment_one, moment_two):
    n_pipe = lax.axis_size("pipe")
    n_tensor = lax.axis_size("tensor")
    pipe_rank = lax.axis_index("pipe")
    micro_count = x_in.shape[1]
    images = x_in.shape[2]
    shard_len = x_in.shape[3]
    channels = x_in.shape[4]
    seq_len = shard_len * n_tensor
    row_start = lax.axis_index("tensor") * shard_len
    head_cols = master.shape[2] // 4
    local_heads = head_cols // HD
    score_root = math.sqrt(HD)
    scale_vec = layer_scale[0]
    gain_vec = norm_gain[0]
    weights = lax.all_gather(master[0].astype(jnp.bfloat16), "dp", axis=0, tiled=True)
    w_qkv = weights[:, : 3 * head_cols]
    w_out = weights[:, 3 * head_cols :]
    full_x = lax.all_gather(x_in[0], "tensor", axis=2, tiled=True).astype(jnp.float32)
    full_inverse, full_unit = normalize(full_x)
    normed = (full_unit * gain_vec).astype(jnp.bfloat16)
    local_unit = lax.dynamic_slice_in_dim(full_unit, row_start, shard_len, 2)
    projected = jnp.einsum(
        "mbsd,dc->mbsc", normed, w_qkv, preferred_element_type=jnp.float32
    ).astype(jnp.bfloat16)
    projected = projected.reshape(micro_count, images, seq_len, 3, local_heads, HD)
    query = projected[:, :, :, 0]
    keys = projected[:, :, :, 1]
    values = projected[:, :, :, 2]
    scores = (
        jnp.einsum("mbqhe,mbkhe->mbhqk", query, keys, preferred_element_type=jnp.float32)
        / score_root
    )
    probs = jax.nn.softmax(scores, axis=-1)
    probs_low = probs.astype(jnp.bfloat16)
    attended = jnp.einsum(
        "mbhqk,mbkhe->mbqhe", probs_low, values, preferred_element_type=jnp.float32
    ).astype(jnp.bfloat16)
    attended_flat = attended.reshape(micro_count, images, seq_len, head_cols)

    def backward_segment(micro_index, incoming):
        query_now = select_micro(query, micro_index)
        keys_now = select_micro(keys, micro_index)
        values_now = select_micro(values, micro_index)
        probs_now = select_micro(probs, micro_index)
        probs_low_now = select_micro(probs_low, micro_index)
        attended_now = select_micro(attended, micro_index)
        scaled = (scale_vec * incoming.astype(jnp.float32)).astype(jnp.bfloat16)
        d_att = jnp.einsum("bsd,dc->bsc", scaled, w_out, preferred_element_type=jnp.float32).astype(
            jnp.bfloat16
        )
        d_att = d_att.reshape(images, seq_len, local_heads, HD)
        d_prob = jnp.einsum(
            "bqhe,bkhe->bhqk", d_att, values_now, preferred_element_type=jnp.float32
        )
        row_delta = jnp.einsum(
            "bqhe,bqhe->bhq", d_att, attended_now, preferred_element_type=jnp.float32
        )
        d_score = (probs_now * (d_prob - row_delta[..., None]) / score_root).astype(jnp.bfloat16)
        d_query = jnp.einsum(
            "bhqk,bkhe->bqhe", d_score, keys_now, preferred_element_type=jnp.float32
        ).astype(jnp.bfloat16)
        d_keys = jnp.einsum(
            "bhqk,bqhe->bkhe", d_score, query_now, preferred_element_type=jnp.float32
        ).astype(jnp.bfloat16)
        d_values = jnp.einsum(
            "bhqk,bqhe->bkhe", probs_low_now, d_att, preferred_element_type=jnp.float32
        ).astype(jnp.bfloat16)
        d_proj = jnp.concatenate([d_query, d_keys, d_values], axis=2).reshape(
            images, seq_len, 3 * head_cols
        )
        partial_sum = jnp.einsum("bsc,dc->bsd", d_proj, w_qkv, preferred_element_type=jnp.float32)
        return (partial_sum, d_proj, scaled)

    def spare_segment(micro_index, incoming):
        return (
            jnp.zeros((images, seq_len, channels), jnp.float32),
            jnp.zeros((images, seq_len, 3 * head_cols), jnp.bfloat16),
            jnp.zeros((images, seq_len, channels), jnp.bfloat16),
        )

    segments = n_pipe + micro_count - 1
    is_last = pipe_rank == n_pipe - 1
    received = jnp.zeros((images, seq_len, channels), jnp.bfloat16)
    slots = micro_count + 1
    grads_out = jnp.zeros((slots, images, shard_len, channels), jnp.bfloat16)
    proj_saved = jnp.zeros((slots, images, seq_len, 3 * head_cols), jnp.bfloat16)
    scaled_saved = jnp.zeros((slots, images, seq_len, channels), jnp.bfloat16)
    grad_saved = jnp.zeros((slots, images, seq_len, channels), jnp.bfloat16)
    gain_part = jnp.zeros((channels,), jnp.float32)
    for segment_step in range(segments):
        micro_index = segment_step - (n_pipe - 1) + pipe_rank
        active = jnp.logical_and(micro_index >= 0, micro_index < micro_count)
        micro_index = jnp.clip(micro_index, 0, micro_count - 1)
        slot_index = jnp.where(active, micro_index, micro_count)
        arrived = received
        incoming = jnp.where(is_last, select_micro(out_grad, micro_index), arrived)
        partial_sum, d_proj, scaled = lax.cond(
            active, backward_segment, spare_segment, micro_index, incoming
        )
        pieces = partial_sum.astype(jnp.bfloat16).reshape(images, n_tensor, shard_len, channels)
        landed = lax.all_to_all(pieces, "tensor", split_axis=1, concat_axis=1, tiled=True)
        own_d = jnp.sum(landed.astype(jnp.float32), axis=1)
        d_normed = lax.all_gather(own_d.astype(jnp.bfloat16), "tensor", axis=1, tiled=True).astype(
            own_d.dtype
        )
        own_unit = select_micro(local_unit, micro_index)
        sel_unit = select_micro(full_unit, micro_index)
        sel_inverse = select_micro(full_inverse, micro_index)
        d_unit = d_normed * gain_vec
        d_input = sel_inverse * (
            d_unit - sel_unit * jnp.mean(d_unit * sel_unit, axis=-1, keepdims=True)
        )
        passed = (incoming.astype(jnp.float32) + d_input).astype(jnp.bfloat16)
        own_passed = lax.dynamic_slice_in_dim(passed, row_start, shard_len, 1)
        gain_part = gain_part + jnp.where(active, jnp.sum(own_d * own_unit, axis=(0, 1)), 0.0)
        grads_out = store_slot(grads_out, own_passed, slot_index)
        proj_saved = store_slot(proj_saved, d_proj, slot_index)
        scaled_saved = store_slot(scaled_saved, scaled, slot_index)
        grad_saved = store_slot(grad_saved, incoming, slot_index)
        if segment_step + 1 < segments:
            received = from_behind(passed, "pipe", -1)
    grads_kept = grads_out[:micro_count]
    proj_kept = proj_saved[:micro_count]
    scaled_kept = scaled_saved[:micro_count]
    grad_kept = grad_saved[:micro_count]
    grad_qkv = jnp.einsum("mbsd,mbsc->dc", normed, proj_kept, preferred_element_type=jnp.float32)
    grad_out = jnp.einsum(
        "mbsd,mbsc->dc", scaled_kept, attended_flat, preferred_element_type=jnp.float32
    )
    weight_grad = lax.psum_scatter(
        jnp.concatenate([grad_qkv, grad_out], axis=1).astype(jnp.bfloat16),
        "dp",
        scatter_dimension=0,
        tiled=True,
    ).astype(jnp.float32)
    summed_out = jnp.einsum(
        "mbsd,mbsc->dc", grad_kept, attended_flat, preferred_element_type=jnp.float32
    )
    scale_part = jnp.sum(w_out.astype(jnp.float32) * summed_out, axis=1)
    scale_grad, gain_grad = lax.psum((scale_part, gain_part), ("dp", "tensor"))
    bias_one = 1.0 - beta_one**adam_step
    bias_two = 1.0 - beta_two**adam_step
    first_new = beta_one * moment_one[0] + (1.0 - beta_one) * weight_grad
    second_new = beta_two * moment_two[0] + (1.0 - beta_two) * weight_grad * weight_grad
    update = first_new / bias_one / (jnp.sqrt(second_new / bias_two) + adam_eps)
    master_new = master[0] - learn_rate * (update + weight_decay * master[0])
    scale_both = jnp.stack([scale_grad, gain_grad])
    return (grads_kept[None], master_new[None], first_new[None], second_new[None], scale_both[None])


def solution(mesh):
    placed = (
        P("pipe", None, "dp", "tensor", None),
        P(None, "dp", None, None),
        P("pipe", None),
        P("pipe", None),
        P("pipe", "dp", "tensor"),
        P("pipe", "dp", "tensor"),
        P("pipe", "dp", "tensor"),
    )
    two_by_two = mesh.shape["dp"] == 4 and mesh.shape["tensor"] == 2
    return jax.shard_map(
        local_two_by_two if two_by_two else local_any,
        mesh=mesh,
        in_specs=placed,
        out_specs=(
            P("pipe", None, "dp", "tensor", None),
            P("pipe", "dp", "tensor"),
            P("pipe", "dp", "tensor"),
            P("pipe", "dp", "tensor"),
            P("pipe", None, None),
        ),
        check_vma=False,
    )
```

```python
import functools
import math

import jax
import jax.numpy as jnp
from jax import lax
from jax.experimental import pallas as pl
from jax.experimental.pallas import tpu as pltpu
from jax.sharding import PartitionSpec as P

HD = 128

beta_one = 0.9
beta_two = 0.95
adam_eps = 1e-08
learn_rate = 0.001
weight_decay = 0.05
adam_step = 100.0
norm_eps = 1e-06
VMEM_LIMIT = 64 * 1024 * 1024

VMEM = "vmem"
SMEM = pl.BlockSpec(memory_space=pltpu.SMEM)
ANY = pl.BlockSpec(memory_space=pl.ANY)
bf16 = jnp.bfloat16
f32 = jnp.float32


def dot(a, b, dims=((1,), (0,))):
    return lax.dot_general(a, b, (dims, ((), ())), preferred_element_type=jnp.float32)


def shape_of(shape, dtype):
    return jax.ShapeDtypeStruct(shape, dtype)


def round_up(value, unit):
    return (value + unit - 1) // unit * unit


def call(kernel, args, specs, outs, out_specs, scratch=(), aliases=None, moved=0):
    def spec_of(spec, value):
        if spec != VMEM:
            return spec
        return pl.BlockSpec(value.shape, lambda i: (0,) * len(value.shape))

    return pl.pallas_call(
        kernel,
        grid=(1,),
        out_shape=outs,
        in_specs=[spec_of(spec, value) for spec, value in zip(specs, args)],
        out_specs=[spec_of(spec, value) for spec, value in zip(out_specs, outs)],
        scratch_shapes=list(scratch),
        input_output_aliases=aliases or {},
        compiler_params=pltpu.CompilerParams(vmem_limit_bytes=VMEM_LIMIT),
        cost_estimate=pl.CostEstimate(flops=0, bytes_accessed=moved, transcendentals=0),
    )(*args)


def start_all(copies):
    for copy in copies:
        copy.start()


def wait_all(copies):
    for copy in copies:
        copy.wait()


def pick(ref, micro):
    return ref[micro] if len(ref.shape) == 3 else ref[...]


def rows_at(start, size):
    return pl.ds(pl.multiple_of(start, 16), size)


def normalize_kernel(
    place_ref, mine_ref, other_ref, gain_ref, _, normed_ref, sent_ref, turned_ref
):
    micros, shard, channels = mine_ref.shape
    rank = place_ref[5]
    normed_ref[...] = jnp.zeros_like(normed_ref)
    for m in range(micros):
        for source, at in ((mine_ref, rank), (other_ref, 1 - rank)):
            values = source[m].astype(f32)
            inverse = lax.rsqrt(jnp.mean(values * values, axis=-1, keepdims=True) + norm_eps)
            normed = (values * inverse * gain_ref[...]).astype(bf16)
            normed_ref[rows_at(m * 2 * shard + at * shard, shard), :channels] = normed
    sent_ref[...] = normed_ref[...]
    turned_ref[...] = normed_ref[...].T


def normalize(place, mine, other, gain, early):
    micros, shard, channels = mine.shape
    rows, padded = micros * shard * 2, round_up(channels, 128)
    return call(
        normalize_kernel,
        [place, mine, other, gain, early],
        [SMEM, VMEM, VMEM, VMEM, ANY],
        [shape_of((rows, padded), bf16)] * 2 + [shape_of((padded, rows), bf16)],
        [VMEM] * 3,
    )


def round_kernel(chunk, chunks, master_ref, low_ref, wide, sems):
    width = wide.shape[2]
    copies = [
        pltpu.make_async_copy(
            master_ref.at[0, :, pl.ds((n * chunks + chunk) * width, width)], wide.at[n], sems.at[n]
        )
        for n in range(4)
    ]
    start_all(copies)
    for n in range(4):
        copies[n].wait()
        low_ref[:, n * width : (n + 1) * width] = wide[n].astype(bf16)


def rounded_chunk(master, chunk, chunks):
    _, depth, cols = master.shape
    width = cols // 4 // chunks
    return call(
        functools.partial(round_kernel, chunk, chunks),
        [master],
        [ANY],
        [shape_of((depth, 4 * width), bf16)],
        [VMEM],
        [pltpu.VMEM((4, depth, width), f32), pltpu.SemaphoreType.DMA((4,))],
    )[0]


def attend(projected, att_ref, probs_ref, seq, width):
    root = math.sqrt(HD)
    heads = width // HD
    for m in range(projected.shape[0] // seq):
        span = slice(m * seq, (m + 1) * seq)
        for h in range(heads):
            query, keys, values = [
                projected[span, n * width + h * HD : n * width + (h + 1) * HD] for n in range(3)
            ]
            scores = dot(query, keys, ((1,), (1,))) * (1.0 / root)
            scores = jnp.exp(scores - jnp.max(scores, axis=-1, keepdims=True))
            probs = scores / jnp.sum(scores, axis=-1, keepdims=True)
            probs_ref[(m * heads + h) * seq : (m * heads + h + 1) * seq, :] = probs
            att_ref[span, h * HD : (h + 1) * HD] = dot(probs.astype(bf16), values).astype(bf16)


def forward_kernel(chunk, channels, seq, place_ref, normed_ref, *refs):
    pieces = refs[:4]
    *refs, normed, buffer, turned, acts, att, probs, sems, out_sems = refs
    targets = [ref.at[chunk] for ref in refs[-5:]]
    depth = pieces[0].shape[0]
    width = pieces[0].shape[1] // 4
    targets[1] = refs[-4].at[:, pl.ds(chunk * width, width)]
    copies = [
        pltpu.make_async_copy(piece, buffer.at[rows_at(place_ref[at], depth), :], sems.at[at])
        for at, piece in enumerate(pieces)
    ]
    copies.append(pltpu.make_async_copy(normed_ref, normed, sems.at[4]))
    start_all(copies)
    buffer[channels:, :] = jnp.zeros((buffer.shape[0] - channels, buffer.shape[1]), bf16)
    wait_all(copies)
    w_out = buffer.at[pl.ds(0, channels), pl.ds(3 * width, width)]
    written = [
        pltpu.make_async_copy(source, target, out_sems.at[n])
        for n, (source, target) in enumerate(zip((acts, att, probs, w_out, turned), targets))
    ]
    written[3].start()
    turned[...] = buffer[:, : 3 * width].T
    written[4].start()
    projected = dot(normed[...], buffer[:, : 3 * width]).astype(bf16)
    acts[...] = projected
    written[0].start()
    attend(projected, att, probs, seq, width)
    written[1].start()
    written[2].start()
    wait_all(written)


def saved_shapes(rows, width, chunks, seq):
    return [
        shape_of((chunks, rows, 3 * width), bf16),
        shape_of((rows, width * chunks), bf16),
        shape_of((chunks, rows * width // HD, seq), f32),
    ]


def forward(place, normed, pieces, chunk, chunks, channels, seq, earlier):
    rows, padded = normed.shape
    cols = pieces[0].shape[1]
    width = cols // 4
    outs = saved_shapes(rows, width, chunks, seq) + [
        shape_of((chunks, channels, width), bf16),
        shape_of((chunks, 3 * width, padded), bf16),
    ]
    args = [place, normed, *pieces]
    aliases = {}
    if earlier is not None:
        aliases = {len(args) + n: n for n in range(5)}
        args += list(earlier)
    return call(
        functools.partial(forward_kernel, chunk, channels, seq),
        args,
        [SMEM] + [ANY] * (len(args) - 1),
        outs,
        [ANY] * 5,
        [
            pltpu.VMEM((rows, padded), bf16),
            pltpu.VMEM((padded, cols), bf16),
            pltpu.VMEM((3 * width, padded), bf16),
            pltpu.VMEM((rows, 3 * width), bf16),
            pltpu.VMEM((rows, width), bf16),
            pltpu.VMEM((rows * width // HD, seq), f32),
            pltpu.SemaphoreType.DMA((5,)),
            pltpu.SemaphoreType.DMA((5,)),
        ],
        aliases,
        moved=20 * channels * cols,
    )


def forward_far_kernel(first, count, seq, normed_ref, turned_ref, *refs):
    *refs, normed, normed_turned, turned, acts, atts, probs, sems, out_sems = refs
    acts_ref, att_ref, probs_ref, turned_rows_ref = refs[-4:]
    copies = [pltpu.make_async_copy(normed_ref, normed, sems.at[count])]
    copies += [
        pltpu.make_async_copy(turned_ref.at[first + c], turned.at[c], sems.at[c])
        for c in range(count)
    ]
    start_all(copies)
    copies[0].wait()
    width = turned.shape[1] // 3
    written = []
    if first == 0:
        normed_turned[...] = normed[...].T
        written.append(
            pltpu.make_async_copy(normed_turned, turned_rows_ref, out_sems.at[0, 3])
        )
        written[-1].start()
    for c in range(count):
        copies[1 + c].wait()
        projected = dot(normed[...], turned[c], ((1,), (1,))).astype(bf16)
        acts[c] = projected
        attend(projected, atts.at[c], probs.at[c], seq, width)
        targets = (
            acts_ref.at[first + c],
            att_ref.at[:, pl.ds((first + c) * width, width)],
            probs_ref.at[first + c],
        )
        for n, source in enumerate((acts, atts, probs)):
            written.append(pltpu.make_async_copy(source.at[c], targets[n], out_sems.at[c, n]))
            written[-1].start()
    wait_all(written)


def forward_far(normed, turned, first, count, seq, earlier):
    rows, padded = normed.shape
    chunks, triple, _ = turned.shape
    width = triple // 3
    args = [normed, turned]
    aliases = {}
    if earlier is not None:
        aliases = {len(args) + n: n for n in range(4)}
        args += list(earlier)
    return call(
        functools.partial(forward_far_kernel, first, count, seq),
        args,
        [ANY] * len(args),
        [*saved_shapes(rows, width, chunks, seq), shape_of((padded, rows), bf16)],
        [ANY] * 4,
        [
            pltpu.VMEM((rows, padded), bf16),
            pltpu.VMEM((padded, rows), bf16),
            pltpu.VMEM((count, triple, padded), bf16),
            pltpu.VMEM((count, rows, triple), bf16),
            pltpu.VMEM((count, rows, width), bf16),
            pltpu.VMEM((count, rows * width // HD, seq), f32),
            pltpu.SemaphoreType.DMA((count + 1,)),
            pltpu.SemaphoreType.DMA((count, 4)),
        ],
        aliases,
    )


def loads_of(sources, buffers, sems, first, rows):
    acts, att, probs, *weights = sources
    chunks = acts.shape[0]
    width = att.shape[1] // chunks
    heads = width // HD
    loads = []
    for c in range(chunks):
        views = [acts.at[c, pl.ds(first, rows), :]]
        views.append(att.at[pl.ds(first, rows), pl.ds(c * width, width)])
        views.append(probs.at[c, pl.ds(first * heads, rows * heads), :])
        views += [weight.at[c] for weight in weights]
        loads.append(
            [
                pltpu.make_async_copy(view, buffers[n].at[c], sems.at[c, n])
                for n, view in enumerate(views)
            ]
        )
    return loads


def buffers_of(sources, rows):
    acts, att, probs, *weights = sources
    chunks, all_rows, triple = acts.shape
    width = triple // 3
    buffers = [
        pltpu.VMEM((chunks, rows, triple), bf16),
        pltpu.VMEM((chunks, rows, width), bf16),
        pltpu.VMEM((chunks, rows * width // HD, probs.shape[2]), f32),
    ]
    buffers += [pltpu.VMEM(weight.shape, bf16) for weight in weights]
    return [*buffers, pltpu.SemaphoreType.DMA((chunks, len(buffers)))]


def head_gradients(scaled, seq, loads, buffers, proj, after=None):
    root = math.sqrt(HD)
    acts, atts, probs, w_outs = buffers[:4]
    chunks, _, width = atts.shape
    heads = width // HD
    head_cols = chunks * width
    for c in range(chunks):
        wait_all(loads[c][:4])
        d_att = dot(scaled, w_outs[c]).astype(bf16)
        for m in range(scaled.shape[0] // seq):
            span = slice(m * seq, (m + 1) * seq)
            grads = [[], [], []]
            for h in range(heads):
                query, keys, values = [
                    acts[c, span, n * width + h * HD : n * width + (h + 1) * HD] for n in range(3)
                ]
                attended = atts[c, span, h * HD : (h + 1) * HD].astype(f32)
                at = (m * heads + h) * seq
                prob = probs[c, at : at + seq, :]
                d_head = d_att[span, h * HD : (h + 1) * HD]
                d_prob = dot(d_head, values, ((1,), (1,)))
                delta = jnp.sum(d_head.astype(f32) * attended, axis=-1, keepdims=True)
                d_score = (prob * (d_prob - delta) * (1.0 / root)).astype(bf16)
                grads[0].append(dot(d_score, keys).astype(bf16))
                grads[1].append(dot(d_score, query, ((0,), (0,))).astype(bf16))
                grads[2].append(dot(prob.astype(bf16), d_head, ((0,), (0,))).astype(bf16))
            for n in range(3):
                begin = n * head_cols + c * width
                for h in range(heads):
                    proj[span, begin + h * HD : begin + (h + 1) * HD] = grads[n][h]
        if after is not None:
            after(c, jnp.concatenate([value for group in grads for value in group], axis=1))


def micro_of(ref, micro):
    return ref.at[micro] if len(ref.shape) == 3 else ref


def scaled_turned(scaled, padded):
    rows, channels = scaled.shape
    return jnp.concatenate([scaled, jnp.zeros((rows, padded - channels), bf16)], axis=1).T


def backward_kernel(chunks, micro, section, halves, seq, place_ref, scale_ref, *refs):
    sources, refs = refs[:5], refs[5:]
    *buffers, sems, total, proj, merged, turned_in, keep, send, own_sems = refs[-13:]
    refs = refs[:-13]
    rank = place_ref[5]
    active = place_ref[4] == section
    shard, channels = keep.shape
    if halves:
        mine_ref, other_ref, before_ref, *refs = refs
        proj_ref, turned_ref, keep_ref, send_ref, merged_ref = refs[-5:]

        @pl.when(jnp.logical_not(active))
        def _():
            hand_on(micro_of(before_ref, micro), merged, merged_ref, own_sems.at[0])

    else:
        incoming_ref, *refs = refs
        proj_ref, turned_ref, keep_ref, send_ref = refs[-4:]

    @pl.when(active)
    def _():
        if halves:
            arrive = [
                pltpu.make_async_copy(
                    ref, merged.at[rows_at(at * shard, shard), :], own_sems.at[n]
                )
                for n, (ref, at) in enumerate(((mine_ref, rank), (other_ref, 1 - rank)))
            ]
        else:
            arrive = [pltpu.make_async_copy(micro_of(incoming_ref, micro), merged, own_sems.at[0])]
        start_all(arrive)
        loads = loads_of(sources, buffers, sems, micro * seq, seq)
        for group in loads[:2]:
            start_all(group)
        wait_all(arrive)
        outs = []

        def write(source, target):
            outs.append(pltpu.make_async_copy(source, target, own_sems.at[2 + len(outs)]))
            outs[-1].start()

        if halves:
            write(merged, merged_ref)
        scaled = (scale_ref[...] * merged[...].astype(f32)).astype(bf16)
        turned_in[...] = scaled_turned(scaled, turned_in.shape[0])
        write(turned_in, turned_ref)
        turned = buffers[4]

        def add(c, grads):
            wait_all(loads[c][4:])
            if c + 2 < chunks:
                start_all(loads[c + 2])
            part = dot(grads, turned[c])
            if c == 0:
                total[...] = part
            else:
                total[...] += part

        head_gradients(scaled, seq, loads, buffers, proj, add)
        write(proj, proj_ref)
        send[...] = total[rows_at((1 - rank) * shard, shard), :channels].astype(bf16)
        write(send, send_ref)
        keep[...] = total[rows_at(rank * shard, shard), :channels].astype(bf16)
        write(keep, keep_ref)
        wait_all(outs)


def backward(place, scale, saved, weights, micro, section, seq, incoming, before, old):
    chunks, channels, width = weights[0].shape
    padded = weights[1].shape[2]
    halves = isinstance(incoming, tuple)
    args = [place, scale, *saved, *weights]
    args += [*incoming, before] if halves else [incoming]
    aliases = {}
    if old is not None:
        aliases = {len(args) + n: n for n in range(2)}
        args += list(old)
    outs = [
        shape_of((seq, 3 * width * chunks), bf16),
        shape_of((padded, seq), bf16),
        shape_of((seq // 2, channels), bf16),
        shape_of((seq // 2, channels), bf16),
    ]
    if halves:
        outs.append(shape_of((seq, channels), bf16))
    return call(
        functools.partial(backward_kernel, chunks, micro, section, halves, seq),
        args,
        [SMEM, VMEM] + [ANY] * (len(args) - 2),
        outs,
        [ANY] * len(outs),
        buffers_of([*saved, *weights], seq)
        + [
            pltpu.VMEM((seq, padded), f32),
            pltpu.VMEM((seq, 3 * width * chunks), bf16),
            pltpu.VMEM((seq, channels), bf16),
            pltpu.VMEM((padded, seq), bf16),
            pltpu.VMEM((seq // 2, channels), bf16),
            pltpu.VMEM((seq // 2, channels), bf16),
            pltpu.SemaphoreType.DMA((7,)),
        ],
        aliases,
    )


def backward_far_kernel(chunks, seq, scale_ref, *refs):
    sources = refs[:4]
    *refs, acts, atts, probs, w_outs, sems = refs[4:]
    buffers = (acts, atts, probs, w_outs)
    *incoming, proj_ref, turned_ref = refs
    loads = loads_of(sources, buffers, sems, 0, proj_ref.shape[0])
    for group in loads:
        start_all(group)
    scaled = jnp.concatenate(
        [(scale_ref[...] * ref[...].astype(f32)).astype(bf16) for ref in incoming]
    )
    turned_ref[...] = scaled_turned(scaled, turned_ref.shape[0])
    head_gradients(scaled, seq, loads, buffers, proj_ref)


def backward_far(scale, saved, w_outs, seq, incoming):
    chunks, channels, width = w_outs.shape
    rows = len(incoming) * seq
    return call(
        functools.partial(backward_far_kernel, chunks, seq),
        [scale, *saved, w_outs, *incoming],
        [VMEM] + [ANY] * 4 + [VMEM] * len(incoming),
        [
            shape_of((rows, 3 * width * chunks), bf16),
            shape_of((round_up(channels, 128), rows), bf16),
        ],
        [VMEM] * 2,
        buffers_of([*saved, w_outs], rows),
    )


def hand_on(source, through, target, sem):
    for copy in (
        pltpu.make_async_copy(source, through, sem),
        pltpu.make_async_copy(through, target, sem),
    ):
        copy.start()
        copy.wait()


def merge_kernel(micro, section, place_ref, mine_ref, other_ref, before_ref, merged_ref, merged, sems):
    shard = mine_ref.shape[0]
    rank = place_ref[5]
    active = place_ref[4] == section

    @pl.when(active)
    def _():
        copies = [
            pltpu.make_async_copy(ref, merged.at[rows_at(at * shard, shard), :], sems.at[n])
            for n, (ref, at) in enumerate(((mine_ref, rank), (other_ref, 1 - rank)))
        ]
        start_all(copies)
        wait_all(copies)
        copy = pltpu.make_async_copy(merged, merged_ref, sems.at[0])
        copy.start()
        copy.wait()

    @pl.when(jnp.logical_not(active))
    def _():
        hand_on(micro_of(before_ref, micro), merged, merged_ref, sems.at[0])


def merge(place, mine, other, before, micro, section):
    shard, channels = mine.shape
    return call(
        functools.partial(merge_kernel, micro, section),
        [place, mine, other, before],
        [SMEM, ANY, ANY, ANY],
        [shape_of((2 * shard, channels), bf16)],
        [ANY],
        [pltpu.VMEM((2 * shard, channels), bf16), pltpu.SemaphoreType.DMA((2,))],
    )[0]


def input_kernel(micro, section, place_ref, gain_ref, keep_ref, landed_ref, grad_ref, x_ref, *refs):
    new_ref, sum_ref, keep, landed, grad, own, new, total, sems = refs[-9:]
    shard = keep.shape[0]

    @pl.when(place_ref[4] == section)
    def _():
        if len(grad_ref.shape) == 2:
            grad_from = grad_ref
        else:
            grad_from = grad_ref.at[micro, rows_at(place_ref[5] * shard, shard), :]
        loads = [
            pltpu.make_async_copy(source, target, sems.at[n])
            for n, (source, target) in enumerate(
                ((x_ref.at[micro], own), (keep_ref, keep), (landed_ref, landed), (grad_from, grad))
            )
        ]
        start_all(loads)
        loads[0].wait()
        wide = own[...].astype(f32)
        inverse = lax.rsqrt(jnp.mean(wide * wide, axis=-1, keepdims=True) + norm_eps)
        unit = wide * inverse
        wait_all(loads[1:])
        d_normed = keep[...].astype(f32) + landed[...].astype(f32)
        d_unit = d_normed * gain_ref[...]
        d_input = inverse * (d_unit - unit * jnp.mean(d_unit * unit, axis=-1, keepdims=True))
        new[...] = (grad[...].astype(f32) + d_input).astype(bf16)
        out = pltpu.make_async_copy(new, new_ref, sems.at[4])
        out.start()
        total[...] = jnp.sum(d_normed * unit, axis=0, keepdims=True)
        out_sum = pltpu.make_async_copy(total, sum_ref, sems.at[5])
        out_sum.start()
        out.wait()
        out_sum.wait()


def input_gradient(place, keep, landed, grad, x_own, micro, section, gain, old):
    shard, channels = keep.shape
    args = [place, gain, keep, landed, grad, x_own, *old]
    return call(
        functools.partial(input_kernel, micro, section),
        args,
        [SMEM, VMEM] + [ANY] * (len(args) - 2),
        [shape_of((shard, channels), bf16), shape_of((1, channels), f32)],
        [ANY, ANY],
        [
            *[pltpu.VMEM((shard, channels), bf16)] * 5,
            pltpu.VMEM((1, channels), f32),
            pltpu.SemaphoreType.DMA((6,)),
        ],
        {6 + n: n for n in range(len(old))},
    )


def adam(grad, master, first, second):
    bias_one = 1.0 - beta_one**adam_step
    bias_two = 1.0 - beta_two**adam_step
    first_new = beta_one * first + (1.0 - beta_one) * grad
    second_new = beta_two * second + (1.0 - beta_two) * grad * grad
    corrected = second_new * (1.0 / bias_two)
    root = corrected * lax.rsqrt(corrected)
    update = first_new * (learn_rate / bias_one) / (root + adam_eps)
    return master * (1.0 - learn_rate * weight_decay) - update, first_new, second_new


AHEAD = 2


def update_kernel(lefts, parts, first, right_col, first_col, blocks, place_ref, *refs):
    turned, refs = refs[:lefts], refs[lefts:]
    rights, refs = refs[:parts], refs[parts:]
    state, refs = refs[:3], refs[3:]
    if not first:
        refs = refs[3:]
    new_state, refs = refs[:3], refs[3:]
    sums = None
    if first:
        sums, refs = refs[0], refs[1:]
    left, right, held, left_sems, right_sems, in_sems, out_sems = refs
    depth = left.shape[0]
    width = right.shape[2]

    left_copies, begin = [], 0
    for at, value in enumerate(turned):
        rows = value.shape[1]
        left_copies.append(
            pltpu.make_async_copy(
                value.at[rows_at(place_ref[0], depth), :],
                left.at[:, pl.ds(begin, rows)],
                left_sems.at[at],
            )
        )
        begin += rows

    def loads(block):
        copies, begin = [], 0
        for at, value in enumerate(rights):
            rows = value.shape[0]
            copies.append(
                pltpu.make_async_copy(
                    value.at[:, pl.ds(right_col + block * width, width)],
                    right.at[block, pl.ds(begin, rows), :],
                    right_sems.at[block, at],
                )
            )
            begin += rows
        for at, value in enumerate(state):
            copies.append(
                pltpu.make_async_copy(
                    value.at[0, :, pl.ds(first_col + block * width, width)],
                    held.at[block, at],
                    in_sems.at[block, at],
                )
            )
        return copies

    pending = [loads(block) for block in range(blocks)]
    start_all(left_copies)
    for block in range(min(AHEAD, blocks)):
        start_all(pending[block])
    wait_all(left_copies)
    written = []
    for block in range(blocks):
        wait_all(pending[block])
        if block + AHEAD < blocks:
            start_all(pending[block + AHEAD])
        grad = dot(left[...], right[block])
        master = held[block, 0]
        values = adam(grad, master, held[block, 1], held[block, 2])
        if first:
            low = master.astype(bf16).astype(f32)
            part = jnp.sum(low * grad, axis=1, keepdims=True)
            if block == 0:
                sums[...] = part
            else:
                sums[...] += part
        for at, value in enumerate(values):
            held[block, at] = value
            written.append(
                pltpu.make_async_copy(
                    held.at[block, at],
                    new_state[at].at[0, :, pl.ds(first_col + block * width, width)],
                    out_sems.at[block, at],
                )
            )
            written[-1].start()
    wait_all(written)


def update(place, turned, rights, right_col, state, earlier, first_col, cols, block=512):
    _, depth, _ = state[0].shape
    tokens = sum(value.shape[1] for value in turned)
    first = earlier is None
    blocks = cols // block
    args = [place, *turned, *rights, *state]
    outs = [shape_of(state[0].shape, f32)] * 3
    out_specs = [ANY] * 3
    aliases = {}
    if first:
        outs.append(shape_of((depth, 1), f32))
        out_specs.append(VMEM)
    else:
        aliases = {len(args) + i: i for i in range(3)}
        args += list(earlier)
    return call(
        functools.partial(
            update_kernel, len(turned), len(rights), first, right_col, first_col, blocks
        ),
        args,
        [SMEM] + [ANY] * (len(args) - 1),
        outs,
        out_specs,
        [
            pltpu.VMEM((depth, tokens), bf16),
            pltpu.VMEM((blocks, tokens, block), bf16),
            pltpu.VMEM((blocks, 3, depth, block), f32),
            pltpu.SemaphoreType.DMA((len(turned),)),
            pltpu.SemaphoreType.DMA((blocks, len(rights))),
            pltpu.SemaphoreType.DMA((blocks, 3)),
            pltpu.SemaphoreType.DMA((blocks, 3)),
        ],
        aliases,
        moved=24 * depth * cols,
    )


def swap(value, axis, mask):
    return lax.ppermute(value, axis, [(i, i ^ mask) for i in range(lax.axis_size(axis))])


def after(value, *others):
    return lax.optimization_barrier((value, *others))[0]


def local_two_by_two(x_in, out_grad, layer_scale, norm_gain, master, moment_one, moment_two):
    n_pipe = lax.axis_size("pipe")
    pipe_rank = lax.axis_index("pipe")
    data_rank = lax.axis_index("dp")
    rank = lax.axis_index("tensor")
    micros, _, shard, channels = x_in.shape[1:]
    seq = shard * 2
    depth, all_cols = master.shape[1:]
    head_cols = all_cols // 4
    chunks = 4 if head_cols % (4 * HD) == 0 else 1
    width = head_cols // chunks
    gain, scale = norm_gain, layer_scale
    place = jnp.stack(
        [(data_rank ^ k) * depth for k in range(4)] + [pipe_rank, rank]
    ).astype(jnp.int32)

    x_own = x_in[0, :, 0]
    x_other = swap(x_own, "tensor", 1)

    own = [rounded_chunk(master, c, chunks) for c in range(chunks)]
    far = [swap(value, "dp", 2) for value in own]
    if chunks > 2:
        x_other, own[2], own[3], far[0], far[1] = lax.optimization_barrier(
            (x_other, own[2], own[3], far[0], far[1])
        )
        far[2:] = [swap(value, "dp", 2) for value in own[2:]]
    normed, normed_sent, normed_turned = normalize(place, x_own, x_other, gain, out_grad[:, 0])
    values = None
    for c in range(chunks):
        arrived = far[c] if c < chunks - 1 or not values else after(far[c], values[0])
        pieces = [own[c], swap(own[c], "dp", 1), arrived, swap(arrived, "dp", 1)]
        values = forward(place, normed, pieces, c, chunks, channels, seq, values)
    saved, weights = values[:3], values[3:]
    normed_far = swap(after(normed_sent, far[-1]), "dp", 2)

    def with_sibling(values):
        return [*values, *[swap(value, "dp", 1) for value in values]]

    kept = [None] * micros
    passed = [None] * micros
    sums = [None] * micros
    incoming = [out_grad[:, 0]] * micros
    incoming_far = [None] * micros
    straight = [(i + 1, i) for i in range(n_pipe - 1)]
    bounds = [min(chunks, 2 * n) for n in range(n_pipe)]
    saved_far = None
    for stage in range(n_pipe):
        section = n_pipe - 1 - stage
        own_rows = list(incoming)
        arrived = list(incoming)
        if stage > 0:
            own_rows = [lax.ppermute(passed[m], "pipe", straight) for m in range(micros)]
            part = bounds[stage] - bounds[stage - 1]
            if part:
                saved_far = forward_far(
                    after(normed_far, *passed), weights[1], bounds[stage - 1], part, seq, saved_far
                )
                own_rows = [after(mine, saved_far[0]) for mine in own_rows]
            arrived = [(mine, swap(mine, "tensor", 1)) for mine in own_rows]
        sent = []
        for m in range(micros):
            if sent:
                first = sent[0][0]
                if isinstance(arrived[m], tuple):
                    arrived[m] = (arrived[m][0], after(arrived[m][1], first))
                else:
                    arrived[m] = after(arrived[m], first)
            if stage == n_pipe - 1:
                if stage > 0:
                    incoming[m] = merge(place, *arrived[m], incoming[m], m, section)
                    arrived[m] = incoming[m]
                incoming_far[m] = swap(incoming[m], "dp", 2)
            outs = backward(
                place, scale, saved, weights, m, section, seq, arrived[m], incoming[m], kept[m]
            )
            kept[m], (keep, send) = outs[:2], outs[2:4]
            if len(outs) > 4:
                incoming[m] = outs[4]
            sent.append((keep, swap(send, "tensor", 1)))
        for m in range(micros):
            old = [] if stage == 0 else [passed[m], sums[m]]
            passed[m], sums[m] = input_gradient(
                place, *sent[m], own_rows[m], x_own, m, section, gain, old
            )
    input_grads = jnp.stack(passed)[None, :, None]

    attended = with_sibling([saved[1], saved_far[1]])
    normed_all = with_sibling([normed_turned, saved_far[3]])
    incoming_far, attended[2], attended[3], normed_all[2], normed_all[3] = lax.optimization_barrier(
        (incoming_far, *attended[2:], *normed_all[2:], sent[-1][0])
    )[:-1]
    proj_far, scaled_far = backward_far(scale, saved_far[:3], weights[0], seq, incoming_far)

    state = [master, moment_one, moment_two]
    scaled_all = with_sibling([*[value[1] for value in kept], scaled_far])
    projs = with_sibling([*[value[0] for value in kept], proj_far])
    projs[-1], scaled_all[-1] = lax.optimization_barrier((projs[-1], scaled_all[-1]))
    *new_state, row_sums = update(
        place, scaled_all, attended, 0, state, None, 3 * head_cols, head_cols
    )
    scale_part = row_sums.T / lax.dynamic_slice_in_dim(scale, data_rank * depth, depth, 1)
    vectors = jnp.concatenate(
        [
            lax.dynamic_update_slice_in_dim(
                jnp.zeros((1, channels), f32), scale_part, data_rank * depth, 1
            ),
            sum(sums),
        ]
    )
    vectors = vectors + swap(vectors, "dp", 1) + swap(vectors, "dp", 2) + swap(vectors, "dp", 3)
    new_state = update(place, normed_all, projs, 0, state, new_state, 0, 2 * head_cols)
    vectors = after(vectors, new_state[0])
    vectors = vectors + swap(vectors, "tensor", 1)
    new_state = update(
        place, normed_all, projs, 2 * head_cols, state, new_state, 2 * head_cols, head_cols
    )
    return (input_grads, *new_state, vectors[None])


def from_behind(block, axis, distance):
    devices = range(lax.axis_size(axis))
    route = [(i - distance, i) for i in devices if i - distance in devices]
    return lax.ppermute(block, axis, route)


def normalize_rows(values_in):
    inverse = lax.rsqrt(jnp.mean(values_in * values_in, axis=-1, keepdims=True) + norm_eps)
    return (inverse, values_in * inverse)


def select_micro(array, micro_index):
    return lax.dynamic_index_in_dim(array, micro_index, 0, keepdims=False)


def store_slot(buffer, value, slot_index):
    return lax.dynamic_update_index_in_dim(buffer, value, slot_index, 0)


def local_any(x_in, out_grad, layer_scale, norm_gain, master, moment_one, moment_two):
    n_pipe = lax.axis_size("pipe")
    n_tensor = lax.axis_size("tensor")
    pipe_rank = lax.axis_index("pipe")
    micro_count = x_in.shape[1]
    images = x_in.shape[2]
    shard_len = x_in.shape[3]
    channels = x_in.shape[4]
    seq_len = shard_len * n_tensor
    row_start = lax.axis_index("tensor") * shard_len
    head_cols = master.shape[2] // 4
    local_heads = head_cols // HD
    score_root = math.sqrt(HD)
    scale_vec = layer_scale[0]
    gain_vec = norm_gain[0]
    weights = lax.all_gather(master[0].astype(jnp.bfloat16), "dp", axis=0, tiled=True)
    w_qkv = weights[:, : 3 * head_cols]
    w_out = weights[:, 3 * head_cols :]
    full_x = lax.all_gather(x_in[0], "tensor", axis=2, tiled=True).astype(jnp.float32)
    full_inverse, full_unit = normalize_rows(full_x)
    normed = (full_unit * gain_vec).astype(jnp.bfloat16)
    local_unit = lax.dynamic_slice_in_dim(full_unit, row_start, shard_len, 2)
    projected = jnp.einsum(
        "mbsd,dc->mbsc", normed, w_qkv, preferred_element_type=jnp.float32
    ).astype(jnp.bfloat16)
    projected = projected.reshape(micro_count, images, seq_len, 3, local_heads, HD)
    query = projected[:, :, :, 0]
    keys = projected[:, :, :, 1]
    values = projected[:, :, :, 2]
    scores = (
        jnp.einsum("mbqhe,mbkhe->mbhqk", query, keys, preferred_element_type=jnp.float32)
        / score_root
    )
    probs = jax.nn.softmax(scores, axis=-1)
    probs_low = probs.astype(jnp.bfloat16)
    attended = jnp.einsum(
        "mbhqk,mbkhe->mbqhe", probs_low, values, preferred_element_type=jnp.float32
    ).astype(jnp.bfloat16)
    attended_flat = attended.reshape(micro_count, images, seq_len, head_cols)

    def backward_segment(micro_index, incoming):
        query_now = select_micro(query, micro_index)
        keys_now = select_micro(keys, micro_index)
        values_now = select_micro(values, micro_index)
        probs_now = select_micro(probs, micro_index)
        probs_low_now = select_micro(probs_low, micro_index)
        attended_now = select_micro(attended, micro_index)
        scaled = (scale_vec * incoming.astype(jnp.float32)).astype(jnp.bfloat16)
        d_att = jnp.einsum("bsd,dc->bsc", scaled, w_out, preferred_element_type=jnp.float32).astype(
            jnp.bfloat16
        )
        d_att = d_att.reshape(images, seq_len, local_heads, HD)
        d_prob = jnp.einsum(
            "bqhe,bkhe->bhqk", d_att, values_now, preferred_element_type=jnp.float32
        )
        row_delta = jnp.einsum(
            "bqhe,bqhe->bhq", d_att, attended_now, preferred_element_type=jnp.float32
        )
        d_score = (probs_now * (d_prob - row_delta[..., None]) / score_root).astype(jnp.bfloat16)
        d_query = jnp.einsum(
            "bhqk,bkhe->bqhe", d_score, keys_now, preferred_element_type=jnp.float32
        ).astype(jnp.bfloat16)
        d_keys = jnp.einsum(
            "bhqk,bqhe->bkhe", d_score, query_now, preferred_element_type=jnp.float32
        ).astype(jnp.bfloat16)
        d_values = jnp.einsum(
            "bhqk,bqhe->bkhe", probs_low_now, d_att, preferred_element_type=jnp.float32
        ).astype(jnp.bfloat16)
        d_proj = jnp.concatenate([d_query, d_keys, d_values], axis=2).reshape(
            images, seq_len, 3 * head_cols
        )
        partial_sum = jnp.einsum("bsc,dc->bsd", d_proj, w_qkv, preferred_element_type=jnp.float32)
        return (partial_sum, d_proj, scaled)

    def spare_segment(micro_index, incoming):
        return (
            jnp.zeros((images, seq_len, channels), jnp.float32),
            jnp.zeros((images, seq_len, 3 * head_cols), jnp.bfloat16),
            jnp.zeros((images, seq_len, channels), jnp.bfloat16),
        )

    segments = n_pipe + micro_count - 1
    is_last = pipe_rank == n_pipe - 1
    received = jnp.zeros((images, seq_len, channels), jnp.bfloat16)
    slots = micro_count + 1
    grads_out = jnp.zeros((slots, images, shard_len, channels), jnp.bfloat16)
    proj_saved = jnp.zeros((slots, images, seq_len, 3 * head_cols), jnp.bfloat16)
    scaled_saved = jnp.zeros((slots, images, seq_len, channels), jnp.bfloat16)
    grad_saved = jnp.zeros((slots, images, seq_len, channels), jnp.bfloat16)
    gain_part = jnp.zeros((channels,), jnp.float32)
    for segment_step in range(segments):
        micro_index = segment_step - (n_pipe - 1) + pipe_rank
        active = jnp.logical_and(micro_index >= 0, micro_index < micro_count)
        micro_index = jnp.clip(micro_index, 0, micro_count - 1)
        slot_index = jnp.where(active, micro_index, micro_count)
        arrived = received
        incoming = jnp.where(is_last, select_micro(out_grad, micro_index), arrived)
        partial_sum, d_proj, scaled = lax.cond(
            active, backward_segment, spare_segment, micro_index, incoming
        )
        pieces = partial_sum.astype(jnp.bfloat16).reshape(images, n_tensor, shard_len, channels)
        landed = lax.all_to_all(pieces, "tensor", split_axis=1, concat_axis=1, tiled=True)
        own_d = jnp.sum(landed.astype(jnp.float32), axis=1)
        d_normed = lax.all_gather(own_d.astype(jnp.bfloat16), "tensor", axis=1, tiled=True).astype(
            own_d.dtype
        )
        own_unit = select_micro(local_unit, micro_index)
        sel_unit = select_micro(full_unit, micro_index)
        sel_inverse = select_micro(full_inverse, micro_index)
        d_unit = d_normed * gain_vec
        d_input = sel_inverse * (
            d_unit - sel_unit * jnp.mean(d_unit * sel_unit, axis=-1, keepdims=True)
        )
        passed = (incoming.astype(jnp.float32) + d_input).astype(jnp.bfloat16)
        own_passed = lax.dynamic_slice_in_dim(passed, row_start, shard_len, 1)
        gain_part = gain_part + jnp.where(active, jnp.sum(own_d * own_unit, axis=(0, 1)), 0.0)
        grads_out = store_slot(grads_out, own_passed, slot_index)
        proj_saved = store_slot(proj_saved, d_proj, slot_index)
        scaled_saved = store_slot(scaled_saved, scaled, slot_index)
        grad_saved = store_slot(grad_saved, incoming, slot_index)
        if segment_step + 1 < segments:
            received = from_behind(passed, "pipe", -1)
    grads_kept = grads_out[:micro_count]
    proj_kept = proj_saved[:micro_count]
    scaled_kept = scaled_saved[:micro_count]
    grad_kept = grad_saved[:micro_count]
    grad_qkv = jnp.einsum("mbsd,mbsc->dc", normed, proj_kept, preferred_element_type=jnp.float32)
    grad_out = jnp.einsum(
        "mbsd,mbsc->dc", scaled_kept, attended_flat, preferred_element_type=jnp.float32
    )
    weight_grad = lax.psum_scatter(
        jnp.concatenate([grad_qkv, grad_out], axis=1).astype(jnp.bfloat16),
        "dp",
        scatter_dimension=0,
        tiled=True,
    ).astype(jnp.float32)
    summed_out = jnp.einsum(
        "mbsd,mbsc->dc", grad_kept, attended_flat, preferred_element_type=jnp.float32
    )
    scale_part = jnp.sum(w_out.astype(jnp.float32) * summed_out, axis=1)
    scale_grad, gain_grad = lax.psum((scale_part, gain_part), ("dp", "tensor"))
    bias_one = 1.0 - beta_one**adam_step
    bias_two = 1.0 - beta_two**adam_step
    first_new = beta_one * moment_one[0] + (1.0 - beta_one) * weight_grad
    second_new = beta_two * moment_two[0] + (1.0 - beta_two) * weight_grad * weight_grad
    update = first_new / bias_one / (jnp.sqrt(second_new / bias_two) + adam_eps)
    master_new = master[0] - learn_rate * (update + weight_decay * master[0])
    scale_both = jnp.stack([scale_grad, gain_grad])
    return (grads_kept[None], master_new[None], first_new[None], second_new[None], scale_both[None])


def solution(mesh):
    placed = (
        P("pipe", None, "dp", "tensor", None),
        P(None, "dp", None, None),
        P("pipe", None),
        P("pipe", None),
        P("pipe", "dp", "tensor"),
        P("pipe", "dp", "tensor"),
        P("pipe", "dp", "tensor"),
    )
    two_by_two = mesh.shape["dp"] == 4 and mesh.shape["tensor"] == 2
    return jax.shard_map(
        local_two_by_two if two_by_two else local_any,
        mesh=mesh,
        in_specs=placed,
        out_specs=(
            P("pipe", None, "dp", "tensor", None),
            P("pipe", "dp", "tensor"),
            P("pipe", "dp", "tensor"),
            P("pipe", "dp", "tensor"),
            P("pipe", None, None),
        ),
        check_vma=False,
    )
```

```python
import functools
import math

import jax
import jax.numpy as jnp
from jax import lax
from jax.experimental import pallas as pl
from jax.experimental.pallas import tpu as pltpu
from jax.sharding import PartitionSpec as P

HD = 128

beta_one = 0.9
beta_two = 0.95
adam_eps = 1e-08
learn_rate = 0.001
weight_decay = 0.05
adam_step = 100.0
norm_eps = 1e-06
VMEM_LIMIT = 64 * 1024 * 1024

VMEM = "vmem"
SMEM = pl.BlockSpec(memory_space=pltpu.SMEM)
ANY = pl.BlockSpec(memory_space=pl.ANY)
bf16 = jnp.bfloat16
f32 = jnp.float32


def dot(a, b, dims=((1,), (0,))):
    return lax.dot_general(a, b, (dims, ((), ())), preferred_element_type=jnp.float32)


def shape_of(shape, dtype):
    return jax.ShapeDtypeStruct(shape, dtype)


def round_up(value, unit):
    return (value + unit - 1) // unit * unit


def call(kernel, args, specs, outs, out_specs, scratch=(), aliases=None, moved=0):
    def spec_of(spec, value):
        if spec != VMEM:
            return spec
        return pl.BlockSpec(value.shape, lambda i: (0,) * len(value.shape))

    return pl.pallas_call(
        kernel,
        grid=(1,),
        out_shape=outs,
        in_specs=[spec_of(spec, value) for spec, value in zip(specs, args)],
        out_specs=[spec_of(spec, value) for spec, value in zip(out_specs, outs)],
        scratch_shapes=list(scratch),
        input_output_aliases=aliases or {},
        compiler_params=pltpu.CompilerParams(vmem_limit_bytes=VMEM_LIMIT),
        cost_estimate=pl.CostEstimate(flops=0, bytes_accessed=moved, transcendentals=0),
    )(*args)


def start_all(copies):
    for copy in copies:
        copy.start()


def wait_all(copies):
    for copy in copies:
        copy.wait()


def pick(ref, micro):
    return ref[micro] if len(ref.shape) == 3 else ref[...]


def rows_at(start, size):
    return pl.ds(pl.multiple_of(start, 16), size)


def normalize_kernel(
    place_ref, mine_ref, other_ref, gain_ref, _, normed_ref, sent_ref, turned_ref
):
    micros, shard, channels = mine_ref.shape
    rank = place_ref[5]
    normed_ref[...] = jnp.zeros_like(normed_ref)
    for m in range(micros):
        for source, at in ((mine_ref, rank), (other_ref, 1 - rank)):
            values = source[m].astype(f32)
            inverse = lax.rsqrt(jnp.mean(values * values, axis=-1, keepdims=True) + norm_eps)
            normed = (values * inverse * gain_ref[...]).astype(bf16)
            normed_ref[rows_at(m * 2 * shard + at * shard, shard), :channels] = normed
    sent_ref[...] = normed_ref[...]
    turned_ref[...] = normed_ref[...].T


def normalize(place, mine, other, gain, early):
    micros, shard, channels = mine.shape
    rows, padded = micros * shard * 2, round_up(channels, 128)
    return call(
        normalize_kernel,
        [place, mine, other, gain, early],
        [SMEM, VMEM, VMEM, VMEM, ANY],
        [shape_of((rows, padded), bf16)] * 2 + [shape_of((padded, rows), bf16)],
        [VMEM] * 3,
    )


def round_kernel(chunk, chunks, master_ref, low_ref, wide, sems):
    width = wide.shape[2]
    copies = [
        pltpu.make_async_copy(
            master_ref.at[0, :, pl.ds((n * chunks + chunk) * width, width)], wide.at[n], sems.at[n]
        )
        for n in range(4)
    ]
    start_all(copies)
    for n in range(4):
        copies[n].wait()
        low_ref[:, n * width : (n + 1) * width] = wide[n].astype(bf16)


def rounded_chunk(master, chunk, chunks):
    _, depth, cols = master.shape
    width = cols // 4 // chunks
    return call(
        functools.partial(round_kernel, chunk, chunks),
        [master],
        [ANY],
        [shape_of((depth, 4 * width), bf16)],
        [VMEM],
        [pltpu.VMEM((4, depth, width), f32), pltpu.SemaphoreType.DMA((4,))],
    )[0]


def attend(projected, att_ref, probs_ref, seq, width):
    root = math.sqrt(HD)
    heads = width // HD
    for m in range(projected.shape[0] // seq):
        span = slice(m * seq, (m + 1) * seq)
        for h in range(heads):
            query, keys, values = [
                projected[span, n * width + h * HD : n * width + (h + 1) * HD] for n in range(3)
            ]
            scores = dot(query, keys, ((1,), (1,))) * (1.0 / root)
            scores = jnp.exp(scores - jnp.max(scores, axis=-1, keepdims=True))
            probs = scores / jnp.sum(scores, axis=-1, keepdims=True)
            probs_ref[(m * heads + h) * seq : (m * heads + h + 1) * seq, :] = probs
            att_ref[span, h * HD : (h + 1) * HD] = dot(probs.astype(bf16), values).astype(bf16)


def forward_kernel(chunk, channels, seq, place_ref, normed_ref, *refs):
    pieces = refs[:4]
    *refs, normed, buffer, turned, acts, att, probs, sems, out_sems = refs
    targets = [ref.at[chunk] for ref in refs[-5:]]
    depth = pieces[0].shape[0]
    width = pieces[0].shape[1] // 4
    targets[1] = refs[-4].at[:, pl.ds(chunk * width, width)]
    copies = [
        pltpu.make_async_copy(piece, buffer.at[rows_at(place_ref[at], depth), :], sems.at[at])
        for at, piece in enumerate(pieces)
    ]
    copies.append(pltpu.make_async_copy(normed_ref, normed, sems.at[4]))
    start_all(copies)
    buffer[channels:, :] = jnp.zeros((buffer.shape[0] - channels, buffer.shape[1]), bf16)
    wait_all(copies)
    w_out = buffer.at[pl.ds(0, channels), pl.ds(3 * width, width)]
    written = [
        pltpu.make_async_copy(source, target, out_sems.at[n])
        for n, (source, target) in enumerate(zip((acts, att, probs, w_out, turned), targets))
    ]
    written[3].start()
    turned[...] = buffer[:, : 3 * width].T
    written[4].start()
    projected = dot(normed[...], buffer[:, : 3 * width]).astype(bf16)
    acts[...] = projected
    written[0].start()
    attend(projected, att, probs, seq, width)
    written[1].start()
    written[2].start()
    wait_all(written)


def saved_shapes(rows, width, chunks, seq):
    return [
        shape_of((chunks, rows, 3 * width), bf16),
        shape_of((rows, width * chunks), bf16),
        shape_of((chunks, rows * width // HD, seq), f32),
    ]


def forward(place, normed, pieces, chunk, chunks, channels, seq, earlier):
    rows, padded = normed.shape
    cols = pieces[0].shape[1]
    width = cols // 4
    outs = saved_shapes(rows, width, chunks, seq) + [
        shape_of((chunks, channels, width), bf16),
        shape_of((chunks, 3 * width, padded), bf16),
    ]
    args = [place, normed, *pieces]
    aliases = {}
    if earlier is not None:
        aliases = {len(args) + n: n for n in range(5)}
        args += list(earlier)
    return call(
        functools.partial(forward_kernel, chunk, channels, seq),
        args,
        [SMEM] + [ANY] * (len(args) - 1),
        outs,
        [ANY] * 5,
        [
            pltpu.VMEM((rows, padded), bf16),
            pltpu.VMEM((padded, cols), bf16),
            pltpu.VMEM((3 * width, padded), bf16),
            pltpu.VMEM((rows, 3 * width), bf16),
            pltpu.VMEM((rows, width), bf16),
            pltpu.VMEM((rows * width // HD, seq), f32),
            pltpu.SemaphoreType.DMA((5,)),
            pltpu.SemaphoreType.DMA((5,)),
        ],
        aliases,
        moved=3 * channels * cols,
    )


def forward_far_kernel(first, count, seq, normed_ref, turned_ref, *refs):
    *refs, normed, normed_turned, turned, acts, atts, probs, sems, out_sems = refs
    acts_ref, att_ref, probs_ref, turned_rows_ref = refs[-4:]
    copies = [pltpu.make_async_copy(normed_ref, normed, sems.at[count])]
    copies += [
        pltpu.make_async_copy(turned_ref.at[first + c], turned.at[c], sems.at[c])
        for c in range(count)
    ]
    start_all(copies)
    copies[0].wait()
    width = turned.shape[1] // 3
    written = []
    if first == 0:
        normed_turned[...] = normed[...].T
        written.append(
            pltpu.make_async_copy(normed_turned, turned_rows_ref, out_sems.at[0, 3])
        )
        written[-1].start()
    for c in range(count):
        copies[1 + c].wait()
        projected = dot(normed[...], turned[c], ((1,), (1,))).astype(bf16)
        acts[c] = projected
        attend(projected, atts.at[c], probs.at[c], seq, width)
        targets = (
            acts_ref.at[first + c],
            att_ref.at[:, pl.ds((first + c) * width, width)],
            probs_ref.at[first + c],
        )
        for n, source in enumerate((acts, atts, probs)):
            written.append(pltpu.make_async_copy(source.at[c], targets[n], out_sems.at[c, n]))
            written[-1].start()
    wait_all(written)


def forward_far(normed, turned, first, count, seq, earlier):
    rows, padded = normed.shape
    chunks, triple, _ = turned.shape
    width = triple // 3
    args = [normed, turned]
    aliases = {}
    if earlier is not None:
        aliases = {len(args) + n: n for n in range(4)}
        args += list(earlier)
    return call(
        functools.partial(forward_far_kernel, first, count, seq),
        args,
        [ANY] * len(args),
        [*saved_shapes(rows, width, chunks, seq), shape_of((padded, rows), bf16)],
        [ANY] * 4,
        [
            pltpu.VMEM((rows, padded), bf16),
            pltpu.VMEM((padded, rows), bf16),
            pltpu.VMEM((count, triple, padded), bf16),
            pltpu.VMEM((count, rows, triple), bf16),
            pltpu.VMEM((count, rows, width), bf16),
            pltpu.VMEM((count, rows * width // HD, seq), f32),
            pltpu.SemaphoreType.DMA((count + 1,)),
            pltpu.SemaphoreType.DMA((count, 4)),
        ],
        aliases,
    )


def loads_of(sources, buffers, sems, first, rows):
    acts, att, probs, w_out, *turned = sources
    chunks = acts.shape[0]
    heads = att.shape[1] // chunks // HD
    views = [
        (acts.at[:, pl.ds(first, rows), :], buffers[0]),
        (att.at[pl.ds(first, rows), :], buffers[1]),
        (probs.at[:, pl.ds(first * heads, rows * heads), :], buffers[2]),
        (w_out, buffers[3]),
    ]
    views += [(weight.at[c], buffers[4].at[c]) for weight in turned for c in range(chunks)]
    copies = [
        pltpu.make_async_copy(source, target, sems.at[n])
        for n, (source, target) in enumerate(views)
    ]
    return copies[:4], copies[4:]


def buffers_of(sources, rows):
    acts, att, probs, *weights = sources
    chunks, all_rows, triple = acts.shape
    buffers = [
        pltpu.VMEM((chunks, rows, triple), bf16),
        pltpu.VMEM((rows, att.shape[1]), bf16),
        pltpu.VMEM((chunks, probs.shape[1] * rows // all_rows, probs.shape[2]), f32),
    ]
    buffers += [pltpu.VMEM(weight.shape, bf16) for weight in weights]
    return [*buffers, pltpu.SemaphoreType.DMA((4 + chunks,))]


def head_gradients(scaled, seq, buffers, proj):
    root = math.sqrt(HD)
    acts, att, probs, w_outs = buffers[:4]
    chunks, _, triple = acts.shape
    width = triple // 3
    heads = width // HD
    head_cols = chunks * width
    d_atts = [dot(scaled, w_outs[c]).astype(bf16) for c in range(chunks)]
    for c in range(chunks):
        for m in range(scaled.shape[0] // seq):
            span = slice(m * seq, (m + 1) * seq)
            for h in range(heads):
                query, keys, values = [
                    acts[c, span, n * width + h * HD : n * width + (h + 1) * HD] for n in range(3)
                ]
                begin = c * width + h * HD
                attended = att[span, begin : begin + HD].astype(f32)
                at = (m * heads + h) * seq
                prob = probs[c, at : at + seq, :]
                d_head = d_atts[c][span, h * HD : (h + 1) * HD]
                d_prob = dot(d_head, values, ((1,), (1,)))
                delta = jnp.sum(d_head.astype(f32) * attended, axis=-1, keepdims=True)
                d_score = (prob * (d_prob - delta) * (1.0 / root)).astype(bf16)
                grads = (
                    dot(d_score, keys),
                    dot(d_score, query, ((0,), (0,))),
                    dot(prob.astype(bf16), d_head, ((0,), (0,))),
                )
                for n, value in enumerate(grads):
                    place = n * head_cols + begin
                    proj[span, place : place + HD] = value.astype(bf16)


def micro_of(ref, micro):
    return ref.at[micro] if len(ref.shape) == 3 else ref


def scaled_turned(scaled, padded):
    rows, channels = scaled.shape
    return jnp.concatenate([scaled, jnp.zeros((rows, padded - channels), bf16)], axis=1).T


def backward_kernel(chunks, micro, section, halves, seq, place_ref, scale_ref, *refs):
    sources, refs = refs[:5], refs[5:]
    *buffers, sems, total, proj, merged, turned_in, keep, send, own_sems = refs[-13:]
    refs = refs[:-13]
    rank = place_ref[5]
    active = place_ref[4] == section
    shard, channels = keep.shape
    if halves:
        mine_ref, other_ref, before_ref, *refs = refs
        proj_ref, turned_ref, keep_ref, send_ref, merged_ref = refs[-5:]

        @pl.when(jnp.logical_not(active))
        def _():
            hand_on(micro_of(before_ref, micro), merged, merged_ref, own_sems.at[0])

    else:
        incoming_ref, *refs = refs
        proj_ref, turned_ref, keep_ref, send_ref = refs[-4:]

    @pl.when(active)
    def _():
        if halves:
            arrive = [
                pltpu.make_async_copy(
                    ref, merged.at[rows_at(at * shard, shard), :], own_sems.at[n]
                )
                for n, (ref, at) in enumerate(((mine_ref, rank), (other_ref, 1 - rank)))
            ]
        else:
            arrive = [pltpu.make_async_copy(micro_of(incoming_ref, micro), merged, own_sems.at[0])]
        start_all(arrive)
        early, late = loads_of(sources, buffers, sems, micro * seq, seq)
        start_all(early)
        late[0].start()
        wait_all(arrive)
        outs = []

        def write(source, target):
            outs.append(pltpu.make_async_copy(source, target, own_sems.at[2 + len(outs)]))
            outs[-1].start()

        if halves:
            write(merged, merged_ref)
        scaled = (scale_ref[...] * merged[...].astype(f32)).astype(bf16)
        turned_in[...] = scaled_turned(scaled, turned_in.shape[0])
        write(turned_in, turned_ref)
        wait_all(early)
        start_all(late[1:])
        head_gradients(scaled, seq, buffers, proj)
        turned = buffers[4]
        width = turned.shape[1] // 3
        for c in range(chunks):
            late[c].wait()
            begin = [(n * chunks + c) * width for n in range(3)]
            grads = jnp.concatenate([proj[:, at : at + width] for at in begin], axis=1)
            part = dot(grads, turned[c])
            if c == 0:
                total[...] = part
            else:
                total[...] += part
        write(proj, proj_ref)
        send[...] = total[rows_at((1 - rank) * shard, shard), :channels].astype(bf16)
        write(send, send_ref)
        keep[...] = total[rows_at(rank * shard, shard), :channels].astype(bf16)
        write(keep, keep_ref)
        wait_all(outs)


def backward(place, scale, saved, weights, micro, section, seq, incoming, before, old):
    chunks, channels, width = weights[0].shape
    padded = weights[1].shape[2]
    halves = isinstance(incoming, tuple)
    args = [place, scale, *saved, *weights]
    args += [*incoming, before] if halves else [incoming]
    aliases = {}
    if old is not None:
        aliases = {len(args) + n: n for n in range(2)}
        args += list(old)
    outs = [
        shape_of((seq, 3 * width * chunks), bf16),
        shape_of((padded, seq), bf16),
        shape_of((seq // 2, channels), bf16),
        shape_of((seq // 2, channels), bf16),
    ]
    if halves:
        outs.append(shape_of((seq, channels), bf16))
    return call(
        functools.partial(backward_kernel, chunks, micro, section, halves, seq),
        args,
        [SMEM, VMEM] + [ANY] * (len(args) - 2),
        outs,
        [ANY] * len(outs),
        buffers_of([*saved, *weights], seq)
        + [
            pltpu.VMEM((seq, padded), f32),
            pltpu.VMEM((seq, 3 * width * chunks), bf16),
            pltpu.VMEM((seq, channels), bf16),
            pltpu.VMEM((padded, seq), bf16),
            pltpu.VMEM((seq // 2, channels), bf16),
            pltpu.VMEM((seq // 2, channels), bf16),
            pltpu.SemaphoreType.DMA((7,)),
        ],
        aliases,
    )


def backward_far_kernel(chunks, seq, scale_ref, *refs):
    sources = refs[:4]
    *refs, acts, atts, probs, w_outs, sems = refs[4:]
    buffers = (acts, atts, probs, w_outs)
    *incoming, proj_ref, turned_ref = refs
    loads, _ = loads_of(sources, buffers, sems, 0, proj_ref.shape[0])
    start_all(loads)
    scaled = jnp.concatenate(
        [(scale_ref[...] * ref[...].astype(f32)).astype(bf16) for ref in incoming]
    )
    turned_ref[...] = scaled_turned(scaled, turned_ref.shape[0])
    wait_all(loads)
    head_gradients(scaled, seq, buffers, proj_ref)


def backward_far(scale, saved, w_outs, seq, incoming):
    chunks, channels, width = w_outs.shape
    rows = len(incoming) * seq
    return call(
        functools.partial(backward_far_kernel, chunks, seq),
        [scale, *saved, w_outs, *incoming],
        [VMEM] + [ANY] * 4 + [VMEM] * len(incoming),
        [
            shape_of((rows, 3 * width * chunks), bf16),
            shape_of((round_up(channels, 128), rows), bf16),
        ],
        [VMEM] * 2,
        buffers_of([*saved, w_outs], rows),
    )


def hand_on(source, through, target, sem):
    for copy in (
        pltpu.make_async_copy(source, through, sem),
        pltpu.make_async_copy(through, target, sem),
    ):
        copy.start()
        copy.wait()


def input_kernel(micro, section, place_ref, gain_ref, keep_ref, landed_ref, grad_ref, x_ref, *refs):
    new_ref, sum_ref, keep, landed, grad, own, new, total, sems = refs[-9:]
    shard = keep.shape[0]

    @pl.when(place_ref[4] == section)
    def _():
        if len(grad_ref.shape) == 2:
            grad_from = grad_ref
        else:
            grad_from = grad_ref.at[micro, rows_at(place_ref[5] * shard, shard), :]
        loads = [
            pltpu.make_async_copy(source, target, sems.at[n])
            for n, (source, target) in enumerate(
                ((x_ref.at[micro], own), (keep_ref, keep), (landed_ref, landed), (grad_from, grad))
            )
        ]
        start_all(loads)
        loads[0].wait()
        wide = own[...].astype(f32)
        inverse = lax.rsqrt(jnp.mean(wide * wide, axis=-1, keepdims=True) + norm_eps)
        unit = wide * inverse
        wait_all(loads[1:])
        d_normed = keep[...].astype(f32) + landed[...].astype(f32)
        d_unit = d_normed * gain_ref[...]
        d_input = inverse * (d_unit - unit * jnp.mean(d_unit * unit, axis=-1, keepdims=True))
        new[...] = (grad[...].astype(f32) + d_input).astype(bf16)
        out = pltpu.make_async_copy(new, new_ref, sems.at[4])
        out.start()
        total[...] = jnp.sum(d_normed * unit, axis=0, keepdims=True)
        out_sum = pltpu.make_async_copy(total, sum_ref, sems.at[5])
        out_sum.start()
        out.wait()
        out_sum.wait()


def input_gradient(place, keep, landed, grad, x_own, micro, section, gain, old):
    shard, channels = keep.shape
    args = [place, gain, keep, landed, grad, x_own, *old]
    return call(
        functools.partial(input_kernel, micro, section),
        args,
        [SMEM, VMEM] + [ANY] * (len(args) - 2),
        [shape_of((shard, channels), bf16), shape_of((1, channels), f32)],
        [ANY, ANY],
        [
            *[pltpu.VMEM((shard, channels), bf16)] * 5,
            pltpu.VMEM((1, channels), f32),
            pltpu.SemaphoreType.DMA((6,)),
        ],
        {6 + n: n for n in range(len(old))},
    )


def adam(grad, master, first, second):
    bias_one = 1.0 - beta_one**adam_step
    bias_two = 1.0 - beta_two**adam_step
    first_new = beta_one * first + (1.0 - beta_one) * grad
    second_new = beta_two * second + (1.0 - beta_two) * grad * grad
    corrected = second_new * (1.0 / bias_two)
    root = corrected * lax.rsqrt(corrected)
    update = first_new * (learn_rate / bias_one) / (root + adam_eps)
    return master * (1.0 - learn_rate * weight_decay) - update, first_new, second_new


AHEAD = 3


def update_kernel(lefts, parts, first, right_col, first_col, blocks, place_ref, *refs):
    turned, refs = refs[:lefts], refs[lefts:]
    rights, refs = refs[:parts], refs[parts:]
    state, refs = refs[:3], refs[3:]
    if not first:
        refs = refs[3:]
    new_state, refs = refs[:3], refs[3:]
    sums = None
    if first:
        sums, refs = refs[0], refs[1:]
    left, right, held, left_sems, right_sems, in_sems, out_sems = refs
    depth = left.shape[0]
    width = right.shape[2]

    left_copies, begin = [], 0
    for at, value in enumerate(turned):
        rows = value.shape[1]
        left_copies.append(
            pltpu.make_async_copy(
                value.at[rows_at(place_ref[0], depth), :],
                left.at[:, pl.ds(begin, rows)],
                left_sems.at[at],
            )
        )
        begin += rows

    def loads(block):
        copies, begin = [], 0
        for at, value in enumerate(rights):
            rows = value.shape[0]
            copies.append(
                pltpu.make_async_copy(
                    value.at[:, pl.ds(right_col + block * width, width)],
                    right.at[block, pl.ds(begin, rows), :],
                    right_sems.at[block, at],
                )
            )
            begin += rows
        for at, value in enumerate(state):
            copies.append(
                pltpu.make_async_copy(
                    value.at[0, :, pl.ds(first_col + block * width, width)],
                    held.at[block, at],
                    in_sems.at[block, at],
                )
            )
        return copies

    pending = [loads(block) for block in range(blocks)]
    start_all(left_copies)
    for block in range(min(AHEAD, blocks)):
        start_all(pending[block])
    wait_all(left_copies)
    written = []
    for block in range(blocks):
        wait_all(pending[block])
        if block + AHEAD < blocks:
            start_all(pending[block + AHEAD])
        grad = dot(left[...], right[block])
        master = held[block, 0]
        values = adam(grad, master, held[block, 1], held[block, 2])
        if first:
            low = master.astype(bf16).astype(f32)
            part = jnp.sum(low * grad, axis=1, keepdims=True)
            if block == 0:
                sums[...] = part
            else:
                sums[...] += part
        for at, value in enumerate(values):
            held[block, at] = value
            written.append(
                pltpu.make_async_copy(
                    held.at[block, at],
                    new_state[at].at[0, :, pl.ds(first_col + block * width, width)],
                    out_sems.at[block, at],
                )
            )
            written[-1].start()
    wait_all(written)


def update(place, turned, rights, right_col, state, earlier, first_col, cols, block=512):
    _, depth, _ = state[0].shape
    tokens = sum(value.shape[1] for value in turned)
    first = earlier is None
    blocks = cols // block
    args = [place, *turned, *rights, *state]
    outs = [shape_of(state[0].shape, f32)] * 3
    out_specs = [ANY] * 3
    aliases = {}
    if first:
        outs.append(shape_of((depth, 1), f32))
        out_specs.append(VMEM)
    else:
        aliases = {len(args) + i: i for i in range(3)}
        args += list(earlier)
    return call(
        functools.partial(
            update_kernel, len(turned), len(rights), first, right_col, first_col, blocks
        ),
        args,
        [SMEM] + [ANY] * (len(args) - 1),
        outs,
        out_specs,
        [
            pltpu.VMEM((depth, tokens), bf16),
            pltpu.VMEM((blocks, tokens, block), bf16),
            pltpu.VMEM((blocks, 3, depth, block), f32),
            pltpu.SemaphoreType.DMA((len(turned),)),
            pltpu.SemaphoreType.DMA((blocks, len(rights))),
            pltpu.SemaphoreType.DMA((blocks, 3)),
            pltpu.SemaphoreType.DMA((blocks, 3)),
        ],
        aliases,
        moved=24 * depth * cols,
    )


def swap(value, axis, mask):
    return lax.ppermute(value, axis, [(i, i ^ mask) for i in range(lax.axis_size(axis))])


def after(value, *others):
    return lax.optimization_barrier((value, *others))[0]


def local_two_by_two(x_in, out_grad, layer_scale, norm_gain, master, moment_one, moment_two):
    n_pipe = lax.axis_size("pipe")
    pipe_rank = lax.axis_index("pipe")
    data_rank = lax.axis_index("dp")
    rank = lax.axis_index("tensor")
    micros, _, shard, channels = x_in.shape[1:]
    seq = shard * 2
    depth, all_cols = master.shape[1:]
    head_cols = all_cols // 4
    chunks = 4 if head_cols % (4 * HD) == 0 else 1
    width = head_cols // chunks
    gain, scale = norm_gain, layer_scale
    place = jnp.stack(
        [(data_rank ^ k) * depth for k in range(4)] + [pipe_rank, rank]
    ).astype(jnp.int32)

    x_own = x_in[0, :, 0]
    x_other = swap(x_own, "tensor", 1)

    own = [rounded_chunk(master, c, chunks) for c in range(chunks)]
    far = [swap(value, "dp", 2) for value in own]
    if chunks > 2:
        x_other, own[2], own[3], far[0], far[1] = lax.optimization_barrier(
            (x_other, own[2], own[3], far[0], far[1])
        )
        far[2:] = [swap(value, "dp", 2) for value in own[2:]]
    normed, normed_sent, normed_turned = normalize(place, x_own, x_other, gain, out_grad[:, 0])
    values = None
    for c in range(chunks):
        arrived = far[c] if c < 2 else after(far[c], values[0])
        pieces = [own[c], swap(own[c], "dp", 1), arrived, swap(arrived, "dp", 1)]
        values = forward(place, normed, pieces, c, chunks, channels, seq, values)
    saved, weights = values[:3], values[3:]
    normed_far = swap(after(normed_sent, far[-1]), "dp", 2)

    def with_sibling(values):
        return [*values, *[swap(value, "dp", 1) for value in values]]

    kept = [None] * micros
    passed = [None] * micros
    sums = [None] * micros
    incoming = [out_grad[:, 0]] * micros
    incoming_far = [None] * micros
    straight = [(i + 1, i) for i in range(n_pipe - 1)]
    bounds = [min(chunks, 2 * n) for n in range(n_pipe)]
    saved_far = None
    for stage in range(n_pipe):
        section = n_pipe - 1 - stage
        own_rows = list(incoming)
        arrived = list(incoming)
        if stage > 0:
            own_rows = [lax.ppermute(passed[m], "pipe", straight) for m in range(micros)]
            part = bounds[stage] - bounds[stage - 1]
            if part:
                saved_far = forward_far(
                    after(normed_far, *passed), weights[1], bounds[stage - 1], part, seq, saved_far
                )
                own_rows = [after(mine, saved_far[0]) for mine in own_rows]
            arrived = [(mine, swap(mine, "tensor", 1)) for mine in own_rows]
        sent = []
        for m in range(micros):
            if sent:
                first = sent[0][0]
                if isinstance(arrived[m], tuple):
                    arrived[m] = (arrived[m][0], after(arrived[m][1], first))
                else:
                    arrived[m] = after(arrived[m], first)
            outs = backward(
                place, scale, saved, weights, m, section, seq, arrived[m], incoming[m], kept[m]
            )
            kept[m], (keep, send) = outs[:2], outs[2:4]
            if len(outs) > 4:
                incoming[m] = outs[4]
            if stage == n_pipe - 1:
                incoming_far[m] = swap(incoming[m], "dp", 2)
            sent.append((keep, swap(send, "tensor", 1)))
        for m in range(micros):
            old = [] if stage == 0 else [passed[m], sums[m]]
            passed[m], sums[m] = input_gradient(
                place, *sent[m], own_rows[m], x_own, m, section, gain, old
            )
    input_grads = jnp.stack(passed)[None, :, None]

    attended = with_sibling([saved[1], saved_far[1]])
    normed_all = with_sibling([normed_turned, saved_far[3]])
    incoming_far, attended[2], attended[3], normed_all[2], normed_all[3] = lax.optimization_barrier(
        (incoming_far, *attended[2:], *normed_all[2:], *passed)
    )[: -len(passed)]
    proj_far, scaled_far = backward_far(scale, saved_far[:3], weights[0], seq, incoming_far)

    state = [master, moment_one, moment_two]
    scaled_all = with_sibling([*[value[1] for value in kept], scaled_far])
    projs = with_sibling([*[value[0] for value in kept], proj_far])
    projs[-1], scaled_all[-1] = lax.optimization_barrier((projs[-1], scaled_all[-1]))
    *new_state, row_sums = update(
        place, scaled_all, attended, 0, state, None, 3 * head_cols, head_cols
    )
    scale_part = row_sums.T / lax.dynamic_slice_in_dim(scale, data_rank * depth, depth, 1)
    vectors = jnp.concatenate(
        [
            lax.dynamic_update_slice_in_dim(
                jnp.zeros((1, channels), f32), scale_part, data_rank * depth, 1
            ),
            sum(sums),
        ]
    )
    vectors = vectors + swap(vectors, "dp", 1) + swap(vectors, "dp", 2) + swap(vectors, "dp", 3)
    new_state = update(place, normed_all, projs, 0, state, new_state, 0, 2 * head_cols)
    vectors = after(vectors, new_state[0])
    vectors = vectors + swap(vectors, "tensor", 1)
    new_state = update(
        place, normed_all, projs, 2 * head_cols, state, new_state, 2 * head_cols, head_cols
    )
    return (input_grads, *new_state, vectors[None])


def from_behind(block, axis, distance):
    devices = range(lax.axis_size(axis))
    route = [(i - distance, i) for i in devices if i - distance in devices]
    return lax.ppermute(block, axis, route)


def normalize_rows(values_in):
    inverse = lax.rsqrt(jnp.mean(values_in * values_in, axis=-1, keepdims=True) + norm_eps)
    return (inverse, values_in * inverse)


def select_micro(array, micro_index):
    return lax.dynamic_index_in_dim(array, micro_index, 0, keepdims=False)


def store_slot(buffer, value, slot_index):
    return lax.dynamic_update_index_in_dim(buffer, value, slot_index, 0)


def local_any(x_in, out_grad, layer_scale, norm_gain, master, moment_one, moment_two):
    n_pipe = lax.axis_size("pipe")
    n_tensor = lax.axis_size("tensor")
    pipe_rank = lax.axis_index("pipe")
    micro_count = x_in.shape[1]
    images = x_in.shape[2]
    shard_len = x_in.shape[3]
    channels = x_in.shape[4]
    seq_len = shard_len * n_tensor
    row_start = lax.axis_index("tensor") * shard_len
    head_cols = master.shape[2] // 4
    local_heads = head_cols // HD
    score_root = math.sqrt(HD)
    scale_vec = layer_scale[0]
    gain_vec = norm_gain[0]
    weights = lax.all_gather(master[0].astype(jnp.bfloat16), "dp", axis=0, tiled=True)
    w_qkv = weights[:, : 3 * head_cols]
    w_out = weights[:, 3 * head_cols :]
    full_x = lax.all_gather(x_in[0], "tensor", axis=2, tiled=True).astype(jnp.float32)
    full_inverse, full_unit = normalize_rows(full_x)
    normed = (full_unit * gain_vec).astype(jnp.bfloat16)
    local_unit = lax.dynamic_slice_in_dim(full_unit, row_start, shard_len, 2)
    projected = jnp.einsum(
        "mbsd,dc->mbsc", normed, w_qkv, preferred_element_type=jnp.float32
    ).astype(jnp.bfloat16)
    projected = projected.reshape(micro_count, images, seq_len, 3, local_heads, HD)
    query = projected[:, :, :, 0]
    keys = projected[:, :, :, 1]
    values = projected[:, :, :, 2]
    scores = (
        jnp.einsum("mbqhe,mbkhe->mbhqk", query, keys, preferred_element_type=jnp.float32)
        / score_root
    )
    probs = jax.nn.softmax(scores, axis=-1)
    probs_low = probs.astype(jnp.bfloat16)
    attended = jnp.einsum(
        "mbhqk,mbkhe->mbqhe", probs_low, values, preferred_element_type=jnp.float32
    ).astype(jnp.bfloat16)
    attended_flat = attended.reshape(micro_count, images, seq_len, head_cols)

    def backward_segment(micro_index, incoming):
        query_now = select_micro(query, micro_index)
        keys_now = select_micro(keys, micro_index)
        values_now = select_micro(values, micro_index)
        probs_now = select_micro(probs, micro_index)
        probs_low_now = select_micro(probs_low, micro_index)
        attended_now = select_micro(attended, micro_index)
        scaled = (scale_vec * incoming.astype(jnp.float32)).astype(jnp.bfloat16)
        d_att = jnp.einsum("bsd,dc->bsc", scaled, w_out, preferred_element_type=jnp.float32).astype(
            jnp.bfloat16
        )
        d_att = d_att.reshape(images, seq_len, local_heads, HD)
        d_prob = jnp.einsum(
            "bqhe,bkhe->bhqk", d_att, values_now, preferred_element_type=jnp.float32
        )
        row_delta = jnp.einsum(
            "bqhe,bqhe->bhq", d_att, attended_now, preferred_element_type=jnp.float32
        )
        d_score = (probs_now * (d_prob - row_delta[..., None]) / score_root).astype(jnp.bfloat16)
        d_query = jnp.einsum(
            "bhqk,bkhe->bqhe", d_score, keys_now, preferred_element_type=jnp.float32
        ).astype(jnp.bfloat16)
        d_keys = jnp.einsum(
            "bhqk,bqhe->bkhe", d_score, query_now, preferred_element_type=jnp.float32
        ).astype(jnp.bfloat16)
        d_values = jnp.einsum(
            "bhqk,bqhe->bkhe", probs_low_now, d_att, preferred_element_type=jnp.float32
        ).astype(jnp.bfloat16)
        d_proj = jnp.concatenate([d_query, d_keys, d_values], axis=2).reshape(
            images, seq_len, 3 * head_cols
        )
        partial_sum = jnp.einsum("bsc,dc->bsd", d_proj, w_qkv, preferred_element_type=jnp.float32)
        return (partial_sum, d_proj, scaled)

    def spare_segment(micro_index, incoming):
        return (
            jnp.zeros((images, seq_len, channels), jnp.float32),
            jnp.zeros((images, seq_len, 3 * head_cols), jnp.bfloat16),
            jnp.zeros((images, seq_len, channels), jnp.bfloat16),
        )

    segments = n_pipe + micro_count - 1
    is_last = pipe_rank == n_pipe - 1
    received = jnp.zeros((images, seq_len, channels), jnp.bfloat16)
    slots = micro_count + 1
    grads_out = jnp.zeros((slots, images, shard_len, channels), jnp.bfloat16)
    proj_saved = jnp.zeros((slots, images, seq_len, 3 * head_cols), jnp.bfloat16)
    scaled_saved = jnp.zeros((slots, images, seq_len, channels), jnp.bfloat16)
    grad_saved = jnp.zeros((slots, images, seq_len, channels), jnp.bfloat16)
    gain_part = jnp.zeros((channels,), jnp.float32)
    for segment_step in range(segments):
        micro_index = segment_step - (n_pipe - 1) + pipe_rank
        active = jnp.logical_and(micro_index >= 0, micro_index < micro_count)
        micro_index = jnp.clip(micro_index, 0, micro_count - 1)
        slot_index = jnp.where(active, micro_index, micro_count)
        arrived = received
        incoming = jnp.where(is_last, select_micro(out_grad, micro_index), arrived)
        partial_sum, d_proj, scaled = lax.cond(
            active, backward_segment, spare_segment, micro_index, incoming
        )
        pieces = partial_sum.astype(jnp.bfloat16).reshape(images, n_tensor, shard_len, channels)
        landed = lax.all_to_all(pieces, "tensor", split_axis=1, concat_axis=1, tiled=True)
        own_d = jnp.sum(landed.astype(jnp.float32), axis=1)
        d_normed = lax.all_gather(own_d.astype(jnp.bfloat16), "tensor", axis=1, tiled=True).astype(
            own_d.dtype
        )
        own_unit = select_micro(local_unit, micro_index)
        sel_unit = select_micro(full_unit, micro_index)
        sel_inverse = select_micro(full_inverse, micro_index)
        d_unit = d_normed * gain_vec
        d_input = sel_inverse * (
            d_unit - sel_unit * jnp.mean(d_unit * sel_unit, axis=-1, keepdims=True)
        )
        passed = (incoming.astype(jnp.float32) + d_input).astype(jnp.bfloat16)
        own_passed = lax.dynamic_slice_in_dim(passed, row_start, shard_len, 1)
        gain_part = gain_part + jnp.where(active, jnp.sum(own_d * own_unit, axis=(0, 1)), 0.0)
        grads_out = store_slot(grads_out, own_passed, slot_index)
        proj_saved = store_slot(proj_saved, d_proj, slot_index)
        scaled_saved = store_slot(scaled_saved, scaled, slot_index)
        grad_saved = store_slot(grad_saved, incoming, slot_index)
        if segment_step + 1 < segments:
            received = from_behind(passed, "pipe", -1)
    grads_kept = grads_out[:micro_count]
    proj_kept = proj_saved[:micro_count]
    scaled_kept = scaled_saved[:micro_count]
    grad_kept = grad_saved[:micro_count]
    grad_qkv = jnp.einsum("mbsd,mbsc->dc", normed, proj_kept, preferred_element_type=jnp.float32)
    grad_out = jnp.einsum(
        "mbsd,mbsc->dc", scaled_kept, attended_flat, preferred_element_type=jnp.float32
    )
    weight_grad = lax.psum_scatter(
        jnp.concatenate([grad_qkv, grad_out], axis=1).astype(jnp.bfloat16),
        "dp",
        scatter_dimension=0,
        tiled=True,
    ).astype(jnp.float32)
    summed_out = jnp.einsum(
        "mbsd,mbsc->dc", grad_kept, attended_flat, preferred_element_type=jnp.float32
    )
    scale_part = jnp.sum(w_out.astype(jnp.float32) * summed_out, axis=1)
    scale_grad, gain_grad = lax.psum((scale_part, gain_part), ("dp", "tensor"))
    bias_one = 1.0 - beta_one**adam_step
    bias_two = 1.0 - beta_two**adam_step
    first_new = beta_one * moment_one[0] + (1.0 - beta_one) * weight_grad
    second_new = beta_two * moment_two[0] + (1.0 - beta_two) * weight_grad * weight_grad
    update = first_new / bias_one / (jnp.sqrt(second_new / bias_two) + adam_eps)
    master_new = master[0] - learn_rate * (update + weight_decay * master[0])
    scale_both = jnp.stack([scale_grad, gain_grad])
    return (grads_kept[None], master_new[None], first_new[None], second_new[None], scale_both[None])


def solution(mesh):
    placed = (
        P("pipe", None, "dp", "tensor", None),
        P(None, "dp", None, None),
        P("pipe", None),
        P("pipe", None),
        P("pipe", "dp", "tensor"),
        P("pipe", "dp", "tensor"),
        P("pipe", "dp", "tensor"),
    )
    two_by_two = mesh.shape["dp"] == 4 and mesh.shape["tensor"] == 2
    return jax.shard_map(
        local_two_by_two if two_by_two else local_any,
        mesh=mesh,
        in_specs=placed,
        out_specs=(
            P("pipe", None, "dp", "tensor", None),
            P("pipe", "dp", "tensor"),
            P("pipe", "dp", "tensor"),
            P("pipe", "dp", "tensor"),
            P("pipe", None, None),
        ),
        check_vma=False,
    )
```

```python
import functools
import math

import jax
import jax.numpy as jnp
from jax import lax
from jax.experimental import pallas as pl
from jax.experimental.pallas import tpu as pltpu
from jax.sharding import PartitionSpec as P

HD = 128

beta_one = 0.9
beta_two = 0.95
adam_eps = 1e-08
learn_rate = 0.001
weight_decay = 0.05
adam_step = 100.0
norm_eps = 1e-06
VMEM_LIMIT = 64 * 1024 * 1024

VMEM = "vmem"
SMEM = pl.BlockSpec(memory_space=pltpu.SMEM)
ANY = pl.BlockSpec(memory_space=pl.ANY)
bf16 = jnp.bfloat16
f32 = jnp.float32


def dot(a, b, dims=((1,), (0,))):
    return lax.dot_general(a, b, (dims, ((), ())), preferred_element_type=jnp.float32)


def shape_of(shape, dtype):
    return jax.ShapeDtypeStruct(shape, dtype)


def round_up(value, unit):
    return (value + unit - 1) // unit * unit


def call(kernel, args, specs, outs, out_specs, scratch=(), aliases=None, moved=0):
    def spec_of(spec, value):
        if spec != VMEM:
            return spec
        return pl.BlockSpec(value.shape, lambda i: (0,) * len(value.shape))

    return pl.pallas_call(
        kernel,
        grid=(1,),
        out_shape=outs,
        in_specs=[spec_of(spec, value) for spec, value in zip(specs, args)],
        out_specs=[spec_of(spec, value) for spec, value in zip(out_specs, outs)],
        scratch_shapes=list(scratch),
        input_output_aliases=aliases or {},
        compiler_params=pltpu.CompilerParams(vmem_limit_bytes=VMEM_LIMIT),
        cost_estimate=pl.CostEstimate(flops=0, bytes_accessed=moved, transcendentals=0),
    )(*args)


def start_all(copies):
    for copy in copies:
        copy.start()


def wait_all(copies):
    for copy in copies:
        copy.wait()


def pick(ref, micro):
    return ref[micro] if len(ref.shape) == 3 else ref[...]


def rows_at(start, size):
    return pl.ds(pl.multiple_of(start, 16), size)


def normalize_kernel(
    place_ref, mine_ref, other_ref, gain_ref, _, normed_ref, sent_ref, turned_ref
):
    micros, shard, channels = mine_ref.shape
    rank = place_ref[5]
    normed_ref[...] = jnp.zeros_like(normed_ref)
    for m in range(micros):
        for source, at in ((mine_ref, rank), (other_ref, 1 - rank)):
            values = source[m].astype(f32)
            inverse = lax.rsqrt(jnp.mean(values * values, axis=-1, keepdims=True) + norm_eps)
            normed = (values * inverse * gain_ref[...]).astype(bf16)
            normed_ref[rows_at(m * 2 * shard + at * shard, shard), :channels] = normed
    sent_ref[...] = normed_ref[...]
    turned_ref[...] = normed_ref[...].T


def normalize(place, mine, other, gain, early):
    micros, shard, channels = mine.shape
    rows, padded = micros * shard * 2, round_up(channels, 128)
    return call(
        normalize_kernel,
        [place, mine, other, gain, early],
        [SMEM, VMEM, VMEM, VMEM, ANY],
        [shape_of((rows, padded), bf16)] * 2 + [shape_of((padded, rows), bf16)],
        [VMEM] * 3,
    )


def round_kernel(chunk, chunks, master_ref, low_ref, wide, sems):
    width = wide.shape[2]
    copies = [
        pltpu.make_async_copy(
            master_ref.at[0, :, pl.ds((n * chunks + chunk) * width, width)], wide.at[n], sems.at[n]
        )
        for n in range(4)
    ]
    start_all(copies)
    for n in range(4):
        copies[n].wait()
        low_ref[:, n * width : (n + 1) * width] = wide[n].astype(bf16)


def rounded_chunk(master, chunk, chunks):
    _, depth, cols = master.shape
    width = cols // 4 // chunks
    return call(
        functools.partial(round_kernel, chunk, chunks),
        [master],
        [ANY],
        [shape_of((depth, 4 * width), bf16)],
        [VMEM],
        [pltpu.VMEM((4, depth, width), f32), pltpu.SemaphoreType.DMA((4,))],
    )[0]


def attend(projected, att_ref, probs_ref, seq, width):
    root = math.sqrt(HD)
    heads = width // HD
    for m in range(projected.shape[0] // seq):
        span = slice(m * seq, (m + 1) * seq)
        for h in range(heads):
            query, keys, values = [
                projected[span, n * width + h * HD : n * width + (h + 1) * HD] for n in range(3)
            ]
            scores = dot(query, keys, ((1,), (1,))) * (1.0 / root)
            scores = jnp.exp(scores - jnp.max(scores, axis=-1, keepdims=True))
            probs = scores / jnp.sum(scores, axis=-1, keepdims=True)
            probs_ref[(m * heads + h) * seq : (m * heads + h + 1) * seq, :] = probs
            att_ref[span, h * HD : (h + 1) * HD] = dot(probs.astype(bf16), values).astype(bf16)


def forward_kernel(chunk, channels, seq, place_ref, normed_ref, *refs):
    pieces = refs[:4]
    *refs, normed, buffer, turned, acts, att, probs, sems, out_sems = refs
    targets = [ref.at[chunk] for ref in refs[-5:]]
    depth = pieces[0].shape[0]
    width = pieces[0].shape[1] // 4
    targets[1] = refs[-4].at[:, pl.ds(chunk * width, width)]
    copies = [
        pltpu.make_async_copy(piece, buffer.at[rows_at(place_ref[at], depth), :], sems.at[at])
        for at, piece in enumerate(pieces)
    ]
    copies.append(pltpu.make_async_copy(normed_ref, normed, sems.at[4]))
    start_all(copies)
    buffer[channels:, :] = jnp.zeros((buffer.shape[0] - channels, buffer.shape[1]), bf16)
    wait_all(copies)
    w_out = buffer.at[pl.ds(0, channels), pl.ds(3 * width, width)]
    written = [
        pltpu.make_async_copy(source, target, out_sems.at[n])
        for n, (source, target) in enumerate(zip((acts, att, probs, w_out, turned), targets))
    ]
    written[3].start()
    turned[...] = buffer[:, : 3 * width].T
    written[4].start()
    projected = dot(normed[...], buffer[:, : 3 * width]).astype(bf16)
    acts[...] = projected
    written[0].start()
    attend(projected, att, probs, seq, width)
    written[1].start()
    written[2].start()
    wait_all(written)


def saved_shapes(rows, width, chunks, seq):
    return [
        shape_of((chunks, rows, 3 * width), bf16),
        shape_of((rows, width * chunks), bf16),
        shape_of((chunks, rows * width // HD, seq), f32),
    ]


def forward(place, normed, pieces, chunk, chunks, channels, seq, earlier):
    rows, padded = normed.shape
    cols = pieces[0].shape[1]
    width = cols // 4
    outs = saved_shapes(rows, width, chunks, seq) + [
        shape_of((chunks, channels, width), bf16),
        shape_of((chunks, 3 * width, padded), bf16),
    ]
    args = [place, normed, *pieces]
    aliases = {}
    if earlier is not None:
        aliases = {len(args) + n: n for n in range(5)}
        args += list(earlier)
    return call(
        functools.partial(forward_kernel, chunk, channels, seq),
        args,
        [SMEM] + [ANY] * (len(args) - 1),
        outs,
        [ANY] * 5,
        [
            pltpu.VMEM((rows, padded), bf16),
            pltpu.VMEM((padded, cols), bf16),
            pltpu.VMEM((3 * width, padded), bf16),
            pltpu.VMEM((rows, 3 * width), bf16),
            pltpu.VMEM((rows, width), bf16),
            pltpu.VMEM((rows * width // HD, seq), f32),
            pltpu.SemaphoreType.DMA((5,)),
            pltpu.SemaphoreType.DMA((5,)),
        ],
        aliases,
    )


def forward_far_kernel(first, count, seq, normed_ref, turned_ref, *refs):
    *refs, normed, normed_turned, turned, acts, atts, probs, sems, out_sems = refs
    acts_ref, att_ref, probs_ref, turned_rows_ref = refs[-4:]
    copies = [pltpu.make_async_copy(normed_ref, normed, sems.at[count])]
    copies += [
        pltpu.make_async_copy(turned_ref.at[first + c], turned.at[c], sems.at[c])
        for c in range(count)
    ]
    start_all(copies)
    copies[0].wait()
    width = turned.shape[1] // 3
    written = []
    if first == 0:
        normed_turned[...] = normed[...].T
        written.append(
            pltpu.make_async_copy(normed_turned, turned_rows_ref, out_sems.at[0, 3])
        )
        written[-1].start()
    for c in range(count):
        copies[1 + c].wait()
        projected = dot(normed[...], turned[c], ((1,), (1,))).astype(bf16)
        acts[c] = projected
        attend(projected, atts.at[c], probs.at[c], seq, width)
        targets = (
            acts_ref.at[first + c],
            att_ref.at[:, pl.ds((first + c) * width, width)],
            probs_ref.at[first + c],
        )
        for n, source in enumerate((acts, atts, probs)):
            written.append(pltpu.make_async_copy(source.at[c], targets[n], out_sems.at[c, n]))
            written[-1].start()
    wait_all(written)


def forward_far(normed, turned, first, count, seq, earlier):
    rows, padded = normed.shape
    chunks, triple, _ = turned.shape
    width = triple // 3
    args = [normed, turned]
    aliases = {}
    if earlier is not None:
        aliases = {len(args) + n: n for n in range(4)}
        args += list(earlier)
    return call(
        functools.partial(forward_far_kernel, first, count, seq),
        args,
        [ANY] * len(args),
        [*saved_shapes(rows, width, chunks, seq), shape_of((padded, rows), bf16)],
        [ANY] * 4,
        [
            pltpu.VMEM((rows, padded), bf16),
            pltpu.VMEM((padded, rows), bf16),
            pltpu.VMEM((count, triple, padded), bf16),
            pltpu.VMEM((count, rows, triple), bf16),
            pltpu.VMEM((count, rows, width), bf16),
            pltpu.VMEM((count, rows * width // HD, seq), f32),
            pltpu.SemaphoreType.DMA((count + 1,)),
            pltpu.SemaphoreType.DMA((count, 4)),
        ],
        aliases,
    )


def loads_of(sources, buffers, sems, first, rows):
    acts, att, probs, w_out, *turned = sources
    chunks = acts.shape[0]
    heads = att.shape[1] // chunks // HD
    views = [
        (acts.at[:, pl.ds(first, rows), :], buffers[0]),
        (att.at[pl.ds(first, rows), :], buffers[1]),
        (probs.at[:, pl.ds(first * heads, rows * heads), :], buffers[2]),
        (w_out, buffers[3]),
    ]
    views += [(weight.at[c], buffers[4].at[c]) for weight in turned for c in range(chunks)]
    copies = [
        pltpu.make_async_copy(source, target, sems.at[n])
        for n, (source, target) in enumerate(views)
    ]
    return copies[:4], copies[4:]


def buffers_of(sources, rows):
    acts, att, probs, *weights = sources
    chunks, all_rows, triple = acts.shape
    buffers = [
        pltpu.VMEM((chunks, rows, triple), bf16),
        pltpu.VMEM((rows, att.shape[1]), bf16),
        pltpu.VMEM((chunks, probs.shape[1] * rows // all_rows, probs.shape[2]), f32),
    ]
    buffers += [pltpu.VMEM(weight.shape, bf16) for weight in weights]
    return [*buffers, pltpu.SemaphoreType.DMA((4 + chunks,))]


def head_gradients(scaled, seq, buffers, proj):
    root = math.sqrt(HD)
    acts, att, probs, w_outs = buffers[:4]
    chunks, _, triple = acts.shape
    width = triple // 3
    heads = width // HD
    head_cols = chunks * width
    d_atts = [dot(scaled, w_outs[c]).astype(bf16) for c in range(chunks)]
    for c in range(chunks):
        for m in range(scaled.shape[0] // seq):
            span = slice(m * seq, (m + 1) * seq)
            for h in range(heads):
                query, keys, values = [
                    acts[c, span, n * width + h * HD : n * width + (h + 1) * HD] for n in range(3)
                ]
                begin = c * width + h * HD
                attended = att[span, begin : begin + HD].astype(f32)
                at = (m * heads + h) * seq
                prob = probs[c, at : at + seq, :]
                d_head = d_atts[c][span, h * HD : (h + 1) * HD]
                d_prob = dot(d_head, values, ((1,), (1,)))
                delta = jnp.sum(d_head.astype(f32) * attended, axis=-1, keepdims=True)
                d_score = (prob * (d_prob - delta) * (1.0 / root)).astype(bf16)
                grads = (
                    dot(d_score, keys),
                    dot(d_score, query, ((0,), (0,))),
                    dot(prob.astype(bf16), d_head, ((0,), (0,))),
                )
                for n, value in enumerate(grads):
                    place = n * head_cols + begin
                    proj[span, place : place + HD] = value.astype(bf16)


def micro_of(ref, micro):
    return ref.at[micro] if len(ref.shape) == 3 else ref


def scaled_turned(scaled, padded):
    rows, channels = scaled.shape
    return jnp.concatenate([scaled, jnp.zeros((rows, padded - channels), bf16)], axis=1).T


def backward_kernel(chunks, micro, section, halves, seq, place_ref, scale_ref, *refs):
    sources, refs = refs[:5], refs[5:]
    *buffers, sems, total, proj, merged, turned_in, keep, send, own_sems = refs[-13:]
    refs = refs[:-13]
    rank = place_ref[5]
    active = place_ref[4] == section
    shard, channels = keep.shape
    if halves:
        mine_ref, other_ref, before_ref, *refs = refs
        proj_ref, turned_ref, keep_ref, send_ref, merged_ref = refs[-5:]

        @pl.when(jnp.logical_not(active))
        def _():
            hand_on(micro_of(before_ref, micro), merged, merged_ref, own_sems.at[0])

    else:
        incoming_ref, *refs = refs
        proj_ref, turned_ref, keep_ref, send_ref = refs[-4:]

    @pl.when(active)
    def _():
        if halves:
            arrive = [
                pltpu.make_async_copy(
                    ref, merged.at[rows_at(at * shard, shard), :], own_sems.at[n]
                )
                for n, (ref, at) in enumerate(((mine_ref, rank), (other_ref, 1 - rank)))
            ]
        else:
            arrive = [pltpu.make_async_copy(micro_of(incoming_ref, micro), merged, own_sems.at[0])]
        start_all(arrive)
        early, late = loads_of(sources, buffers, sems, micro * seq, seq)
        start_all(early)
        late[0].start()
        wait_all(arrive)
        outs = []

        def write(source, target):
            outs.append(pltpu.make_async_copy(source, target, own_sems.at[2 + len(outs)]))
            outs[-1].start()

        if halves:
            write(merged, merged_ref)
        scaled = (scale_ref[...] * merged[...].astype(f32)).astype(bf16)
        turned_in[...] = scaled_turned(scaled, turned_in.shape[0])
        write(turned_in, turned_ref)
        wait_all(early)
        start_all(late[1:])
        head_gradients(scaled, seq, buffers, proj)
        turned = buffers[4]
        width = turned.shape[1] // 3
        for c in range(chunks):
            late[c].wait()
            begin = [(n * chunks + c) * width for n in range(3)]
            grads = jnp.concatenate([proj[:, at : at + width] for at in begin], axis=1)
            part = dot(grads, turned[c])
            if c == 0:
                total[...] = part
            else:
                total[...] += part
        write(proj, proj_ref)
        send[...] = total[rows_at((1 - rank) * shard, shard), :channels].astype(bf16)
        write(send, send_ref)
        keep[...] = total[rows_at(rank * shard, shard), :channels].astype(bf16)
        write(keep, keep_ref)
        wait_all(outs)


def backward(place, scale, saved, weights, micro, section, seq, incoming, before, old):
    chunks, channels, width = weights[0].shape
    padded = weights[1].shape[2]
    halves = isinstance(incoming, tuple)
    args = [place, scale, *saved, *weights]
    args += [*incoming, before] if halves else [incoming]
    aliases = {}
    if old is not None:
        aliases = {len(args) + n: n for n in range(2)}
        args += list(old)
    outs = [
        shape_of((seq, 3 * width * chunks), bf16),
        shape_of((padded, seq), bf16),
        shape_of((seq // 2, channels), bf16),
        shape_of((seq // 2, channels), bf16),
    ]
    if halves:
        outs.append(shape_of((seq, channels), bf16))
    return call(
        functools.partial(backward_kernel, chunks, micro, section, halves, seq),
        args,
        [SMEM, VMEM] + [ANY] * (len(args) - 2),
        outs,
        [ANY] * len(outs),
        buffers_of([*saved, *weights], seq)
        + [
            pltpu.VMEM((seq, padded), f32),
            pltpu.VMEM((seq, 3 * width * chunks), bf16),
            pltpu.VMEM((seq, channels), bf16),
            pltpu.VMEM((padded, seq), bf16),
            pltpu.VMEM((seq // 2, channels), bf16),
            pltpu.VMEM((seq // 2, channels), bf16),
            pltpu.SemaphoreType.DMA((7,)),
        ],
        aliases,
    )


def backward_far_kernel(micro, seq, scale_ref, *refs):
    sources = refs[:4]
    *refs, acts, atts, probs, w_outs, sems = refs[4:]
    buffers = (acts, atts, probs, w_outs)
    incoming_ref, proj_ref, turned_ref = refs
    loads, _ = loads_of(sources, buffers, sems, micro * seq, seq)
    start_all(loads)
    scaled = (scale_ref[...] * incoming_ref[...].astype(f32)).astype(bf16)
    turned_ref[...] = scaled_turned(scaled, turned_ref.shape[0])
    wait_all(loads)
    head_gradients(scaled, seq, buffers, proj_ref)


def backward_far(scale, saved, w_outs, seq, incoming, micro):
    chunks, channels, width = w_outs.shape
    return call(
        functools.partial(backward_far_kernel, micro, seq),
        [scale, *saved, w_outs, incoming],
        [VMEM] + [ANY] * 4 + [VMEM],
        [
            shape_of((seq, 3 * width * chunks), bf16),
            shape_of((round_up(channels, 128), seq), bf16),
        ],
        [VMEM] * 2,
        buffers_of([*saved, w_outs], seq),
    )


def hand_on(source, through, target, sem):
    for copy in (
        pltpu.make_async_copy(source, through, sem),
        pltpu.make_async_copy(through, target, sem),
    ):
        copy.start()
        copy.wait()


def input_kernel(micro, section, place_ref, gain_ref, keep_ref, landed_ref, grad_ref, x_ref, *refs):
    new_ref, sum_ref, keep, landed, grad, own, new, total, sems = refs[-9:]
    shard = keep.shape[0]

    @pl.when(place_ref[4] == section)
    def _():
        if len(grad_ref.shape) == 2:
            grad_from = grad_ref
        else:
            grad_from = grad_ref.at[micro, rows_at(place_ref[5] * shard, shard), :]
        loads = [
            pltpu.make_async_copy(source, target, sems.at[n])
            for n, (source, target) in enumerate(
                ((x_ref.at[micro], own), (keep_ref, keep), (landed_ref, landed), (grad_from, grad))
            )
        ]
        start_all(loads)
        loads[0].wait()
        wide = own[...].astype(f32)
        inverse = lax.rsqrt(jnp.mean(wide * wide, axis=-1, keepdims=True) + norm_eps)
        unit = wide * inverse
        wait_all(loads[1:])
        d_normed = keep[...].astype(f32) + landed[...].astype(f32)
        d_unit = d_normed * gain_ref[...]
        d_input = inverse * (d_unit - unit * jnp.mean(d_unit * unit, axis=-1, keepdims=True))
        new[...] = (grad[...].astype(f32) + d_input).astype(bf16)
        out = pltpu.make_async_copy(new, new_ref, sems.at[4])
        out.start()
        total[...] = jnp.sum(d_normed * unit, axis=0, keepdims=True)
        out_sum = pltpu.make_async_copy(total, sum_ref, sems.at[5])
        out_sum.start()
        out.wait()
        out_sum.wait()


def input_gradient(place, keep, landed, grad, x_own, micro, section, gain, old):
    shard, channels = keep.shape
    args = [place, gain, keep, landed, grad, x_own, *old]
    return call(
        functools.partial(input_kernel, micro, section),
        args,
        [SMEM, VMEM] + [ANY] * (len(args) - 2),
        [shape_of((shard, channels), bf16), shape_of((1, channels), f32)],
        [ANY, ANY],
        [
            *[pltpu.VMEM((shard, channels), bf16)] * 5,
            pltpu.VMEM((1, channels), f32),
            pltpu.SemaphoreType.DMA((6,)),
        ],
        {6 + n: n for n in range(len(old))},
    )


def adam(grad, master, first, second):
    bias_one = 1.0 - beta_one**adam_step
    bias_two = 1.0 - beta_two**adam_step
    first_new = beta_one * first + (1.0 - beta_one) * grad
    second_new = beta_two * second + (1.0 - beta_two) * grad * grad
    corrected = second_new * (1.0 / bias_two)
    root = corrected * lax.rsqrt(corrected)
    update = first_new * (learn_rate / bias_one) / (root + adam_eps)
    return master * (1.0 - learn_rate * weight_decay) - update, first_new, second_new


AHEAD = 3


def update_kernel(lefts, parts, first, right_col, first_col, blocks, place_ref, *refs):
    turned, refs = refs[:lefts], refs[lefts:]
    rights, refs = refs[:parts], refs[parts:]
    state, refs = refs[:3], refs[3:]
    if first:
        scale, refs = refs[0], refs[1:]
    else:
        refs = refs[3:]
    new_state, refs = refs[:3], refs[3:]
    if first:
        shares, refs = refs[0], refs[1:]
    left, right, held, left_sems, right_sems, in_sems, out_sems = refs
    depth = left.shape[0]
    width = right.shape[2]

    left_copies, begin = [], 0
    for at, value in enumerate(turned):
        rows = value.shape[1]
        left_copies.append(
            pltpu.make_async_copy(
                value.at[rows_at(place_ref[0], depth), :],
                left.at[:, pl.ds(begin, rows)],
                left_sems.at[at],
            )
        )
        begin += rows

    def loads(block):
        copies, begin = [], 0
        for at, value in enumerate(rights):
            rows = value.shape[0]
            copies.append(
                pltpu.make_async_copy(
                    value.at[:, pl.ds(right_col + block * width, width)],
                    right.at[block, pl.ds(begin, rows), :],
                    right_sems.at[block, at],
                )
            )
            begin += rows
        for at, value in enumerate(state):
            copies.append(
                pltpu.make_async_copy(
                    value.at[0, :, pl.ds(first_col + block * width, width)],
                    held.at[block, at],
                    in_sems.at[block, at],
                )
            )
        return copies

    pending = [loads(block) for block in range(blocks)]
    start_all(left_copies)
    for block in range(min(AHEAD, blocks)):
        start_all(pending[block])
    wait_all(left_copies)
    written = []
    for block in range(blocks):
        wait_all(pending[block])
        if block + AHEAD < blocks:
            start_all(pending[block + AHEAD])
        grad = dot(left[...], right[block])
        master = held[block, 0]
        values = adam(grad, master, held[block, 1], held[block, 2])
        if first:
            low = master.astype(bf16).astype(f32)
            part = jnp.sum(low * grad, axis=1, keepdims=True)
            sums = part if block == 0 else sums + part
            if block == blocks - 1:
                turned_sums = jnp.broadcast_to(sums, (depth, 128)).T
                shares[...] = turned_sums[:1, :] / scale[...]
        for at, value in enumerate(values):
            held[block, at] = value
            written.append(
                pltpu.make_async_copy(
                    held.at[block, at],
                    new_state[at].at[0, :, pl.ds(first_col + block * width, width)],
                    out_sems.at[block, at],
                )
            )
            written[-1].start()
    wait_all(written)


def update(place, turned, rights, right_col, state, earlier, first_col, cols, scale=None, block=512):
    _, depth, _ = state[0].shape
    tokens = sum(value.shape[1] for value in turned)
    first = earlier is None
    blocks = cols // block
    args = [place, *turned, *rights, *state]
    outs = [shape_of(state[0].shape, f32)] * 3
    out_specs = [ANY] * 3
    aliases = {}
    if first:
        outs.append(shape_of((1, depth), f32))
        out_specs.append(VMEM)
        args.append(scale)
    else:
        aliases = {len(args) + i: i for i in range(3)}
        args += list(earlier)
    return call(
        functools.partial(
            update_kernel, len(turned), len(rights), first, right_col, first_col, blocks
        ),
        args,
        [SMEM] + [ANY] * (len(args) - 2) + [VMEM if first else ANY],
        outs,
        out_specs,
        [
            pltpu.VMEM((depth, tokens), bf16),
            pltpu.VMEM((blocks, tokens, block), bf16),
            pltpu.VMEM((blocks, 3, depth, block), f32),
            pltpu.SemaphoreType.DMA((len(turned),)),
            pltpu.SemaphoreType.DMA((blocks, len(rights))),
            pltpu.SemaphoreType.DMA((blocks, 3)),
            pltpu.SemaphoreType.DMA((blocks, 3)),
        ],
        aliases,
        moved=24 * depth * cols,
    )


def swap(value, axis, mask):
    return lax.ppermute(value, axis, [(i, i ^ mask) for i in range(lax.axis_size(axis))])


def after(value, *others):
    return lax.optimization_barrier((value, *others))[0]


def local_two_by_two(x_in, out_grad, layer_scale, norm_gain, master, moment_one, moment_two):
    n_pipe = lax.axis_size("pipe")
    pipe_rank = lax.axis_index("pipe")
    data_rank = lax.axis_index("dp")
    rank = lax.axis_index("tensor")
    micros, _, shard, channels = x_in.shape[1:]
    seq = shard * 2
    depth, all_cols = master.shape[1:]
    head_cols = all_cols // 4
    chunks = 4 if head_cols % (4 * HD) == 0 else 1
    width = head_cols // chunks
    gain, scale = norm_gain, layer_scale
    place = jnp.stack(
        [(data_rank ^ k) * depth for k in range(4)] + [pipe_rank, rank]
    ).astype(jnp.int32)

    x_own = x_in[0, :, 0]
    x_other = swap(x_own, "tensor", 1)

    own = [rounded_chunk(master, c, chunks) for c in range(chunks)]
    far = [swap(value, "dp", 2) for value in own]
    normed, normed_sent, normed_turned = normalize(place, x_own, x_other, gain, out_grad[:, 0])
    if chunks > 1:
        normed, own[-1], *far[:-1] = lax.optimization_barrier((normed, own[-1], *far[:-1]))
        far[-1] = swap(own[-1], "dp", 2)
    values = None
    for c in range(chunks):
        arrived = far[c] if c < chunks - 1 or not values else after(far[c], values[0])
        pieces = [own[c], swap(own[c], "dp", 1), arrived, swap(arrived, "dp", 1)]
        values = forward(place, normed, pieces, c, chunks, channels, seq, values)
    saved, weights = values[:3], values[3:]
    normed_far = swap(after(normed_sent, far[-1]), "dp", 2)

    def with_sibling(values):
        return [*values, *[swap(value, "dp", 1) for value in values]]

    kept = [None] * micros
    passed = [None] * micros
    sums = [None] * micros
    incoming = [out_grad[:, 0]] * micros
    incoming_far = [None] * micros
    straight = [(i + 1, i) for i in range(n_pipe - 1)]
    bounds = [min(chunks, 2 * n) for n in range(n_pipe)]
    saved_far = None
    for stage in range(n_pipe):
        section = n_pipe - 1 - stage
        own_rows = list(incoming)
        arrived = list(incoming)
        if stage > 0:
            own_rows = [lax.ppermute(passed[m], "pipe", straight) for m in range(micros)]
            part = bounds[stage] - bounds[stage - 1]
            if part:
                saved_far = forward_far(
                    after(normed_far, *passed), weights[1], bounds[stage - 1], part, seq, saved_far
                )
                own_rows = [after(mine, saved_far[0]) for mine in own_rows]
            arrived = [(mine, swap(mine, "tensor", 1)) for mine in own_rows]
        sent = []
        for m in range(micros):
            if sent:
                first = sent[0][0]
                if isinstance(arrived[m], tuple):
                    arrived[m] = (arrived[m][0], after(arrived[m][1], first))
                else:
                    arrived[m] = after(arrived[m], first)
            outs = backward(
                place, scale, saved, weights, m, section, seq, arrived[m], incoming[m], kept[m]
            )
            kept[m], (keep, send) = outs[:2], outs[2:4]
            if len(outs) > 4:
                incoming[m] = outs[4]
            if stage == n_pipe - 1:
                incoming_far[m] = swap(incoming[m], "dp", 2)
            sent.append((keep, swap(send, "tensor", 1)))
        for m in range(micros):
            old = [] if stage == 0 else [passed[m], sums[m]]
            keep, landed = sent[m]
            if m > 0:
                landed = after(landed, passed[m - 1])
            passed[m], sums[m] = input_gradient(
                place, keep, landed, own_rows[m], x_own, m, section, gain, old
            )
    input_grads = jnp.stack(passed)[None, :, None]

    attended = with_sibling([saved[1], saved_far[1]])
    normed_all = with_sibling([normed_turned, saved_far[3]])
    incoming_far[0], attended[2], attended[3], normed_all[2], normed_all[3] = (
        lax.optimization_barrier((incoming_far[0], *attended[2:], *normed_all[2:], *passed))[
            : -len(passed)
        ]
    )
    projs_far, scaled_far = [], []
    for m in range(micros):
        arrived = incoming_far[m] if m == 0 else after(incoming_far[m], projs_far[-1])
        outs = backward_far(scale, saved_far[:3], weights[0], seq, arrived, m)
        projs_far.append(outs[0])
        scaled_far.append(outs[1])
    state = [master, moment_one, moment_two]
    scaled_all = with_sibling([*[value[1] for value in kept], *scaled_far])
    projs = with_sibling([*[value[0] for value in kept], *projs_far])
    projs[-1], scaled_all[-1] = lax.optimization_barrier((projs[-1], scaled_all[-1]))
    scale_cols = lax.dynamic_slice_in_dim(scale, data_rank * depth, depth, 1)
    *new_state, scale_part = update(
        place, scaled_all, attended, 0, state, None, 3 * head_cols, head_cols, scale_cols
    )
    vectors = jnp.concatenate(
        [
            lax.dynamic_update_slice_in_dim(
                jnp.zeros((1, channels), f32), scale_part, data_rank * depth, 1
            ),
            sum(sums),
        ]
    )
    shares = [vectors]
    for d in range(4):
        for t in range(2):
            if d or t:
                pairs = [(2 * i + u, 2 * (i ^ d) + (u ^ t)) for i in range(4) for u in range(2)]
                shares.append(lax.ppermute(vectors, ("dp", "tensor"), pairs))
    new_state = update(place, normed_all, projs, 0, state, new_state, 0, 3 * head_cols)
    shares = lax.optimization_barrier((*shares, new_state[0]))[:-1]
    vectors = sum(shares)
    return (input_grads, *new_state, vectors[None])


def from_behind(block, axis, distance):
    devices = range(lax.axis_size(axis))
    route = [(i - distance, i) for i in devices if i - distance in devices]
    return lax.ppermute(block, axis, route)


def normalize_rows(values_in):
    inverse = lax.rsqrt(jnp.mean(values_in * values_in, axis=-1, keepdims=True) + norm_eps)
    return (inverse, values_in * inverse)


def select_micro(array, micro_index):
    return lax.dynamic_index_in_dim(array, micro_index, 0, keepdims=False)


def store_slot(buffer, value, slot_index):
    return lax.dynamic_update_index_in_dim(buffer, value, slot_index, 0)


def local_any(x_in, out_grad, layer_scale, norm_gain, master, moment_one, moment_two):
    n_pipe = lax.axis_size("pipe")
    n_tensor = lax.axis_size("tensor")
    pipe_rank = lax.axis_index("pipe")
    micro_count = x_in.shape[1]
    images = x_in.shape[2]
    shard_len = x_in.shape[3]
    channels = x_in.shape[4]
    seq_len = shard_len * n_tensor
    row_start = lax.axis_index("tensor") * shard_len
    head_cols = master.shape[2] // 4
    local_heads = head_cols // HD
    score_root = math.sqrt(HD)
    scale_vec = layer_scale[0]
    gain_vec = norm_gain[0]
    weights = lax.all_gather(master[0].astype(jnp.bfloat16), "dp", axis=0, tiled=True)
    w_qkv = weights[:, : 3 * head_cols]
    w_out = weights[:, 3 * head_cols :]
    full_x = lax.all_gather(x_in[0], "tensor", axis=2, tiled=True).astype(jnp.float32)
    full_inverse, full_unit = normalize_rows(full_x)
    normed = (full_unit * gain_vec).astype(jnp.bfloat16)
    local_unit = lax.dynamic_slice_in_dim(full_unit, row_start, shard_len, 2)
    projected = jnp.einsum(
        "mbsd,dc->mbsc", normed, w_qkv, preferred_element_type=jnp.float32
    ).astype(jnp.bfloat16)
    projected = projected.reshape(micro_count, images, seq_len, 3, local_heads, HD)
    query = projected[:, :, :, 0]
    keys = projected[:, :, :, 1]
    values = projected[:, :, :, 2]
    scores = (
        jnp.einsum("mbqhe,mbkhe->mbhqk", query, keys, preferred_element_type=jnp.float32)
        / score_root
    )
    probs = jax.nn.softmax(scores, axis=-1)
    probs_low = probs.astype(jnp.bfloat16)
    attended = jnp.einsum(
        "mbhqk,mbkhe->mbqhe", probs_low, values, preferred_element_type=jnp.float32
    ).astype(jnp.bfloat16)
    attended_flat = attended.reshape(micro_count, images, seq_len, head_cols)

    def backward_segment(micro_index, incoming):
        query_now = select_micro(query, micro_index)
        keys_now = select_micro(keys, micro_index)
        values_now = select_micro(values, micro_index)
        probs_now = select_micro(probs, micro_index)
        probs_low_now = select_micro(probs_low, micro_index)
        attended_now = select_micro(attended, micro_index)
        scaled = (scale_vec * incoming.astype(jnp.float32)).astype(jnp.bfloat16)
        d_att = jnp.einsum("bsd,dc->bsc", scaled, w_out, preferred_element_type=jnp.float32).astype(
            jnp.bfloat16
        )
        d_att = d_att.reshape(images, seq_len, local_heads, HD)
        d_prob = jnp.einsum(
            "bqhe,bkhe->bhqk", d_att, values_now, preferred_element_type=jnp.float32
        )
        row_delta = jnp.einsum(
            "bqhe,bqhe->bhq", d_att, attended_now, preferred_element_type=jnp.float32
        )
        d_score = (probs_now * (d_prob - row_delta[..., None]) / score_root).astype(jnp.bfloat16)
        d_query = jnp.einsum(
            "bhqk,bkhe->bqhe", d_score, keys_now, preferred_element_type=jnp.float32
        ).astype(jnp.bfloat16)
        d_keys = jnp.einsum(
            "bhqk,bqhe->bkhe", d_score, query_now, preferred_element_type=jnp.float32
        ).astype(jnp.bfloat16)
        d_values = jnp.einsum(
            "bhqk,bqhe->bkhe", probs_low_now, d_att, preferred_element_type=jnp.float32
        ).astype(jnp.bfloat16)
        d_proj = jnp.concatenate([d_query, d_keys, d_values], axis=2).reshape(
            images, seq_len, 3 * head_cols
        )
        partial_sum = jnp.einsum("bsc,dc->bsd", d_proj, w_qkv, preferred_element_type=jnp.float32)
        return (partial_sum, d_proj, scaled)

    def spare_segment(micro_index, incoming):
        return (
            jnp.zeros((images, seq_len, channels), jnp.float32),
            jnp.zeros((images, seq_len, 3 * head_cols), jnp.bfloat16),
            jnp.zeros((images, seq_len, channels), jnp.bfloat16),
        )

    segments = n_pipe + micro_count - 1
    is_last = pipe_rank == n_pipe - 1
    received = jnp.zeros((images, seq_len, channels), jnp.bfloat16)
    slots = micro_count + 1
    grads_out = jnp.zeros((slots, images, shard_len, channels), jnp.bfloat16)
    proj_saved = jnp.zeros((slots, images, seq_len, 3 * head_cols), jnp.bfloat16)
    scaled_saved = jnp.zeros((slots, images, seq_len, channels), jnp.bfloat16)
    grad_saved = jnp.zeros((slots, images, seq_len, channels), jnp.bfloat16)
    gain_part = jnp.zeros((channels,), jnp.float32)
    for segment_step in range(segments):
        micro_index = segment_step - (n_pipe - 1) + pipe_rank
        active = jnp.logical_and(micro_index >= 0, micro_index < micro_count)
        micro_index = jnp.clip(micro_index, 0, micro_count - 1)
        slot_index = jnp.where(active, micro_index, micro_count)
        arrived = received
        incoming = jnp.where(is_last, select_micro(out_grad, micro_index), arrived)
        partial_sum, d_proj, scaled = lax.cond(
            active, backward_segment, spare_segment, micro_index, incoming
        )
        pieces = partial_sum.astype(jnp.bfloat16).reshape(images, n_tensor, shard_len, channels)
        landed = lax.all_to_all(pieces, "tensor", split_axis=1, concat_axis=1, tiled=True)
        own_d = jnp.sum(landed.astype(jnp.float32), axis=1)
        d_normed = lax.all_gather(own_d.astype(jnp.bfloat16), "tensor", axis=1, tiled=True).astype(
            own_d.dtype
        )
        own_unit = select_micro(local_unit, micro_index)
        sel_unit = select_micro(full_unit, micro_index)
        sel_inverse = select_micro(full_inverse, micro_index)
        d_unit = d_normed * gain_vec
        d_input = sel_inverse * (
            d_unit - sel_unit * jnp.mean(d_unit * sel_unit, axis=-1, keepdims=True)
        )
        passed = (incoming.astype(jnp.float32) + d_input).astype(jnp.bfloat16)
        own_passed = lax.dynamic_slice_in_dim(passed, row_start, shard_len, 1)
        gain_part = gain_part + jnp.where(active, jnp.sum(own_d * own_unit, axis=(0, 1)), 0.0)
        grads_out = store_slot(grads_out, own_passed, slot_index)
        proj_saved = store_slot(proj_saved, d_proj, slot_index)
        scaled_saved = store_slot(scaled_saved, scaled, slot_index)
        grad_saved = store_slot(grad_saved, incoming, slot_index)
        if segment_step + 1 < segments:
            received = from_behind(passed, "pipe", -1)
    grads_kept = grads_out[:micro_count]
    proj_kept = proj_saved[:micro_count]
    scaled_kept = scaled_saved[:micro_count]
    grad_kept = grad_saved[:micro_count]
    grad_qkv = jnp.einsum("mbsd,mbsc->dc", normed, proj_kept, preferred_element_type=jnp.float32)
    grad_out = jnp.einsum(
        "mbsd,mbsc->dc", scaled_kept, attended_flat, preferred_element_type=jnp.float32
    )
    weight_grad = lax.psum_scatter(
        jnp.concatenate([grad_qkv, grad_out], axis=1).astype(jnp.bfloat16),
        "dp",
        scatter_dimension=0,
        tiled=True,
    ).astype(jnp.float32)
    summed_out = jnp.einsum(
        "mbsd,mbsc->dc", grad_kept, attended_flat, preferred_element_type=jnp.float32
    )
    scale_part = jnp.sum(w_out.astype(jnp.float32) * summed_out, axis=1)
    scale_grad, gain_grad = lax.psum((scale_part, gain_part), ("dp", "tensor"))
    bias_one = 1.0 - beta_one**adam_step
    bias_two = 1.0 - beta_two**adam_step
    first_new = beta_one * moment_one[0] + (1.0 - beta_one) * weight_grad
    second_new = beta_two * moment_two[0] + (1.0 - beta_two) * weight_grad * weight_grad
    update = first_new / bias_one / (jnp.sqrt(second_new / bias_two) + adam_eps)
    master_new = master[0] - learn_rate * (update + weight_decay * master[0])
    scale_both = jnp.stack([scale_grad, gain_grad])
    return (grads_kept[None], master_new[None], first_new[None], second_new[None], scale_both[None])


def solution(mesh):
    placed = (
        P("pipe", None, "dp", "tensor", None),
        P(None, "dp", None, None),
        P("pipe", None),
        P("pipe", None),
        P("pipe", "dp", "tensor"),
        P("pipe", "dp", "tensor"),
        P("pipe", "dp", "tensor"),
    )
    two_by_two = mesh.shape["dp"] == 4 and mesh.shape["tensor"] == 2
    return jax.shard_map(
        local_two_by_two if two_by_two else local_any,
        mesh=mesh,
        in_specs=placed,
        out_specs=(
            P("pipe", None, "dp", "tensor", None),
            P("pipe", "dp", "tensor"),
            P("pipe", "dp", "tensor"),
            P("pipe", "dp", "tensor"),
            P("pipe", None, None),
        ),
        check_vma=False,
    )
```

```python
import functools
import math

import jax
import jax.numpy as jnp
from jax import lax
from jax.experimental import pallas as pl
from jax.experimental.pallas import tpu as pltpu
from jax.sharding import PartitionSpec as P

HD = 128

beta_one = 0.9
beta_two = 0.95
adam_eps = 1e-08
learn_rate = 0.001
weight_decay = 0.05
adam_step = 100.0
norm_eps = 1e-06
VMEM_LIMIT = 64 * 1024 * 1024

VMEM = "vmem"
SMEM = pl.BlockSpec(memory_space=pltpu.SMEM)
ANY = pl.BlockSpec(memory_space=pl.ANY)
bf16 = jnp.bfloat16
f32 = jnp.float32


def dot(a, b, dims=((1,), (0,))):
    return lax.dot_general(a, b, (dims, ((), ())), preferred_element_type=jnp.float32)


def shape_of(shape, dtype):
    return jax.ShapeDtypeStruct(shape, dtype)


def round_up(value, unit):
    return (value + unit - 1) // unit * unit


def call(kernel, args, specs, outs, out_specs, scratch=(), aliases=None, moved=0):
    def spec_of(spec, value):
        if spec != VMEM:
            return spec
        return pl.BlockSpec(value.shape, lambda i: (0,) * len(value.shape))

    return pl.pallas_call(
        kernel,
        grid=(1,),
        out_shape=outs,
        in_specs=[spec_of(spec, value) for spec, value in zip(specs, args)],
        out_specs=[spec_of(spec, value) for spec, value in zip(out_specs, outs)],
        scratch_shapes=list(scratch),
        input_output_aliases=aliases or {},
        compiler_params=pltpu.CompilerParams(vmem_limit_bytes=VMEM_LIMIT),
        cost_estimate=pl.CostEstimate(flops=0, bytes_accessed=moved, transcendentals=0),
    )(*args)


def start_all(copies):
    for copy in copies:
        copy.start()


def wait_all(copies):
    for copy in copies:
        copy.wait()


def pick(ref, micro):
    return ref[micro] if len(ref.shape) == 3 else ref[...]


def rows_at(start, size):
    return pl.ds(pl.multiple_of(start, 16), size)


def normalize_kernel(
    place_ref, mine_ref, other_ref, gain_ref, _, normed_ref, sent_ref, turned_ref
):
    micros, shard, channels = mine_ref.shape
    rank = place_ref[5]
    normed_ref[...] = jnp.zeros_like(normed_ref)
    for m in range(micros):
        for source, at in ((mine_ref, rank), (other_ref, 1 - rank)):
            values = source[m].astype(f32)
            inverse = lax.rsqrt(jnp.mean(values * values, axis=-1, keepdims=True) + norm_eps)
            normed = (values * inverse * gain_ref[...]).astype(bf16)
            normed_ref[rows_at(m * 2 * shard + at * shard, shard), :channels] = normed
    sent_ref[...] = normed_ref[...]
    turned_ref[...] = normed_ref[...].T


def normalize(place, mine, other, gain, early):
    micros, shard, channels = mine.shape
    rows, padded = micros * shard * 2, round_up(channels, 128)
    return call(
        normalize_kernel,
        [place, mine, other, gain, early],
        [SMEM, VMEM, VMEM, VMEM, ANY],
        [shape_of((rows, padded), bf16)] * 2 + [shape_of((padded, rows), bf16)],
        [VMEM] * 3,
    )


def round_kernel(chunk, chunks, master_ref, low_ref, wide, sems):
    width = wide.shape[2]
    copies = [
        pltpu.make_async_copy(
            master_ref.at[0, :, pl.ds((n * chunks + chunk) * width, width)], wide.at[n], sems.at[n]
        )
        for n in range(4)
    ]
    start_all(copies)
    for n in range(4):
        copies[n].wait()
        low_ref[:, n * width : (n + 1) * width] = wide[n].astype(bf16)


def rounded_chunk(master, chunk, chunks):
    _, depth, cols = master.shape
    width = cols // 4 // chunks
    return call(
        functools.partial(round_kernel, chunk, chunks),
        [master],
        [ANY],
        [shape_of((depth, 4 * width), bf16)],
        [VMEM],
        [pltpu.VMEM((4, depth, width), f32), pltpu.SemaphoreType.DMA((4,))],
    )[0]


def attend(projected, att_ref, probs_ref, seq, width):
    root = math.sqrt(HD)
    heads = width // HD
    for m in range(projected.shape[0] // seq):
        span = slice(m * seq, (m + 1) * seq)
        for h in range(heads):
            query, keys, values = [
                projected[span, n * width + h * HD : n * width + (h + 1) * HD] for n in range(3)
            ]
            scores = dot(query, keys, ((1,), (1,))) * (1.0 / root)
            scores = jnp.exp(scores - jnp.max(scores, axis=-1, keepdims=True))
            probs = scores / jnp.sum(scores, axis=-1, keepdims=True)
            probs_ref[(m * heads + h) * seq : (m * heads + h + 1) * seq, :] = probs
            att_ref[span, h * HD : (h + 1) * HD] = dot(probs.astype(bf16), values).astype(bf16)


def forward_kernel(chunk, channels, seq, place_ref, normed_ref, *refs):
    pieces = refs[:4]
    *refs, normed, buffer, turned, acts, att, probs, sems, out_sems = refs
    targets = [ref.at[chunk] for ref in refs[-5:]]
    depth = pieces[0].shape[0]
    width = pieces[0].shape[1] // 4
    targets[1] = refs[-4].at[:, pl.ds(chunk * width, width)]
    copies = [
        pltpu.make_async_copy(piece, buffer.at[rows_at(place_ref[at], depth), :], sems.at[at])
        for at, piece in enumerate(pieces)
    ]
    copies.append(pltpu.make_async_copy(normed_ref, normed, sems.at[4]))
    start_all(copies)
    buffer[channels:, :] = jnp.zeros((buffer.shape[0] - channels, buffer.shape[1]), bf16)
    wait_all(copies)
    w_out = buffer.at[pl.ds(0, channels), pl.ds(3 * width, width)]
    written = [
        pltpu.make_async_copy(source, target, out_sems.at[n])
        for n, (source, target) in enumerate(zip((acts, att, probs, w_out, turned), targets))
    ]
    written[3].start()
    turned[...] = buffer[:, : 3 * width].T
    written[4].start()
    projected = dot(normed[...], buffer[:, : 3 * width]).astype(bf16)
    acts[...] = projected
    written[0].start()
    attend(projected, att, probs, seq, width)
    written[1].start()
    written[2].start()
    wait_all(written)


def saved_shapes(rows, width, chunks, seq):
    return [
        shape_of((chunks, rows, 3 * width), bf16),
        shape_of((rows, width * chunks), bf16),
        shape_of((chunks, rows * width // HD, seq), f32),
    ]


def forward(place, normed, pieces, chunk, chunks, channels, seq, earlier):
    rows, padded = normed.shape
    cols = pieces[0].shape[1]
    width = cols // 4
    outs = saved_shapes(rows, width, chunks, seq) + [
        shape_of((chunks, channels, width), bf16),
        shape_of((chunks, 3 * width, padded), bf16),
    ]
    args = [place, normed, *pieces]
    aliases = {}
    if earlier is not None:
        aliases = {len(args) + n: n for n in range(5)}
        args += list(earlier)
    return call(
        functools.partial(forward_kernel, chunk, channels, seq),
        args,
        [SMEM] + [ANY] * (len(args) - 1),
        outs,
        [ANY] * 5,
        [
            pltpu.VMEM((rows, padded), bf16),
            pltpu.VMEM((padded, cols), bf16),
            pltpu.VMEM((3 * width, padded), bf16),
            pltpu.VMEM((rows, 3 * width), bf16),
            pltpu.VMEM((rows, width), bf16),
            pltpu.VMEM((rows * width // HD, seq), f32),
            pltpu.SemaphoreType.DMA((5,)),
            pltpu.SemaphoreType.DMA((5,)),
        ],
        aliases,
    )


def forward_far_kernel(first, count, seq, normed_ref, turned_ref, *refs):
    *refs, normed, normed_turned, turned, acts, atts, probs, sems, out_sems = refs
    acts_ref, att_ref, probs_ref, turned_rows_ref = refs[-4:]
    copies = [pltpu.make_async_copy(normed_ref, normed, sems.at[count])]
    copies += [
        pltpu.make_async_copy(turned_ref.at[first + c], turned.at[c], sems.at[c])
        for c in range(count)
    ]
    start_all(copies)
    copies[0].wait()
    width = turned.shape[1] // 3
    written = []
    if first == 0:
        normed_turned[...] = normed[...].T
        written.append(
            pltpu.make_async_copy(normed_turned, turned_rows_ref, out_sems.at[0, 3])
        )
        written[-1].start()
    for c in range(count):
        copies[1 + c].wait()
        projected = dot(normed[...], turned[c], ((1,), (1,))).astype(bf16)
        acts[c] = projected
        attend(projected, atts.at[c], probs.at[c], seq, width)
        targets = (
            acts_ref.at[first + c],
            att_ref.at[:, pl.ds((first + c) * width, width)],
            probs_ref.at[first + c],
        )
        for n, source in enumerate((acts, atts, probs)):
            written.append(pltpu.make_async_copy(source.at[c], targets[n], out_sems.at[c, n]))
            written[-1].start()
    wait_all(written)


def forward_far(normed, turned, first, count, seq, earlier):
    rows, padded = normed.shape
    chunks, triple, _ = turned.shape
    width = triple // 3
    args = [normed, turned]
    aliases = {}
    if earlier is not None:
        aliases = {len(args) + n: n for n in range(4)}
        args += list(earlier)
    return call(
        functools.partial(forward_far_kernel, first, count, seq),
        args,
        [ANY] * len(args),
        [*saved_shapes(rows, width, chunks, seq), shape_of((padded, rows), bf16)],
        [ANY] * 4,
        [
            pltpu.VMEM((rows, padded), bf16),
            pltpu.VMEM((padded, rows), bf16),
            pltpu.VMEM((count, triple, padded), bf16),
            pltpu.VMEM((count, rows, triple), bf16),
            pltpu.VMEM((count, rows, width), bf16),
            pltpu.VMEM((count, rows * width // HD, seq), f32),
            pltpu.SemaphoreType.DMA((count + 1,)),
            pltpu.SemaphoreType.DMA((count, 4)),
        ],
        aliases,
    )


def loads_of(sources, buffers, sems, first, rows):
    acts, att, probs, w_out, *turned = sources
    chunks = acts.shape[0]
    heads = att.shape[1] // chunks // HD
    views = [
        (acts.at[:, pl.ds(first, rows), :], buffers[0]),
        (att.at[pl.ds(first, rows), :], buffers[1]),
        (probs.at[:, pl.ds(first * heads, rows * heads), :], buffers[2]),
        (w_out, buffers[3]),
    ]
    views += [(weight.at[c], buffers[4].at[c]) for weight in turned for c in range(chunks)]
    copies = [
        pltpu.make_async_copy(source, target, sems.at[n])
        for n, (source, target) in enumerate(views)
    ]
    return copies[:4], copies[4:]


def buffers_of(sources, rows):
    acts, att, probs, *weights = sources
    chunks, all_rows, triple = acts.shape
    buffers = [
        pltpu.VMEM((chunks, rows, triple), bf16),
        pltpu.VMEM((rows, att.shape[1]), bf16),
        pltpu.VMEM((chunks, probs.shape[1] * rows // all_rows, probs.shape[2]), f32),
    ]
    buffers += [pltpu.VMEM(weight.shape, bf16) for weight in weights]
    return [*buffers, pltpu.SemaphoreType.DMA((4 + chunks,))]


def head_gradients(scaled, seq, buffers, proj):
    root = math.sqrt(HD)
    acts, att, probs, w_outs = buffers[:4]
    chunks, _, triple = acts.shape
    width = triple // 3
    heads = width // HD
    head_cols = chunks * width
    d_atts = [dot(scaled, w_outs[c]).astype(bf16) for c in range(chunks)]
    for c in range(chunks):
        for m in range(scaled.shape[0] // seq):
            span = slice(m * seq, (m + 1) * seq)
            for h in range(heads):
                query, keys, values = [
                    acts[c, span, n * width + h * HD : n * width + (h + 1) * HD] for n in range(3)
                ]
                begin = c * width + h * HD
                attended = att[span, begin : begin + HD].astype(f32)
                at = (m * heads + h) * seq
                prob = probs[c, at : at + seq, :]
                d_head = d_atts[c][span, h * HD : (h + 1) * HD]
                d_prob = dot(d_head, values, ((1,), (1,)))
                delta = jnp.sum(d_head.astype(f32) * attended, axis=-1, keepdims=True)
                d_score = (prob * (d_prob - delta) * (1.0 / root)).astype(bf16)
                grads = (
                    dot(d_score, keys),
                    dot(d_score, query, ((0,), (0,))),
                    dot(prob.astype(bf16), d_head, ((0,), (0,))),
                )
                for n, value in enumerate(grads):
                    place = n * head_cols + begin
                    proj[span, place : place + HD] = value.astype(bf16)


def micro_of(ref, micro):
    return ref.at[micro] if len(ref.shape) == 3 else ref


def scaled_turned(scaled, padded):
    rows, channels = scaled.shape
    return jnp.concatenate([scaled, jnp.zeros((rows, padded - channels), bf16)], axis=1).T


def backward_kernel(chunks, micro, section, halves, seq, place_ref, scale_ref, *refs):
    sources, refs = refs[:5], refs[5:]
    *buffers, sems, total, proj, merged, turned_in, keep, send, own_sems = refs[-13:]
    refs = refs[:-13]
    rank = place_ref[5]
    active = place_ref[4] == section
    shard, channels = keep.shape
    if halves:
        mine_ref, other_ref, before_ref, *refs = refs
        proj_ref, turned_ref, keep_ref, send_ref, merged_ref = refs[-5:]

        @pl.when(jnp.logical_not(active))
        def _():
            hand_on(micro_of(before_ref, micro), merged, merged_ref, own_sems.at[0])

    else:
        incoming_ref, *refs = refs
        proj_ref, turned_ref, keep_ref, send_ref = refs[-4:]

    @pl.when(active)
    def _():
        if halves:
            arrive = [
                pltpu.make_async_copy(
                    ref, merged.at[rows_at(at * shard, shard), :], own_sems.at[n]
                )
                for n, (ref, at) in enumerate(((mine_ref, rank), (other_ref, 1 - rank)))
            ]
        else:
            arrive = [pltpu.make_async_copy(micro_of(incoming_ref, micro), merged, own_sems.at[0])]
        start_all(arrive)
        early, late = loads_of(sources, buffers, sems, micro * seq, seq)
        start_all(early)
        late[0].start()
        wait_all(arrive)
        outs = []

        def write(source, target):
            outs.append(pltpu.make_async_copy(source, target, own_sems.at[2 + len(outs)]))
            outs[-1].start()

        if halves:
            write(merged, merged_ref)
        scaled = (scale_ref[...] * merged[...].astype(f32)).astype(bf16)
        turned_in[...] = scaled_turned(scaled, turned_in.shape[0])
        write(turned_in, turned_ref)
        wait_all(early)
        start_all(late[1:])
        head_gradients(scaled, seq, buffers, proj)
        turned = buffers[4]
        width = turned.shape[1] // 3
        for c in range(chunks):
            late[c].wait()
            begin = [(n * chunks + c) * width for n in range(3)]
            grads = jnp.concatenate([proj[:, at : at + width] for at in begin], axis=1)
            part = dot(grads, turned[c])
            if c == 0:
                total[...] = part
            else:
                total[...] += part
        write(proj, proj_ref)
        send[...] = total[rows_at((1 - rank) * shard, shard), :channels].astype(bf16)
        write(send, send_ref)
        keep[...] = total[rows_at(rank * shard, shard), :channels].astype(bf16)
        write(keep, keep_ref)
        wait_all(outs)


def backward(place, scale, saved, weights, micro, section, seq, incoming, before, old):
    chunks, channels, width = weights[0].shape
    padded = weights[1].shape[2]
    halves = isinstance(incoming, tuple)
    args = [place, scale, *saved, *weights]
    args += [*incoming, before] if halves else [incoming]
    aliases = {}
    if old is not None:
        aliases = {len(args) + n: n for n in range(2)}
        args += list(old)
    outs = [
        shape_of((seq, 3 * width * chunks), bf16),
        shape_of((padded, seq), bf16),
        shape_of((seq // 2, channels), bf16),
        shape_of((seq // 2, channels), bf16),
    ]
    if halves:
        outs.append(shape_of((seq, channels), bf16))
    return call(
        functools.partial(backward_kernel, chunks, micro, section, halves, seq),
        args,
        [SMEM, VMEM] + [ANY] * (len(args) - 2),
        outs,
        [ANY] * len(outs),
        buffers_of([*saved, *weights], seq)
        + [
            pltpu.VMEM((seq, padded), f32),
            pltpu.VMEM((seq, 3 * width * chunks), bf16),
            pltpu.VMEM((seq, channels), bf16),
            pltpu.VMEM((padded, seq), bf16),
            pltpu.VMEM((seq // 2, channels), bf16),
            pltpu.VMEM((seq // 2, channels), bf16),
            pltpu.SemaphoreType.DMA((7,)),
        ],
        aliases,
    )


def backward_far_kernel(micro, seq, scale_ref, *refs):
    sources = refs[:4]
    *refs, acts, atts, probs, w_outs, sems = refs[4:]
    buffers = (acts, atts, probs, w_outs)
    incoming_ref, proj_ref, turned_ref = refs
    loads, _ = loads_of(sources, buffers, sems, micro * seq, seq)
    start_all(loads)
    scaled = (scale_ref[...] * incoming_ref[...].astype(f32)).astype(bf16)
    turned_ref[...] = scaled_turned(scaled, turned_ref.shape[0])
    wait_all(loads)
    head_gradients(scaled, seq, buffers, proj_ref)


def backward_far(scale, saved, w_outs, seq, incoming, micro):
    chunks, channels, width = w_outs.shape
    return call(
        functools.partial(backward_far_kernel, micro, seq),
        [scale, *saved, w_outs, incoming],
        [VMEM] + [ANY] * 4 + [VMEM],
        [
            shape_of((seq, 3 * width * chunks), bf16),
            shape_of((round_up(channels, 128), seq), bf16),
        ],
        [VMEM] * 2,
        buffers_of([*saved, w_outs], seq),
    )


def hand_on(source, through, target, sem):
    for copy in (
        pltpu.make_async_copy(source, through, sem),
        pltpu.make_async_copy(through, target, sem),
    ):
        copy.start()
        copy.wait()


def input_kernel(micro, section, place_ref, gain_ref, keep_ref, landed_ref, grad_ref, x_ref, *refs):
    new_ref, sum_ref, keep, landed, grad, own, new, total, sems = refs[-9:]
    shard = keep.shape[0]

    @pl.when(place_ref[4] == section)
    def _():
        if len(grad_ref.shape) == 2:
            grad_from = grad_ref
        else:
            grad_from = grad_ref.at[micro, rows_at(place_ref[5] * shard, shard), :]
        loads = [
            pltpu.make_async_copy(source, target, sems.at[n])
            for n, (source, target) in enumerate(
                ((x_ref.at[micro], own), (keep_ref, keep), (landed_ref, landed), (grad_from, grad))
            )
        ]
        start_all(loads)
        loads[0].wait()
        wide = own[...].astype(f32)
        inverse = lax.rsqrt(jnp.mean(wide * wide, axis=-1, keepdims=True) + norm_eps)
        unit = wide * inverse
        wait_all(loads[1:])
        d_normed = keep[...].astype(f32) + landed[...].astype(f32)
        d_unit = d_normed * gain_ref[...]
        d_input = inverse * (d_unit - unit * jnp.mean(d_unit * unit, axis=-1, keepdims=True))
        new[...] = (grad[...].astype(f32) + d_input).astype(bf16)
        out = pltpu.make_async_copy(new, new_ref, sems.at[4])
        out.start()
        total[...] = jnp.sum(d_normed * unit, axis=0, keepdims=True)
        out_sum = pltpu.make_async_copy(total, sum_ref, sems.at[5])
        out_sum.start()
        out.wait()
        out_sum.wait()


def input_gradient(place, keep, landed, grad, x_own, micro, section, gain, old):
    shard, channels = keep.shape
    args = [place, gain, keep, landed, grad, x_own, *old]
    return call(
        functools.partial(input_kernel, micro, section),
        args,
        [SMEM, VMEM] + [ANY] * (len(args) - 2),
        [shape_of((shard, channels), bf16), shape_of((1, channels), f32)],
        [ANY, ANY],
        [
            *[pltpu.VMEM((shard, channels), bf16)] * 5,
            pltpu.VMEM((1, channels), f32),
            pltpu.SemaphoreType.DMA((6,)),
        ],
        {6 + n: n for n in range(len(old))},
    )


def adam(grad, master, first, second):
    bias_one = 1.0 - beta_one**adam_step
    bias_two = 1.0 - beta_two**adam_step
    first_new = beta_one * first + (1.0 - beta_one) * grad
    second_new = beta_two * second + (1.0 - beta_two) * grad * grad
    corrected = second_new * (1.0 / bias_two)
    root = corrected * lax.rsqrt(corrected)
    update = first_new * (learn_rate / bias_one) / (root + adam_eps)
    return master * (1.0 - learn_rate * weight_decay) - update, first_new, second_new


AHEAD = 3


def update_kernel(lefts, parts, first, right_col, first_col, blocks, place_ref, *refs):
    turned, refs = refs[:lefts], refs[lefts:]
    rights, refs = refs[:parts], refs[parts:]
    state, refs = refs[:3], refs[3:]
    if first:
        scale, refs = refs[0], refs[1:]
    else:
        refs = refs[3:]
    new_state, refs = refs[:3], refs[3:]
    if first:
        shares, refs = refs[0], refs[1:]
    left, right, held, left_sems, right_sems, in_sems, out_sems = refs
    depth = left.shape[0]
    width = right.shape[2]

    left_copies, begin = [], 0
    for at, value in enumerate(turned):
        rows = value.shape[1]
        left_copies.append(
            pltpu.make_async_copy(
                value.at[rows_at(place_ref[0], depth), :],
                left.at[:, pl.ds(begin, rows)],
                left_sems.at[at],
            )
        )
        begin += rows

    def loads(block):
        copies, begin = [], 0
        for at, value in enumerate(rights):
            rows = value.shape[0]
            copies.append(
                pltpu.make_async_copy(
                    value.at[:, pl.ds(right_col + block * width, width)],
                    right.at[block, pl.ds(begin, rows), :],
                    right_sems.at[block, at],
                )
            )
            begin += rows
        for at, value in enumerate(state):
            copies.append(
                pltpu.make_async_copy(
                    value.at[0, :, pl.ds(first_col + block * width, width)],
                    held.at[block, at],
                    in_sems.at[block, at],
                )
            )
        return copies

    pending = [loads(block) for block in range(blocks)]
    start_all(left_copies)
    for block in range(min(AHEAD, blocks)):
        start_all(pending[block])
    wait_all(left_copies)
    written = []
    for block in range(blocks):
        wait_all(pending[block])
        if block + AHEAD < blocks:
            start_all(pending[block + AHEAD])
        grad = dot(left[...], right[block])
        master = held[block, 0]
        values = adam(grad, master, held[block, 1], held[block, 2])
        if first:
            low = master.astype(bf16).astype(f32)
            part = jnp.sum(low * grad, axis=1, keepdims=True)
            sums = part if block == 0 else sums + part
            if block == blocks - 1:
                turned_sums = jnp.broadcast_to(sums, (depth, 128)).T
                shares[...] = turned_sums[:1, :] / scale[...]
        for at, value in enumerate(values):
            held[block, at] = value
            written.append(
                pltpu.make_async_copy(
                    held.at[block, at],
                    new_state[at].at[0, :, pl.ds(first_col + block * width, width)],
                    out_sems.at[block, at],
                )
            )
            written[-1].start()
    wait_all(written)


def update(place, turned, rights, right_col, state, earlier, first_col, cols, scale=None, block=512):
    _, depth, _ = state[0].shape
    tokens = sum(value.shape[1] for value in turned)
    first = earlier is None
    blocks = cols // block
    args = [place, *turned, *rights, *state]
    outs = [shape_of(state[0].shape, f32)] * 3
    out_specs = [ANY] * 3
    aliases = {}
    if first:
        outs.append(shape_of((1, depth), f32))
        out_specs.append(VMEM)
        args.append(scale)
    else:
        aliases = {len(args) + i: i for i in range(3)}
        args += list(earlier)
    return call(
        functools.partial(
            update_kernel, len(turned), len(rights), first, right_col, first_col, blocks
        ),
        args,
        [SMEM] + [ANY] * (len(args) - 2) + [VMEM if first else ANY],
        outs,
        out_specs,
        [
            pltpu.VMEM((depth, tokens), bf16),
            pltpu.VMEM((blocks, tokens, block), bf16),
            pltpu.VMEM((blocks, 3, depth, block), f32),
            pltpu.SemaphoreType.DMA((len(turned),)),
            pltpu.SemaphoreType.DMA((blocks, len(rights))),
            pltpu.SemaphoreType.DMA((blocks, 3)),
            pltpu.SemaphoreType.DMA((blocks, 3)),
        ],
        aliases,
        moved=24 * depth * cols,
    )


def swap(value, axis, mask):
    return lax.ppermute(value, axis, [(i, i ^ mask) for i in range(lax.axis_size(axis))])


def after(value, *others):
    return lax.optimization_barrier((value, *others))[0]


def local_two_by_two(x_in, out_grad, layer_scale, norm_gain, master, moment_one, moment_two):
    n_pipe = lax.axis_size("pipe")
    pipe_rank = lax.axis_index("pipe")
    data_rank = lax.axis_index("dp")
    rank = lax.axis_index("tensor")
    micros, _, shard, channels = x_in.shape[1:]
    seq = shard * 2
    depth, all_cols = master.shape[1:]
    head_cols = all_cols // 4
    chunks = 4 if head_cols % (4 * HD) == 0 else 1
    width = head_cols // chunks
    gain, scale = norm_gain, layer_scale
    place = jnp.stack(
        [(data_rank ^ k) * depth for k in range(4)] + [pipe_rank, rank]
    ).astype(jnp.int32)

    x_own = x_in[0, :, 0]
    x_other = swap(x_own, "tensor", 1)

    own = [rounded_chunk(master, c, chunks) for c in range(chunks)]
    far = [swap(value, "dp", 2) for value in own]
    normed, normed_sent, normed_turned = normalize(place, x_own, x_other, gain, out_grad[:, 0])
    scale_cols = lax.dynamic_slice_in_dim(scale, data_rank * depth, depth, 1)
    if chunks > 1:
        normed, scale_cols, own[-1], *far[:-1] = lax.optimization_barrier(
            (normed, scale_cols, own[-1], *far[:-1])
        )
        far[-1] = swap(own[-1], "dp", 2)
    values = None
    for c in range(chunks):
        arrived = far[c] if c < chunks - 1 or not values else after(far[c], values[0])
        pieces = [own[c], swap(own[c], "dp", 1), arrived, swap(arrived, "dp", 1)]
        values = forward(place, normed, pieces, c, chunks, channels, seq, values)
    saved, weights = values[:3], values[3:]
    normed_far = swap(after(normed_sent, far[-1]), "dp", 2)

    def with_sibling(values):
        return [*values, *[swap(value, "dp", 1) for value in values]]

    kept = [None] * micros
    passed = [None] * micros
    sums = [None] * micros
    incoming = [out_grad[:, 0]] * micros
    incoming_far = [None] * micros
    straight = [(i + 1, i) for i in range(n_pipe - 1)]
    bounds = [min(chunks, 2 * n) for n in range(n_pipe)]
    saved_far = None
    for stage in range(n_pipe):
        section = n_pipe - 1 - stage
        own_rows = list(incoming)
        arrived = list(incoming)
        if stage > 0:
            own_rows = [lax.ppermute(passed[m], "pipe", straight) for m in range(micros)]
            part = bounds[stage] - bounds[stage - 1]
            if part:
                saved_far = forward_far(
                    after(normed_far, *passed), weights[1], bounds[stage - 1], part, seq, saved_far
                )
                own_rows = [after(mine, saved_far[0]) for mine in own_rows]
            arrived = [(mine, swap(mine, "tensor", 1)) for mine in own_rows]
        sent = []
        for m in range(micros):
            if sent:
                first = sent[0][0]
                if isinstance(arrived[m], tuple):
                    arrived[m] = (arrived[m][0], after(arrived[m][1], first))
                else:
                    arrived[m] = after(arrived[m], first)
            outs = backward(
                place, scale, saved, weights, m, section, seq, arrived[m], incoming[m], kept[m]
            )
            kept[m], (keep, send) = outs[:2], outs[2:4]
            if len(outs) > 4:
                incoming[m] = outs[4]
            if stage == n_pipe - 1:
                incoming_far[m] = swap(incoming[m], "dp", 2)
            sent.append((keep, swap(send, "tensor", 1)))
        for m in range(micros):
            old = [] if stage == 0 else [passed[m], sums[m]]
            keep, landed = sent[m]
            if m > 0:
                landed = after(landed, passed[m - 1])
            passed[m], sums[m] = input_gradient(
                place, keep, landed, own_rows[m], x_own, m, section, gain, old
            )
    input_grads = jnp.stack(passed)[None, :, None]

    attended = with_sibling([saved[1], saved_far[1]])
    normed_all = with_sibling([normed_turned, saved_far[3]])
    incoming_far[0], attended[2], attended[3], normed_all[2], normed_all[3], input_grads = (
        lax.optimization_barrier(
            (incoming_far[0], *attended[2:], *normed_all[2:], input_grads, *passed)
        )[
            : -len(passed)
        ]
    )
    projs_far, scaled_far = [], []
    for m in range(micros):
        arrived = incoming_far[m] if m == 0 else after(incoming_far[m], projs_far[-1])
        outs = backward_far(scale, saved_far[:3], weights[0], seq, arrived, m)
        projs_far.append(outs[0])
        scaled_far.append(outs[1])
    state = [master, moment_one, moment_two]
    scaled_all = with_sibling([*[value[1] for value in kept], *scaled_far])
    projs = with_sibling([*[value[0] for value in kept], *projs_far])
    projs[-1], scaled_all[-1] = lax.optimization_barrier((projs[-1], scaled_all[-1]))
    *new_state, scale_part = update(
        place, scaled_all, attended, 0, state, None, 3 * head_cols, head_cols, scale_cols
    )
    vectors = jnp.concatenate(
        [
            lax.dynamic_update_slice_in_dim(
                jnp.zeros((1, channels), f32), scale_part, data_rank * depth, 1
            ),
            *sums,
        ]
    )
    shares = [vectors]
    for d in range(4):
        for t in range(2):
            if d or t:
                pairs = [(2 * i + u, 2 * (i ^ d) + (u ^ t)) for i in range(4) for u in range(2)]
                shares.append(lax.ppermute(vectors, ("dp", "tensor"), pairs))
    new_state = update(place, normed_all, projs, 0, state, new_state, 0, 3 * head_cols)
    shares = lax.optimization_barrier((*shares, new_state[0]))[:-1]
    vectors = sum(shares)
    vectors = jnp.stack([vectors[0], sum(vectors[1 + m] for m in range(micros))])
    return (input_grads, *new_state, vectors[None])


def from_behind(block, axis, distance):
    devices = range(lax.axis_size(axis))
    route = [(i - distance, i) for i in devices if i - distance in devices]
    return lax.ppermute(block, axis, route)


def normalize_rows(values_in):
    inverse = lax.rsqrt(jnp.mean(values_in * values_in, axis=-1, keepdims=True) + norm_eps)
    return (inverse, values_in * inverse)


def select_micro(array, micro_index):
    return lax.dynamic_index_in_dim(array, micro_index, 0, keepdims=False)


def store_slot(buffer, value, slot_index):
    return lax.dynamic_update_index_in_dim(buffer, value, slot_index, 0)


def local_any(x_in, out_grad, layer_scale, norm_gain, master, moment_one, moment_two):
    n_pipe = lax.axis_size("pipe")
    n_tensor = lax.axis_size("tensor")
    pipe_rank = lax.axis_index("pipe")
    micro_count = x_in.shape[1]
    images = x_in.shape[2]
    shard_len = x_in.shape[3]
    channels = x_in.shape[4]
    seq_len = shard_len * n_tensor
    row_start = lax.axis_index("tensor") * shard_len
    head_cols = master.shape[2] // 4
    local_heads = head_cols // HD
    score_root = math.sqrt(HD)
    scale_vec = layer_scale[0]
    gain_vec = norm_gain[0]
    weights = lax.all_gather(master[0].astype(jnp.bfloat16), "dp", axis=0, tiled=True)
    w_qkv = weights[:, : 3 * head_cols]
    w_out = weights[:, 3 * head_cols :]
    full_x = lax.all_gather(x_in[0], "tensor", axis=2, tiled=True).astype(jnp.float32)
    full_inverse, full_unit = normalize_rows(full_x)
    normed = (full_unit * gain_vec).astype(jnp.bfloat16)
    local_unit = lax.dynamic_slice_in_dim(full_unit, row_start, shard_len, 2)
    projected = jnp.einsum(
        "mbsd,dc->mbsc", normed, w_qkv, preferred_element_type=jnp.float32
    ).astype(jnp.bfloat16)
    projected = projected.reshape(micro_count, images, seq_len, 3, local_heads, HD)
    query = projected[:, :, :, 0]
    keys = projected[:, :, :, 1]
    values = projected[:, :, :, 2]
    scores = (
        jnp.einsum("mbqhe,mbkhe->mbhqk", query, keys, preferred_element_type=jnp.float32)
        / score_root
    )
    probs = jax.nn.softmax(scores, axis=-1)
    probs_low = probs.astype(jnp.bfloat16)
    attended = jnp.einsum(
        "mbhqk,mbkhe->mbqhe", probs_low, values, preferred_element_type=jnp.float32
    ).astype(jnp.bfloat16)
    attended_flat = attended.reshape(micro_count, images, seq_len, head_cols)

    def backward_segment(micro_index, incoming):
        query_now = select_micro(query, micro_index)
        keys_now = select_micro(keys, micro_index)
        values_now = select_micro(values, micro_index)
        probs_now = select_micro(probs, micro_index)
        probs_low_now = select_micro(probs_low, micro_index)
        attended_now = select_micro(attended, micro_index)
        scaled = (scale_vec * incoming.astype(jnp.float32)).astype(jnp.bfloat16)
        d_att = jnp.einsum("bsd,dc->bsc", scaled, w_out, preferred_element_type=jnp.float32).astype(
            jnp.bfloat16
        )
        d_att = d_att.reshape(images, seq_len, local_heads, HD)
        d_prob = jnp.einsum(
            "bqhe,bkhe->bhqk", d_att, values_now, preferred_element_type=jnp.float32
        )
        row_delta = jnp.einsum(
            "bqhe,bqhe->bhq", d_att, attended_now, preferred_element_type=jnp.float32
        )
        d_score = (probs_now * (d_prob - row_delta[..., None]) / score_root).astype(jnp.bfloat16)
        d_query = jnp.einsum(
            "bhqk,bkhe->bqhe", d_score, keys_now, preferred_element_type=jnp.float32
        ).astype(jnp.bfloat16)
        d_keys = jnp.einsum(
            "bhqk,bqhe->bkhe", d_score, query_now, preferred_element_type=jnp.float32
        ).astype(jnp.bfloat16)
        d_values = jnp.einsum(
            "bhqk,bqhe->bkhe", probs_low_now, d_att, preferred_element_type=jnp.float32
        ).astype(jnp.bfloat16)
        d_proj = jnp.concatenate([d_query, d_keys, d_values], axis=2).reshape(
            images, seq_len, 3 * head_cols
        )
        partial_sum = jnp.einsum("bsc,dc->bsd", d_proj, w_qkv, preferred_element_type=jnp.float32)
        return (partial_sum, d_proj, scaled)

    def spare_segment(micro_index, incoming):
        return (
            jnp.zeros((images, seq_len, channels), jnp.float32),
            jnp.zeros((images, seq_len, 3 * head_cols), jnp.bfloat16),
            jnp.zeros((images, seq_len, channels), jnp.bfloat16),
        )

    segments = n_pipe + micro_count - 1
    is_last = pipe_rank == n_pipe - 1
    received = jnp.zeros((images, seq_len, channels), jnp.bfloat16)
    slots = micro_count + 1
    grads_out = jnp.zeros((slots, images, shard_len, channels), jnp.bfloat16)
    proj_saved = jnp.zeros((slots, images, seq_len, 3 * head_cols), jnp.bfloat16)
    scaled_saved = jnp.zeros((slots, images, seq_len, channels), jnp.bfloat16)
    grad_saved = jnp.zeros((slots, images, seq_len, channels), jnp.bfloat16)
    gain_part = jnp.zeros((channels,), jnp.float32)
    for segment_step in range(segments):
        micro_index = segment_step - (n_pipe - 1) + pipe_rank
        active = jnp.logical_and(micro_index >= 0, micro_index < micro_count)
        micro_index = jnp.clip(micro_index, 0, micro_count - 1)
        slot_index = jnp.where(active, micro_index, micro_count)
        arrived = received
        incoming = jnp.where(is_last, select_micro(out_grad, micro_index), arrived)
        partial_sum, d_proj, scaled = lax.cond(
            active, backward_segment, spare_segment, micro_index, incoming
        )
        pieces = partial_sum.astype(jnp.bfloat16).reshape(images, n_tensor, shard_len, channels)
        landed = lax.all_to_all(pieces, "tensor", split_axis=1, concat_axis=1, tiled=True)
        own_d = jnp.sum(landed.astype(jnp.float32), axis=1)
        d_normed = lax.all_gather(own_d.astype(jnp.bfloat16), "tensor", axis=1, tiled=True).astype(
            own_d.dtype
        )
        own_unit = select_micro(local_unit, micro_index)
        sel_unit = select_micro(full_unit, micro_index)
        sel_inverse = select_micro(full_inverse, micro_index)
        d_unit = d_normed * gain_vec
        d_input = sel_inverse * (
            d_unit - sel_unit * jnp.mean(d_unit * sel_unit, axis=-1, keepdims=True)
        )
        passed = (incoming.astype(jnp.float32) + d_input).astype(jnp.bfloat16)
        own_passed = lax.dynamic_slice_in_dim(passed, row_start, shard_len, 1)
        gain_part = gain_part + jnp.where(active, jnp.sum(own_d * own_unit, axis=(0, 1)), 0.0)
        grads_out = store_slot(grads_out, own_passed, slot_index)
        proj_saved = store_slot(proj_saved, d_proj, slot_index)
        scaled_saved = store_slot(scaled_saved, scaled, slot_index)
        grad_saved = store_slot(grad_saved, incoming, slot_index)
        if segment_step + 1 < segments:
            received = from_behind(passed, "pipe", -1)
    grads_kept = grads_out[:micro_count]
    proj_kept = proj_saved[:micro_count]
    scaled_kept = scaled_saved[:micro_count]
    grad_kept = grad_saved[:micro_count]
    grad_qkv = jnp.einsum("mbsd,mbsc->dc", normed, proj_kept, preferred_element_type=jnp.float32)
    grad_out = jnp.einsum(
        "mbsd,mbsc->dc", scaled_kept, attended_flat, preferred_element_type=jnp.float32
    )
    weight_grad = lax.psum_scatter(
        jnp.concatenate([grad_qkv, grad_out], axis=1).astype(jnp.bfloat16),
        "dp",
        scatter_dimension=0,
        tiled=True,
    ).astype(jnp.float32)
    summed_out = jnp.einsum(
        "mbsd,mbsc->dc", grad_kept, attended_flat, preferred_element_type=jnp.float32
    )
    scale_part = jnp.sum(w_out.astype(jnp.float32) * summed_out, axis=1)
    scale_grad, gain_grad = lax.psum((scale_part, gain_part), ("dp", "tensor"))
    bias_one = 1.0 - beta_one**adam_step
    bias_two = 1.0 - beta_two**adam_step
    first_new = beta_one * moment_one[0] + (1.0 - beta_one) * weight_grad
    second_new = beta_two * moment_two[0] + (1.0 - beta_two) * weight_grad * weight_grad
    update = first_new / bias_one / (jnp.sqrt(second_new / bias_two) + adam_eps)
    master_new = master[0] - learn_rate * (update + weight_decay * master[0])
    scale_both = jnp.stack([scale_grad, gain_grad])
    return (grads_kept[None], master_new[None], first_new[None], second_new[None], scale_both[None])


def solution(mesh):
    placed = (
        P("pipe", None, "dp", "tensor", None),
        P(None, "dp", None, None),
        P("pipe", None),
        P("pipe", None),
        P("pipe", "dp", "tensor"),
        P("pipe", "dp", "tensor"),
        P("pipe", "dp", "tensor"),
    )
    two_by_two = mesh.shape["dp"] == 4 and mesh.shape["tensor"] == 2
    return jax.shard_map(
        local_two_by_two if two_by_two else local_any,
        mesh=mesh,
        in_specs=placed,
        out_specs=(
            P("pipe", None, "dp", "tensor", None),
            P("pipe", "dp", "tensor"),
            P("pipe", "dp", "tensor"),
            P("pipe", "dp", "tensor"),
            P("pipe", None, None),
        ),
        check_vma=False,
    )
```
